512 devices in a mesh: ka: 32 (over y_hi, z), ga: 16 (over y_lo, x, core).
Axes of the slice: x: 4, y: 4 (y_hi: 2, y_lo: 2; y = y_hi * 2 + y_lo), z: 16, core: 2. Of those that a mesh axis runs over, the one named last changes fastest.
Arguments:
- cond: bfloat16 [32, 8, 4096], P('ka', None, 'ga'), may hold values from -6 to 6
- vale: bfloat16 [32, 8, 4096], P('ka', None, 'ga'), may hold values from -6 to 6
- screen: bfloat16 [32, 4096, 4096], P('ka', 'ga'), may hold values from -0.0014648438 to 0.0014648438
- qtable: int32 [32, 32], replicated, may hold values from 0 to 31, as said below
- gmap: int32 [32, 4096], P('ka', 'ga'), may hold values from 0 to 4095, as said below
Outputs:
- kernel: float32 [32, 3, 4096], P('ka', None, 'ga')
The draws below stay inside these ranges and needn't reach their ends.
Inputs may be any that keep to these rules, and one draw needn't show every extreme that they name: qtable[k,k2] depends only on (k - k2) mod 32, and each row names every k-difference once. `gmap`: each aligned block of 256 entries of a row is an ordering of that block's own grid indices.
All inputs are finite; a program needn't handle non-finite values.
Results may differ from the reference program's by a relative error of at most 0.0041.
Values may be sent and summed in bfloat16 or wider, within the bound.
No kernel may reach another device: no remote copies, remote signals or barrier semaphores. Data moves between devices by JAX's collectives and lax.ppermute only.
A program may use at most 64 MiB of HBM per device.

```python
import jax
import jax.numpy as jnp
from jax import lax

NG = 4096
NC = 8
NV = 8
NSHIFT = 2
KPTS = 32
GDEV = 256
N_KA = 32


def draw_qtable(key, part):
    key = jax.random.fold_in(key, 1)
    order = jax.random.permutation(key, KPTS).astype(jnp.int32)
    rows = jnp.arange(KPTS, dtype=jnp.int32)
    diff = (rows[:, None] - rows[None, :]) % KPTS
    return order[diff].astype(jnp.int32)


def draw_gmap(key, part):
    key = jax.random.fold_in(key, 2)
    blocks = NG // GDEV
    scores = jax.random.randint(key, (KPTS, blocks, GDEV), 0, 2 ** 16, dtype=jnp.int32)
    scores = scores * GDEV + jnp.arange(GDEV, dtype=jnp.int32)[None, None, :]
    order = jnp.argsort(scores, axis=2, stable=True).astype(jnp.int32)
    base = (jnp.arange(blocks, dtype=jnp.int32) * GDEV)[None, :, None]
    return (order + base).reshape(KPTS, NG).astype(jnp.int32)


def shard_levels(rng, shape, cuts, least, top_value):
    level, own = 1.0, jax.random.fold_in(rng, 6)
    for position, blocks in cuts:
        draws = jnp.exp(jax.random.uniform(jax.random.fold_in(own, position), (blocks,), jnp.float32, least / len(cuts), top_value / len(cuts)))
        level = level * jnp.repeat(draws, shape[position] // blocks).reshape([-1 if axis == position else 1 for axis in range(len(shape))])
    return level


def gaussian(rng, dims, width, limit, shards=(), held_as=jnp.bfloat16):
    array = width * jax.random.normal(rng, dims, jnp.float32)
    if shards:
        array = array * shard_levels(rng, dims, shards, -0.22, 0.18)
    return jnp.clip(array, -limit, limit).astype(held_as)


def setup_inputs(seed: int = 0) -> dict:
    arg_keys = jax.random.split(jax.random.key(seed), 6)
    return {
        "cond": gaussian(arg_keys[0], (KPTS, NC, NG), 1.0, 6.0, ((0, 32), (2, 16))),
        "vale": gaussian(arg_keys[1], (KPTS, NV, NG), 1.0, 6.0, ((0, 32), (2, 16))),
        "screen": gaussian(arg_keys[2], (KPTS, NG, NG), (NG * NG) ** -0.5, 0.0014648438, ((0, 32), (1, 16))),
        "qtable": draw_qtable(jax.random.fold_in(arg_keys[5], 71), 0),
        "gmap": draw_gmap(jax.random.fold_in(arg_keys[5], 71), 0),
    }


def pair_density(own, far):
    product = own.astype(jnp.float32)[:, None, :] * far.astype(jnp.float32)[None, :, :]
    return product.astype(jnp.bfloat16).reshape(-1, own.shape[-1])


def reference(cond, vale, screen, qtable, gmap):
    k_rows = KPTS // N_KA
    indices = jnp.arange(KPTS, dtype=jnp.int32)
    cond_mapped = jnp.take_along_axis(cond, gmap[:, None, :], axis=2)
    vale_mapped = jnp.take_along_axis(vale, gmap[:, None, :], axis=2)
    blocks = []
    for offset in range(NSHIFT + 1):
        for right in range(k_rows):
            partner = (((indices // k_rows - offset) % N_KA) * k_rows + right).astype(jnp.int32)

            def one_row(row, partner=partner):
                other = partner[row]
                qindex = qtable[row, other]
                weight = lax.dynamic_index_in_dim(screen, qindex, 0, keepdims=False)
                dens_c = pair_density(cond[row], cond_mapped[other])
                dens_v = pair_density(vale[row], vale_mapped[other])
                image = jnp.dot(weight, dens_v.T, preferred_element_type=jnp.float32)
                tile = jnp.dot(dens_c.astype(jnp.float32), image, precision=lax.Precision.HIGHEST)
                return tile.reshape(-1)

            blocks.append(lax.map(one_row, indices))
    return jnp.stack(blocks, axis=1)
```

```python
import jax
import jax.numpy as jnp
from jax import lax
from jax.experimental import pallas as pl
from jax.experimental.pallas import tpu as pltpu
from jax.sharding import PartitionSpec as P

NSHIFT = 2
STEP_K = 4


def last_dims(a, b):
    return lax.dot_general(a, b, (((1,), (1,)), ((), ())), preferred_element_type=jnp.float32)


def density(pair):
    pair = pair.astype(jnp.float32)
    own, far = pair[:8], pair[8:]
    product = own[:, None, :] * far[None, :, :]
    return product.reshape(64, pair.shape[-1]).astype(jnp.bfloat16)


def tile_kernel(w_own, w_mate, vale, c_own, c_mate, out, pv, pc_own, pc_mate):
    blocks, _, _, width = vale.shape
    for k in range(STEP_K):
        rows = pl.ds(64 * k, 64)
        for block in range(blocks):
            pv[rows, pl.ds(block * width, width)] = density(vale[block, k])
        pc_own[rows, :] = density(c_own[k])
        pc_mate[rows, :] = density(c_mate[k])
    image_own = last_dims(pv[...], w_own[...]).astype(jnp.bfloat16)
    image_mate = last_dims(pv[...], w_mate[...]).astype(jnp.bfloat16)
    full = last_dims(pc_own[...], image_own) + last_dims(pc_mate[...], image_mate)
    low = lax.broadcasted_iota(jnp.int32, (64, 128), 1) < 64
    for pair in range(STEP_K // 2):
        base = 128 * pair
        strip = full[:, base : base + 128]
        tile = jnp.where(low, strip[base : base + 64], strip[base + 64 : base + 128])
        out[:, pl.ds(4 * pair, 4), :] = tile.reshape(16, 4, 128)


def tiles(w_own, w_mate, vale, c_own, c_mate):
    blocks, n_k, rows, width = vale.shape
    grid_h = w_own.shape[1]
    return pl.pallas_call(
        tile_kernel,
        grid=(n_k // STEP_K,),
        in_specs=[
            pl.BlockSpec(w_own.shape, lambda i: (0, 0)),
            pl.BlockSpec(w_mate.shape, lambda i: (0, 0)),
            pl.BlockSpec((blocks, STEP_K, rows, width), lambda i: (0, i, 0, 0)),
            pl.BlockSpec((STEP_K, rows, width), lambda i: (i, 0, 0)),
            pl.BlockSpec((STEP_K, rows, width), lambda i: (i, 0, 0)),
        ],
        out_specs=pl.BlockSpec((16, 2 * STEP_K, 128), lambda i: (0, i, 0)),
        out_shape=jax.ShapeDtypeStruct((16, 2 * n_k, 128), jnp.float32),
        scratch_shapes=[
            pltpu.VMEM((64 * STEP_K, grid_h), jnp.bfloat16),
            pltpu.VMEM((64 * STEP_K, width), jnp.bfloat16),
            pltpu.VMEM((64 * STEP_K, width), jnp.bfloat16),
        ],
        compiler_params=pltpu.CompilerParams(vmem_limit_bytes=40 * 1024 * 1024),
    )(w_own, w_mate, vale, c_own, c_mate)


def per_device(cond, vale, screen, qtable, gmap):
    n_ka = lax.axis_size("ka")
    n_ga = lax.axis_size("ga")
    n_z = n_ka // 2
    g_width = cond.shape[2]
    my_ka = lax.axis_index("ka")
    my_ga = lax.axis_index("ga")
    core = my_ga % 2
    swap_core = [(i, i ^ 1) for i in range(n_ga)]
    swap_y = [(i, i ^ n_z) for i in range(n_ka)]
    z_groups = [list(range(n_z)), list(range(n_z, n_ka))]

    slab = screen[0]
    slab_mate = lax.ppermute(slab, "ga", swap_core)

    local_map = gmap[0] - my_ga * g_width
    own = jnp.concatenate([vale[0], cond[0]], axis=0)
    mapped = jnp.take(own, local_map, axis=1)
    data = jnp.stack([own, mapped])
    other = lax.ppermute(data, "ka", swap_y)
    first = my_ka < n_z
    both = jnp.stack([jnp.where(first, data, other), jnp.where(first, other, data)])
    sent = jnp.broadcast_to(both[None], (n_z,) + both.shape)
    got = lax.all_to_all(sent, "ka", 0, 0, axis_index_groups=z_groups)
    every = jnp.swapaxes(got, 0, 1).reshape(n_ka, 2, 16, g_width)

    wanted = qtable[: NSHIFT + 1, 0]
    offset = jnp.sum(jnp.where(wanted == my_ka, jnp.arange(NSHIFT + 1, dtype=jnp.int32), 0))
    far = every[:, 1]
    far = jnp.concatenate([far[n_ka - NSHIFT :], far], axis=0)
    far = lax.dynamic_slice_in_dim(far, NSHIFT - offset, n_ka, 0)
    near = every[:, 0]
    v_pairs = jnp.concatenate([near[:, :8], far[:, :8]], axis=1).reshape(2, n_z, 16, g_width)
    c_pairs = jnp.concatenate([near[:, 8:], far[:, 8:]], axis=1).reshape(2, n_z, 16, g_width)
    c_own = lax.dynamic_index_in_dim(c_pairs, core, 0, keepdims=False)
    c_mate = lax.ppermute(
        lax.dynamic_index_in_dim(c_pairs, 1 - core, 0, keepdims=False), "ga", swap_core
    )
    v_sent = jnp.broadcast_to(v_pairs[None], (n_ga // 2,) + v_pairs.shape)
    v_all = lax.all_to_all(v_sent.reshape(n_ga, n_z, 16, g_width), "ga", 0, 0)

    part = tiles(slab, slab_mate, v_all, c_own, c_mate)
    shares = lax.all_to_all(part, "ga", 0, 0)
    total = shares.reshape(n_ga // 2, 2, n_z // 2, 1, 4, 128).sum(0)
    spread = jnp.broadcast_to(total, (2, n_z // 2, 2, 4, 128)).reshape(n_ka, 4, 128)
    rows = lax.all_to_all(spread, "ka", 0, 0)
    mine = jnp.take(rows, wanted, axis=0)
    mine = jnp.where(my_ka % 2 == 0, mine[..., :64], mine[..., 64:])
    return mine.reshape(1, NSHIFT + 1, g_width)


def solution(mesh):
    in_specs = (P("ka", None, "ga"), P("ka", None, "ga"), P("ka", "ga", None), P(), P("ka", "ga"))
    out_specs = P("ka", None, "ga")
    return jax.shard_map(
        per_device, mesh=mesh, in_specs=in_specs, out_specs=out_specs, check_vma=False
    )
```

```python
import jax
import jax.numpy as jnp
from jax import lax
from jax.experimental import pallas as pl
from jax.experimental.pallas import tpu as pltpu
from jax.sharding import PartitionSpec as P

NSHIFT = 2
STEP_K = 4
VMEM = pl.BlockSpec(memory_space=pltpu.VMEM)
SMEM = pl.BlockSpec(memory_space=pltpu.SMEM)


def last_dims(a, b):
    return lax.dot_general(a, b, (((1,), (1,)), ((), ())), preferred_element_type=jnp.float32)


def density(own, far):
    product = own[:, None, :] * far[None, :, :]
    return product.reshape(64, own.shape[-1]).astype(jnp.bfloat16)


def lane_gather(source, places):
    return jnp.take_along_axis(source, places, axis=1, mode="promise_in_bounds")


def mapped(source, places):
    low, high = source[:, :128], source[:, 128:]
    sides = []
    for part in (places[:, :128], places[:, 128:]):
        inner = part & 127
        sides.append(jnp.where(part < 128, lane_gather(low, inner), lane_gather(high, inner)))
    return jnp.concatenate(sides, axis=1)


def map_entries(entries, count, store):
    maps = [entries[count + part].astype(jnp.float32).astype(jnp.int32) for part in range(2)]
    for entry in range(count):
        row = maps[entry // 8][entry % 8 : entry % 8 + 1]
        places = jnp.broadcast_to(row, (8, row.shape[1]))
        store(entry, mapped(entries[entry].astype(jnp.float32), places))


def tile_kernel(table, place, w_own, w_mate, vale, c_own, c_mate, out, far_v, far_c, pv, pc):
    sources, entries, _, width = vale.shape
    n_blocks = sources // 2
    count = entries - 2
    half_z = count - NSHIFT
    my_ka, core = place[0], place[1] % 2
    shift = sum(jnp.where(table[by, 0] == my_ka, by, 0) for by in range(1, NSHIFT + 1))

    @pl.loop(0, sources)
    def _(source):
        y, block = source // n_blocks, source % n_blocks
        lanes = pl.ds(pl.multiple_of(block * width, width), width)

        def store(entry, value):
            far_v[y * count + entry, :, lanes] = value

        map_entries(vale.at[source], count, store)

    for side, c_ref in enumerate((c_own, c_mate)):
        for y in range(2):

            def store(entry, value, y=y, side=side):
                far_c[y * count + entry, :, pl.ds(side * width, width)] = value

            map_entries(c_ref.at[y], count, store)

    low = lax.broadcasted_iota(jnp.int32, (64, 128), 1) < 64
    for y in range(2):
        for part in range(half_z // STEP_K):
            step = y * (half_z // STEP_K) + part
            for k in range(STEP_K):
                entry = NSHIFT + part * STEP_K + k
                other = entry - shift
                crossed = jnp.logical_and(core == 0, other < NSHIFT)
                partner = jnp.where(crossed, 1 - y, y) * count + other
                rows = pl.ds(64 * k, 64)
                for block in range(n_blocks):
                    lanes = pl.ds(block * width, width)
                    own = vale[y * n_blocks + block, entry].astype(jnp.float32)
                    pv[step, rows, lanes] = density(own, far_v[partner, :, lanes])
                for side, c_ref in enumerate((c_own, c_mate)):
                    lanes = pl.ds(side * width, width)
                    own = c_ref[y, entry].astype(jnp.float32)
                    pc[step, rows, lanes] = density(own, far_c[partner, :, lanes])
            full = None
            for side, w_ref in enumerate((w_own, w_mate)):
                image = last_dims(pv[step], w_ref[...]).astype(jnp.bfloat16)
                term = last_dims(pc[step, :, pl.ds(side * width, width)], image)
                full = term if full is None else full + term
            for pair in range(STEP_K // 2):
                base = 128 * pair
                strip = full[:, base : base + 128]
                tile = jnp.where(low, strip[base : base + 64], strip[base + 64 : base + 128])
                out[pl.ds(16 * y, 16), pl.ds(8 * part + 4 * pair, 4), :] = tile.reshape(16, 4, 128)


def tiles(table, place, w_own, w_mate, vale, c_own, c_mate):
    sources, entries, _, width = vale.shape
    count = entries - 2
    grid_h = w_own.shape[1]
    half_z = count - NSHIFT
    steps = 2 * half_z // STEP_K
    return pl.pallas_call(
        tile_kernel,
        in_specs=[SMEM, SMEM] + [VMEM] * 5,
        out_specs=VMEM,
        out_shape=jax.ShapeDtypeStruct((sources, 2 * half_z, 128), jnp.float32),
        scratch_shapes=[
            pltpu.VMEM((2 * count, 8, grid_h), jnp.float32),
            pltpu.VMEM((2 * count, 8, 2 * width), jnp.float32),
            pltpu.VMEM((steps, 64 * STEP_K, grid_h), jnp.bfloat16),
            pltpu.VMEM((steps, 64 * STEP_K, 2 * width), jnp.bfloat16),
        ],
        compiler_params=pltpu.CompilerParams(vmem_limit_bytes=36 * 1024 * 1024),
    )(table, place, w_own, w_mate, vale, c_own, c_mate)


def pack_kernel(got, v_out, c_out):
    n_z, _, _, width = got.shape
    half_z = n_z // 2
    count = half_z + NSHIFT
    row_id = lax.broadcasted_iota(jnp.int32, (8, width), 0)
    for half in range(2):
        spots = [(half * half_z + entry - NSHIFT) % n_z for entry in range(count)]
        packs = []
        for first in range(0, count, 8):
            rows = jnp.zeros((8, width), jnp.float32)
            for entry in range(first, min(first + 8, count)):
                rows = jnp.where(row_id == entry - first, got[spots[entry], 2].astype(jnp.float32), rows)
            packs.append(rows.astype(jnp.bfloat16))
        for part, rows in enumerate(packs):
            c_out[half, count + part] = rows
        for entry, spot in enumerate(spots):
            c_out[half, entry] = got[spot, 1]
        for dest in range(half, v_out.shape[0], 2):
            for part, rows in enumerate(packs):
                v_out[dest, count + part] = rows
            for entry, spot in enumerate(spots):
                v_out[dest, entry] = got[spot, 0]


def pack(got, dests):
    n_z, _, _, width = got.shape
    entries = n_z // 2 + NSHIFT + 2
    return pl.pallas_call(
        pack_kernel,
        in_specs=[VMEM],
        out_specs=[VMEM, VMEM],
        out_shape=[
            jax.ShapeDtypeStruct((dests, entries, 8, width), jnp.bfloat16),
            jax.ShapeDtypeStruct((2, entries, 8, width), jnp.bfloat16),
        ],
        compiler_params=pltpu.CompilerParams(vmem_limit_bytes=8 * 1024 * 1024),
    )(got)


def total_kernel(shares, out):
    sources, rows, _ = shares.shape
    for y in range(2):
        for core in range(2):
            first = y * (sources // 2) + core
            total = shares[first]
            for source in range(first + 2, first + sources // 2, 2):
                total = total + shares[source]
            for pair in range(rows // 4):
                strip = total[4 * pair : 4 * pair + 4]
                for odd in range(2):
                    z = core * (rows // 2) + 2 * pair + odd
                    out[z, pl.ds(4 * y, 4), :] = strip


def totals(shares):
    n_z = shares.shape[1]
    return pl.pallas_call(
        total_kernel,
        in_specs=[VMEM],
        out_specs=VMEM,
        out_shape=jax.ShapeDtypeStruct((n_z, 8, 128), jnp.float32),
        compiler_params=pltpu.CompilerParams(vmem_limit_bytes=4 * 1024 * 1024),
    )(shares)


def pick_kernel(table, place, rows, out):
    n_z = rows.shape[0]
    odd = place[0] % 2 == 1
    low = lax.broadcasted_iota(jnp.int32, (4, 128), 1) < 64
    for by in range(NSHIFT + 1):
        holder = table[by, 0]
        both = rows[holder % n_z]
        strip = jnp.where(holder // n_z == 0, both[:4], both[4:])
        turned = pltpu.roll(strip, 64, 1)
        left = jnp.where(odd, turned, strip)
        right = jnp.where(odd, strip, turned)
        for side in range(2):
            line = jnp.where(low[:1], left[2 * side : 2 * side + 1], right[2 * side + 1 : 2 * side + 2])
            out[0, pl.ds(by, 1), pl.ds(128 * side, 128)] = line


def pick(table, place, rows):
    return pl.pallas_call(
        pick_kernel,
        in_specs=[SMEM, SMEM, VMEM],
        out_specs=VMEM,
        out_shape=jax.ShapeDtypeStruct((1, NSHIFT + 1, 256), jnp.float32),
        compiler_params=pltpu.CompilerParams(vmem_limit_bytes=4 * 1024 * 1024),
    )(table, place, rows)


def per_device(cond, vale, screen, qtable, gmap):
    n_ka = lax.axis_size("ka")
    n_ga = lax.axis_size("ga")
    n_z = n_ka // 2
    g_width = cond.shape[2]
    my_ka = lax.axis_index("ka")
    my_ga = lax.axis_index("ga")
    core = my_ga % 2
    place = jnp.stack([my_ka, my_ga]).astype(jnp.int32)
    swap_core = [(i, i ^ 1) for i in range(n_ga)]
    swap_y = [(i, i ^ n_z) for i in range(n_ka)]
    along_z = [list(range(n_z)), list(range(n_z, n_ka))]
    planes = [
        [(y * n_z + z) * n_ga + g for y in range(2) for g in range(n_ga)] for z in range(n_z)
    ]

    slab = screen[0]
    slab_mate = lax.ppermute(slab, "ga", swap_core)

    local_map = (gmap - my_ga * g_width).astype(jnp.bfloat16)
    data = jnp.stack([vale[0], cond[0], jnp.broadcast_to(local_map, (8, g_width))])
    sent = jnp.broadcast_to(data[None], (n_z,) + data.shape)
    got = lax.all_to_all(sent, "ka", 0, 0, axis_index_groups=along_z)

    v_sent, c_here = pack(got, 2 * n_ga)
    c_other = lax.ppermute(c_here, "ka", swap_y)
    v_all = lax.all_to_all(v_sent, ("ka", "ga"), 0, 0, axis_index_groups=planes)
    first = my_ka < n_z
    c_both = jnp.stack([jnp.where(first, c_here, c_other), jnp.where(first, c_other, c_here)], 1)
    c_own = lax.dynamic_index_in_dim(c_both, core, 0, keepdims=False)
    c_mate = lax.ppermute(
        lax.dynamic_index_in_dim(c_both, 1 - core, 0, keepdims=False), "ga", swap_core
    )

    part = tiles(qtable, place, slab, slab_mate, v_all, c_own, c_mate)
    shares = lax.all_to_all(part, ("ka", "ga"), 0, 0, axis_index_groups=planes)
    rows = lax.all_to_all(totals(shares), "ka", 0, 0, axis_index_groups=along_z)
    return pick(qtable, place, rows)


def solution(mesh):
    in_specs = (P("ka", None, "ga"), P("ka", None, "ga"), P("ka", "ga", None), P(), P("ka", "ga"))
    out_specs = P("ka", None, "ga")
    return jax.shard_map(
        per_device, mesh=mesh, in_specs=in_specs, out_specs=out_specs, check_vma=False
    )
```

```python
import jax
import jax.numpy as jnp
from jax import lax
from jax.experimental import pallas as pl
from jax.experimental.pallas import tpu as pltpu
from jax.sharding import PartitionSpec as P

NSHIFT = 2
STEP_K = 4
CHUNK = 2
VMEM = pl.BlockSpec(memory_space=pltpu.VMEM)
SMEM = pl.BlockSpec(memory_space=pltpu.SMEM)
ANY = pl.BlockSpec(memory_space=pl.ANY)


def last_dims(a, b):
    return lax.dot_general(a, b, (((1,), (1,)), ((), ())), preferred_element_type=jnp.float32)


def density(own, far):
    product = own[:, None, :] * far[None, :, :]
    return product.reshape(64, own.shape[-1]).astype(jnp.bfloat16)


def lane_gather(source, places):
    return jnp.take_along_axis(source, places, axis=1, mode="promise_in_bounds")


def mapped(source, places):
    low, high = source[:, :128], source[:, 128:]
    sides = []
    for part in (places[:, :128], places[:, 128:]):
        inner = part & 127
        sides.append(jnp.where(part < 128, lane_gather(low, inner), lane_gather(high, inner)))
    return jnp.concatenate(sides, axis=1)


def map_entries(entries, count, store):
    maps = [entries[count + part].astype(jnp.float32).astype(jnp.int32) for part in range(2)]
    for entry in range(count):
        row = maps[entry // 8][entry % 8 : entry % 8 + 1]
        places = jnp.broadcast_to(row, (8, row.shape[1]))
        store(entry, mapped(entries[entry].astype(jnp.float32), places))


def tile_kernel(
    table, place, w_own, w_mate, vale, c_keep, c_y, c_core, c_diag, out,
    slab, far_v, far_c, c_all, pv, pc, image, arrived,
):
    sources, entries, _, width = vale.shape
    n_blocks = sources // 2
    count = entries - 2
    half_z = count - NSHIFT
    n_z = 2 * half_z
    my_ka, core = place[0], place[1] % 2
    my_y = my_ka // n_z
    shift = sum(jnp.where(table[by, 0] == my_ka, by, 0) for by in range(1, NSHIFT + 1))
    fetch = pltpu.make_async_copy(w_own, slab, arrived)
    fetch.start()

    def partner(y, entry):
        other = entry - shift
        crossed = jnp.logical_and(core == 0, other < NSHIFT)
        return jnp.where(crossed, 1 - y, y) * count + other

    def form(chunk):
        slot = chunk % far_v.shape[0]
        for y in range(2):
            for inner in range(CHUNK):
                block = chunk * CHUNK + inner

                def store(entry, value):
                    far_v[slot, y * count + entry, :, pl.ds(inner * width, width)] = value

                map_entries(vale.at[y * n_blocks + block], count, store)
        for y in range(2):
            for z in range(half_z):
                rows = pl.ds(64 * (y * half_z + z), 64)
                row = partner(y, z + NSHIFT)
                for inner in range(CHUNK):
                    block = chunk * CHUNK + inner
                    lanes = pl.ds(inner * width, width)
                    own = vale[y * n_blocks + block, z + NSHIFT].astype(jnp.float32)
                    pv[chunk, rows, lanes] = density(own, far_v[slot, row, :, lanes])

    def form_c():
        for side, (mine, other) in enumerate(((c_keep, c_y), (c_core, c_diag))):
            c_all[side, my_y] = mine[...]
            c_all[side, 1 - my_y] = other[...]
        for side in range(2):
            lanes = pl.ds(side * width, width)
            for y in range(2):

                def store(entry, value):
                    far_c[y * count + entry, :, lanes] = value

                map_entries(c_all.at[side, y], count, store)
            for y in range(2):
                for z in range(half_z):
                    own = c_all[side, y, z + NSHIFT].astype(jnp.float32)
                    rows = pl.ds(64 * (y * half_z + z), 64)
                    pc[rows, lanes] = density(own, far_c[partner(y, z + NSHIFT), :, lanes])

    chunks = n_blocks // CHUNK
    form(0)
    fetch.wait()
    for chunk in range(chunks):
        if chunk + 1 < chunks:
            form(chunk + 1)
        else:
            form_c()
        span = pl.ds(chunk * CHUNK * width, CHUNK * width)
        for side, w_ref in enumerate((slab, w_mate)):
            lanes = pl.ds(side * width, width)
            term = last_dims(pv[chunk], w_ref[:, span])
            image[:, lanes] = term if chunk == 0 else image[:, lanes] + term

    low = lax.broadcasted_iota(jnp.int32, (64, 128), 1) < 64
    for y in range(2):
        for part in range(half_z // STEP_K):
            rows = pl.ds(64 * (y * half_z + part * STEP_K), 64 * STEP_K)
            full = last_dims(pc[rows, :], image[rows, :].astype(jnp.bfloat16))
            for pair in range(STEP_K // 2):
                base = 128 * pair
                strip = full[:, base : base + 128]
                tile = jnp.where(low, strip[base : base + 64], strip[base + 64 : base + 128])
                out[pl.ds(16 * y, 16), pl.ds(8 * part + 4 * pair, 4), :] = tile.reshape(16, 4, 128)


def tiles(table, place, w_own, w_mate, vale, c_keep, c_y, c_core, c_diag):
    sources, entries, _, width = vale.shape
    count = entries - 2
    grid_h = w_own.shape[1]
    half_z = count - NSHIFT
    rows = 2 * half_z * 64
    chunks = sources // 2 // CHUNK
    return pl.pallas_call(
        tile_kernel,
        in_specs=[SMEM, SMEM, ANY] + [VMEM] * 6,
        out_specs=VMEM,
        out_shape=jax.ShapeDtypeStruct((sources, 2 * half_z, 128), jnp.float32),
        scratch_shapes=[
            pltpu.VMEM(w_own.shape, jnp.bfloat16),
            pltpu.VMEM((2, 2 * count, 8, CHUNK * width), jnp.float32),
            pltpu.VMEM((2 * count, 8, 2 * width), jnp.float32),
            pltpu.VMEM((2, 2) + c_keep.shape, jnp.bfloat16),
            pltpu.VMEM((chunks, rows, CHUNK * width), jnp.bfloat16),
            pltpu.VMEM((rows, 2 * width), jnp.bfloat16),
            pltpu.VMEM((rows, 2 * width), jnp.float32),
            pltpu.SemaphoreType.DMA(()),
        ],
        compiler_params=pltpu.CompilerParams(vmem_limit_bytes=36 * 1024 * 1024),
    )(table, place, w_own, w_mate, vale, c_keep, c_y, c_core, c_diag)


def spread_kernel(place, cond_in, vale_in, gmap_in, out, cond, vale, gmap, arrived):
    width = cond.shape[2]
    fetches = [
        pltpu.make_async_copy(source, target, arrived.at[number])
        for number, (source, target) in enumerate(((cond_in, cond), (vale_in, vale), (gmap_in, gmap)))
    ]
    for fetch in fetches:
        fetch.start()
    for fetch in fetches:
        fetch.wait()
    places = (gmap[...] - place[1] * width).astype(jnp.float32).astype(jnp.bfloat16)
    places = jnp.broadcast_to(places, (8, width))
    for dest in range(out.shape[0]):
        out[dest, 0] = vale[0]
        out[dest, 1] = cond[0]
        out[dest, 2] = places


def spread(place, cond, vale, gmap, dests):
    return pl.pallas_call(
        spread_kernel,
        in_specs=[SMEM] + [ANY] * 3,
        out_specs=VMEM,
        out_shape=jax.ShapeDtypeStruct((dests, 3) + cond.shape[1:], jnp.bfloat16),
        scratch_shapes=[
            pltpu.VMEM(cond.shape, jnp.bfloat16),
            pltpu.VMEM(vale.shape, jnp.bfloat16),
            pltpu.VMEM(gmap.shape, jnp.int32),
            pltpu.SemaphoreType.DMA((3,)),
        ],
        compiler_params=pltpu.CompilerParams(vmem_limit_bytes=4 * 1024 * 1024),
    )(place, cond, vale, gmap)


def pack_kernel(place, got, v_out, keep, give):
    n_z, _, _, width = got.shape
    half_z = n_z // 2
    count = half_z + NSHIFT
    core = place[1] % 2
    row_id = lax.broadcasted_iota(jnp.int32, (8, width), 0)
    for half in range(2):
        spots = [(half * half_z + entry - NSHIFT) % n_z for entry in range(count)]
        packs = []
        for first in range(0, count, 8):
            rows = jnp.zeros((8, width), jnp.float32)
            for entry in range(first, min(first + 8, count)):
                rows = jnp.where(row_id == entry - first, got[spots[entry], 2].astype(jnp.float32), rows)
            packs.append(rows.astype(jnp.bfloat16))
        for mine, c_out in ((True, keep), (False, give)):

            @pl.when((core == half) == mine)
            def _(c_out=c_out, spots=spots, packs=packs):
                for part, rows in enumerate(packs):
                    c_out[count + part] = rows
                for entry, spot in enumerate(spots):
                    c_out[entry] = got[spot, 1]

        for dest in range(half, v_out.shape[0], 2):
            for part, rows in enumerate(packs):
                v_out[dest, count + part] = rows
            for entry, spot in enumerate(spots):
                v_out[dest, entry] = got[spot, 0]


def pack(place, got, dests):
    n_z, _, _, width = got.shape
    entries = n_z // 2 + NSHIFT + 2
    shape = (entries, 8, width)
    return pl.pallas_call(
        pack_kernel,
        in_specs=[SMEM, VMEM],
        out_specs=[VMEM] * 3,
        out_shape=[
            jax.ShapeDtypeStruct((dests,) + shape, jnp.bfloat16),
            jax.ShapeDtypeStruct(shape, jnp.bfloat16),
            jax.ShapeDtypeStruct(shape, jnp.bfloat16),
        ],
        compiler_params=pltpu.CompilerParams(vmem_limit_bytes=8 * 1024 * 1024),
    )(place, got)


def total_kernel(shares, out):
    sources, rows, _ = shares.shape
    for y in range(2):
        for core in range(2):
            first = y * (sources // 2) + core
            total = shares[first]
            for source in range(first + 2, first + sources // 2, 2):
                total = total + shares[source]
            for pair in range(rows // 4):
                strip = total[4 * pair : 4 * pair + 4]
                for odd in range(2):
                    z = core * (rows // 2) + 2 * pair + odd
                    out[z, pl.ds(4 * y, 4), :] = strip


def totals(shares):
    n_z = shares.shape[1]
    return pl.pallas_call(
        total_kernel,
        in_specs=[VMEM],
        out_specs=VMEM,
        out_shape=jax.ShapeDtypeStruct((n_z, 8, 128), jnp.float32),
        compiler_params=pltpu.CompilerParams(vmem_limit_bytes=4 * 1024 * 1024),
    )(shares)


def pick_kernel(table, place, rows, out):
    n_z = rows.shape[0]
    odd = place[0] % 2 == 1
    low = lax.broadcasted_iota(jnp.int32, (4, 128), 1) < 64
    for by in range(NSHIFT + 1):
        holder = table[by, 0]
        both = rows[holder % n_z]
        strip = jnp.where(holder // n_z == 0, both[:4], both[4:])
        turned = pltpu.roll(strip, 64, 1)
        left = jnp.where(odd, turned, strip)
        right = jnp.where(odd, strip, turned)
        for side in range(2):
            line = jnp.where(low[:1], left[2 * side : 2 * side + 1], right[2 * side + 1 : 2 * side + 2])
            out[by, :, pl.ds(128 * side, 128)] = line


def pick(table, place, rows):
    return pl.pallas_call(
        pick_kernel,
        in_specs=[SMEM, SMEM, VMEM],
        out_specs=VMEM,
        out_shape=jax.ShapeDtypeStruct((NSHIFT + 1, 1, 256), jnp.float32),
        compiler_params=pltpu.CompilerParams(vmem_limit_bytes=4 * 1024 * 1024),
    )(table, place, rows)


def per_device(cond, vale, screen, qtable, gmap):
    n_ka = lax.axis_size("ka")
    n_ga = lax.axis_size("ga")
    n_z = n_ka // 2
    my_ka = lax.axis_index("ka")
    my_ga = lax.axis_index("ga")
    place = jnp.stack([my_ka, my_ga]).astype(jnp.int32)
    swap_core = [(i, i ^ 1) for i in range(n_ga)]
    swap_y = [(i, i ^ n_z) for i in range(n_ka)]
    swap_both = [(k * n_ga + g, (k ^ n_z) * n_ga + (g ^ 1)) for k in range(n_ka) for g in range(n_ga)]
    along_z = [list(range(n_z)), list(range(n_z, n_ka))]
    planes = [
        [(y * n_z + z) * n_ga + g for y in range(2) for g in range(n_ga)] for z in range(n_z)
    ]

    slab = screen[0]
    slab_mate = lax.ppermute(slab, "ga", swap_core)

    sent = spread(place, cond, vale, gmap, n_z)
    got = lax.all_to_all(sent, "ka", 0, 0, axis_index_groups=along_z)

    v_sent, c_keep, c_give = pack(place, got, 2 * n_ga)
    c_y = lax.ppermute(c_keep, "ka", swap_y)
    c_core = lax.ppermute(c_give, "ga", swap_core)
    c_diag = lax.ppermute(c_give, ("ka", "ga"), swap_both)
    v_all = lax.all_to_all(v_sent, ("ka", "ga"), 0, 0, axis_index_groups=planes)

    part = tiles(qtable, place, slab, slab_mate, v_all, c_keep, c_y, c_core, c_diag)
    shares = lax.all_to_all(part, ("ka", "ga"), 0, 0, axis_index_groups=planes)
    rows = lax.all_to_all(totals(shares), "ka", 0, 0, axis_index_groups=along_z)
    return jnp.transpose(pick(qtable, place, rows), (1, 0, 2))


def solution(mesh):
    in_specs = (P("ka", None, "ga"), P("ka", None, "ga"), P("ka", "ga", None), P(), P("ka", "ga"))
    out_specs = P("ka", None, "ga")
    return jax.shard_map(
        per_device, mesh=mesh, in_specs=in_specs, out_specs=out_specs, check_vma=False
    )
```

```python
import jax
import jax.numpy as jnp
from jax import lax
from jax.experimental import pallas as pl
from jax.experimental.pallas import tpu as pltpu
from jax.sharding import PartitionSpec as P

NSHIFT = 2
STEP_K = 4
CHUNK = 2
VMEM = pl.BlockSpec(memory_space=pltpu.VMEM)
SMEM = pl.BlockSpec(memory_space=pltpu.SMEM)
HBM = pl.BlockSpec(memory_space=pltpu.HBM)
ANY = pl.BlockSpec(memory_space=pl.ANY)


def in_hbm(*arrays):
    return [pltpu.with_memory_space_constraint(array, pltpu.HBM) for array in arrays]


def last_dims(a, b):
    return lax.dot_general(a, b, (((1,), (1,)), ((), ())), preferred_element_type=jnp.float32)


def density(own, far):
    product = own[:, None, :] * far[None, :, :]
    return product.reshape(64, own.shape[-1]).astype(jnp.bfloat16)


def lane_gather(source, places):
    return jnp.take_along_axis(source, places, axis=1, mode="promise_in_bounds")


def mapped(source, places):
    low, high = source[:, :128], source[:, 128:]
    sides = []
    for part in (places[:, :128], places[:, 128:]):
        inner = part & 127
        sides.append(jnp.where(part < 128, lane_gather(low, inner), lane_gather(high, inner)))
    return jnp.concatenate(sides, axis=1)


def entry_lanes(entry, width):
    return pl.ds(entry * width, width)


def map_entries(packed, count, width, store):
    maps = []
    for first in range(0, 2 * count, 8):
        lanes = pl.ds(count * width + 16 * first, 128)
        maps.append(packed[:, lanes].astype(jnp.float32).astype(jnp.int32))
    for entry in range(count):
        sides = []
        for side in range(2):
            row = 2 * entry + side
            places = maps[row // 8][row % 8 : row % 8 + 1]
            sides.append(jnp.broadcast_to(places, (8, 128)))
        source = packed[:, entry_lanes(entry, width)].astype(jnp.float32)
        store(entry, mapped(source, jnp.concatenate(sides, axis=1)))


def tile_kernel(
    table, place, w_own, w_mate, vale, c_keep, c_y, c_core, c_diag, out, plan,
    slabs, far_v, far_c, c_all, pv, pc, image, arrived,
):
    n_blocks = vale.shape[0] // 2
    width = w_own.shape[0]
    n_z = out.shape[1]
    half_z = n_z // 2
    count = half_z + NSHIFT
    my_ka, core = place[0], place[1] % 2
    my_y = my_ka // n_z
    shift = sum(jnp.where(table[by, 0] == my_ka, by, 0) for by in range(1, NSHIFT + 1))
    fetches = [
        pltpu.make_async_copy(source, slabs.at[side], arrived.at[side])
        for side, source in enumerate((w_own, w_mate))
    ]
    for fetch in fetches:
        fetch.start()

    upper = lax.broadcasted_iota(jnp.int32, (8, 128), 0) >= 4
    for z in range(n_z):
        tile = jnp.full((8, 128), -1, jnp.int32)
        for by in range(NSHIFT + 1):
            holder = table[by, 0]
            row = jnp.where(upper, holder - n_z, holder)
            tile = jnp.where(row == z, by, tile)
        plan[z] = tile
    plan[n_z] = jnp.full((8, 128), my_ka % 2, jnp.int32)

    def partner(y, entry):
        other = entry - shift
        crossed = jnp.logical_and(core == 0, other < NSHIFT)
        return jnp.where(crossed, 1 - y, y) * count + other

    def form(chunk):
        slot = chunk % far_v.shape[0]
        for y in range(2):
            for inner in range(CHUNK):
                block = chunk * CHUNK + inner

                def store(entry, value):
                    far_v[slot, y * count + entry, :, pl.ds(inner * width, width)] = value

                map_entries(vale.at[y * n_blocks + block], count, width, store)
        for y in range(2):
            for z in range(half_z):
                rows = pl.ds(64 * (y * half_z + z), 64)
                row = partner(y, z + NSHIFT)
                for inner in range(CHUNK):
                    block = chunk * CHUNK + inner
                    lanes = pl.ds(inner * width, width)
                    own = vale[y * n_blocks + block, :, entry_lanes(z + NSHIFT, width)]
                    own = own.astype(jnp.float32)
                    pv[chunk, rows, lanes] = density(own, far_v[slot, row, :, lanes])

    def form_c():
        for side, (mine, other) in enumerate(((c_keep, c_y), (c_core, c_diag))):
            c_all[side, my_y] = mine[...]
            c_all[side, 1 - my_y] = other[...]
        for side in range(2):
            lanes = pl.ds(side * width, width)
            for y in range(2):

                def store(entry, value):
                    far_c[y * count + entry, :, lanes] = value

                map_entries(c_all.at[side, y], count, width, store)
            for y in range(2):
                for z in range(half_z):
                    own = c_all[side, y, :, entry_lanes(z + NSHIFT, width)].astype(jnp.float32)
                    rows = pl.ds(64 * (y * half_z + z), 64)
                    pc[rows, lanes] = density(own, far_c[partner(y, z + NSHIFT), :, lanes])

    chunks = n_blocks // CHUNK
    form(0)
    for fetch in fetches:
        fetch.wait()
    for chunk in range(chunks):
        if chunk + 1 < chunks:
            form(chunk + 1)
        else:
            form_c()
        span = pl.ds(chunk * CHUNK * width, CHUNK * width)
        for side in range(2):
            lanes = pl.ds(side * width, width)
            term = last_dims(pv[chunk], slabs[side, :, span])
            image[:, lanes] = term if chunk == 0 else image[:, lanes] + term

    low = lax.broadcasted_iota(jnp.int32, (64, 128), 1) < 64
    for y in range(2):
        for part in range(half_z // STEP_K):
            rows = pl.ds(64 * (y * half_z + part * STEP_K), 64 * STEP_K)
            full = last_dims(pc[rows, :], image[rows, :].astype(jnp.bfloat16))
            for pair in range(STEP_K // 2):
                base = 128 * pair
                strip = full[:, base : base + 128]
                tile = jnp.where(low, strip[base : base + 64], strip[base + 64 : base + 128])
                out[pl.ds(16 * y, 16), pl.ds(8 * part + 4 * pair, 4), :] = tile.reshape(16, 4, 128)


def tiles(table, place, w_own, w_mate, vale, c_keep, c_y, c_core, c_diag):
    sources = vale.shape[0]
    width, grid_h = w_own.shape
    n_z = table.shape[0] // 2
    count = n_z // 2 + NSHIFT
    rows = n_z * 64
    chunks = sources // 2 // CHUNK
    return pl.pallas_call(
        tile_kernel,
        in_specs=[SMEM, SMEM, HBM, ANY] + [VMEM] * 5,
        out_specs=[VMEM, VMEM],
        out_shape=[
            jax.ShapeDtypeStruct((sources, n_z, 128), jnp.float32),
            jax.ShapeDtypeStruct((n_z + 1, 8, 128), jnp.int32),
        ],
        scratch_shapes=[
            pltpu.VMEM((2,) + w_own.shape, jnp.bfloat16),
            pltpu.VMEM((2, 2 * count, 8, CHUNK * width), jnp.float32),
            pltpu.VMEM((2 * count, 8, 2 * width), jnp.float32),
            pltpu.VMEM((2, 2) + c_keep.shape, jnp.bfloat16),
            pltpu.VMEM((chunks, rows, CHUNK * width), jnp.bfloat16),
            pltpu.VMEM((rows, 2 * width), jnp.bfloat16),
            pltpu.VMEM((rows, 2 * width), jnp.float32),
            pltpu.SemaphoreType.DMA((2,)),
        ],
        compiler_params=pltpu.CompilerParams(vmem_limit_bytes=36 * 1024 * 1024),
    )(table, place, *in_hbm(w_own), w_mate, vale, c_keep, c_y, c_core, c_diag)


def spread_kernel(place, cond_in, vale_in, gmap_in, out, cond, vale, gmap, arrived):
    width = cond.shape[2]
    fetches = [
        pltpu.make_async_copy(source, target, arrived.at[number])
        for number, (source, target) in enumerate(((cond_in, cond), (vale_in, vale), (gmap_in, gmap)))
    ]
    for fetch in fetches:
        fetch.start()
    for fetch in fetches:
        fetch.wait()
    places = (gmap[...] - place[1] * width).astype(jnp.float32)
    top = lax.broadcasted_iota(jnp.int32, (8, 128), 0) == 0
    places = jnp.where(top, places[:, :128], places[:, 128:]).astype(jnp.bfloat16)
    for dest in range(out.shape[0]):
        out[dest, :, :width] = vale[0]
        out[dest, :, width : 2 * width] = cond[0]
        out[dest, :, 2 * width :] = places


def spread(place, cond, vale, gmap, dests):
    return pl.pallas_call(
        spread_kernel,
        in_specs=[SMEM] + [HBM] * 3,
        out_specs=VMEM,
        out_shape=jax.ShapeDtypeStruct((dests, 8, 2 * cond.shape[2] + 128), jnp.bfloat16),
        scratch_shapes=[
            pltpu.VMEM(cond.shape, jnp.bfloat16),
            pltpu.VMEM(vale.shape, jnp.bfloat16),
            pltpu.VMEM(gmap.shape, jnp.int32),
            pltpu.SemaphoreType.DMA((3,)),
        ],
        compiler_params=pltpu.CompilerParams(vmem_limit_bytes=4 * 1024 * 1024),
    )(place, *in_hbm(cond, vale, gmap))


def pack_kernel(place, got, v_out, keep, give):
    n_z = got.shape[0]
    width = (got.shape[2] - 128) // 2
    half_z = n_z // 2
    count = half_z + NSHIFT
    core = place[1] % 2
    row_id = lax.broadcasted_iota(jnp.int32, (8, 128), 0)
    for half in range(2):
        spots = [(half * half_z + entry - NSHIFT) % n_z for entry in range(count)]
        maps = []
        for first in range(0, count, 4):
            tile = jnp.zeros((8, 128), jnp.float32)
            for entry in range(first, min(first + 4, count)):
                pair = got[spots[entry], :, 2 * width :].astype(jnp.float32)
                tile = jnp.where(row_id == 2 * (entry - first), pair[0:1], tile)
                tile = jnp.where(row_id == 2 * (entry - first) + 1, pair[1:2], tile)
            maps.append(tile.astype(jnp.bfloat16))

        def fill(write, column, spots=spots, maps=maps):
            for entry, spot in enumerate(spots):
                write(entry_lanes(entry, width), got[spot, :, column * width : (column + 1) * width])
            for number, tile in enumerate(maps):
                write(pl.ds(count * width + 128 * number, 128), tile)

        for mine, c_out in ((True, keep), (False, give)):

            @pl.when((core == half) == mine)
            def _(c_out=c_out, fill=fill):
                def write(lanes, value):
                    c_out[:, lanes] = value

                fill(write, 1)

        for dest in range(half, v_out.shape[0], 2):

            def write(lanes, value, dest=dest):
                v_out[dest, :, lanes] = value

            fill(write, 0)


def pack(place, got, dests):
    n_z = got.shape[0]
    width = (got.shape[2] - 128) // 2
    count = n_z // 2 + NSHIFT
    shape = (8, count * width + 128 * (-(-count // 4)))
    return pl.pallas_call(
        pack_kernel,
        in_specs=[SMEM, VMEM],
        out_specs=[VMEM] * 3,
        out_shape=[
            jax.ShapeDtypeStruct((dests,) + shape, jnp.bfloat16),
            jax.ShapeDtypeStruct(shape, jnp.bfloat16),
            jax.ShapeDtypeStruct(shape, jnp.bfloat16),
        ],
        compiler_params=pltpu.CompilerParams(vmem_limit_bytes=8 * 1024 * 1024),
    )(place, got)


def total_kernel(shares, out):
    sources, rows, _ = shares.shape
    for y in range(2):
        for core in range(2):
            first = y * (sources // 2) + core
            total = shares[first]
            for source in range(first + 2, first + sources // 2, 2):
                total = total + shares[source]
            for pair in range(rows // 4):
                strip = total[4 * pair : 4 * pair + 4]
                for odd in range(2):
                    z = core * (rows // 2) + 2 * pair + odd
                    out[z, pl.ds(4 * y, 4), :] = strip


def totals(shares):
    n_z = shares.shape[1]
    return pl.pallas_call(
        total_kernel,
        in_specs=[VMEM],
        out_specs=VMEM,
        out_shape=jax.ShapeDtypeStruct((n_z, 8, 128), jnp.float32),
        compiler_params=pltpu.CompilerParams(vmem_limit_bytes=4 * 1024 * 1024),
    )(shares)


def pick_kernel(plan, rows, out):
    n_z = rows.shape[0]
    odd = plan[n_z, 0:4] == 1
    low = lax.broadcasted_iota(jnp.int32, (1, 128), 1) < 64
    for by in range(NSHIFT + 1):
        both = jnp.zeros((8, 128), jnp.float32)
        for z in range(n_z):
            both = jnp.where(plan[z] == by, rows[z], both)
        strip = both[:4] + both[4:]
        turned = pltpu.roll(strip, 64, 1)
        left = jnp.where(odd, turned, strip)
        right = jnp.where(odd, strip, turned)
        for side in range(2):
            line = jnp.where(low, left[2 * side : 2 * side + 1], right[2 * side + 1 : 2 * side + 2])
            out[by, :, pl.ds(128 * side, 128)] = line


def pick(plan, rows):
    return pl.pallas_call(
        pick_kernel,
        in_specs=[VMEM, VMEM],
        out_specs=VMEM,
        out_shape=jax.ShapeDtypeStruct((NSHIFT + 1, 1, 256), jnp.float32),
        compiler_params=pltpu.CompilerParams(vmem_limit_bytes=4 * 1024 * 1024),
    )(plan, rows)


def per_device(cond, vale, screen, qtable, gmap):
    n_ka = lax.axis_size("ka")
    n_ga = lax.axis_size("ga")
    n_z = n_ka // 2
    my_ka = lax.axis_index("ka")
    my_ga = lax.axis_index("ga")
    place = jnp.stack([my_ka, my_ga]).astype(jnp.int32)
    swap_core = [(i, i ^ 1) for i in range(n_ga)]
    swap_y = [(i, i ^ n_z) for i in range(n_ka)]
    swap_both = [(k * n_ga + g, (k ^ n_z) * n_ga + (g ^ 1)) for k in range(n_ka) for g in range(n_ga)]
    along_z = [list(range(n_z)), list(range(n_z, n_ka))]
    planes = [
        [(y * n_z + z) * n_ga + g for y in range(2) for g in range(n_ga)] for z in range(n_z)
    ]

    sent = spread(place, cond, vale, gmap, n_z)
    got = lax.all_to_all(sent, "ka", 0, 0, axis_index_groups=along_z)

    got, slab = lax.optimization_barrier((got, screen[0]))
    slab_mate = lax.ppermute(slab, "ga", swap_core)

    v_sent, c_keep, c_give = pack(place, got, 2 * n_ga)
    c_y = lax.ppermute(c_keep, "ka", swap_y)
    c_core = lax.ppermute(c_give, "ga", swap_core)
    c_diag = lax.ppermute(c_give, ("ka", "ga"), swap_both)
    v_all = lax.all_to_all(v_sent, ("ka", "ga"), 0, 0, axis_index_groups=planes)

    part, plan = tiles(qtable, place, slab, slab_mate, v_all, c_keep, c_y, c_core, c_diag)
    shares = lax.all_to_all(part, ("ka", "ga"), 0, 0, axis_index_groups=planes)
    rows = lax.all_to_all(totals(shares), "ka", 0, 0, axis_index_groups=along_z)
    return jnp.transpose(pick(plan, rows), (1, 0, 2))


def solution(mesh):
    in_specs = (P("ka", None, "ga"), P("ka", None, "ga"), P("ka", "ga", None), P(), P("ka", "ga"))
    out_specs = P("ka", None, "ga")
    return jax.shard_map(
        per_device, mesh=mesh, in_specs=in_specs, out_specs=out_specs, check_vma=False
    )
```

```python
import jax
import jax.numpy as jnp
from jax import lax
from jax.experimental import pallas as pl
from jax.experimental.pallas import tpu as pltpu
from jax.sharding import PartitionSpec as P

NSHIFT = 2
STEP_K = 4
CHUNK = 2
VMEM = pl.BlockSpec(memory_space=pltpu.VMEM)
SMEM = pl.BlockSpec(memory_space=pltpu.SMEM)
HBM = pl.BlockSpec(memory_space=pltpu.HBM)
ANY = pl.BlockSpec(memory_space=pl.ANY)


def in_hbm(*arrays):
    return [pltpu.with_memory_space_constraint(array, pltpu.HBM) for array in arrays]


def last_dims(a, b):
    return lax.dot_general(a, b, (((1,), (1,)), ((), ())), preferred_element_type=jnp.float32)


def density(own, far):
    product = own[:, None, :] * far[None, :, :]
    return product.reshape(64, own.shape[-1]).astype(jnp.bfloat16)


def lane_gather(source, places):
    return jnp.take_along_axis(source, places, axis=1, mode="promise_in_bounds")


def mapped(source, places):
    low, high = source[:, :128], source[:, 128:]
    sides = []
    for part in (places[:, :128], places[:, 128:]):
        inner = part & 127
        sides.append(jnp.where(part < 128, lane_gather(low, inner), lane_gather(high, inner)))
    return jnp.concatenate(sides, axis=1)


def entry_lanes(entry, width):
    return pl.ds(entry * width, width)


def map_entries(packed, count, width, store):
    maps = []
    for first in range(0, 2 * count, 8):
        lanes = pl.ds(count * width + 16 * first, 128)
        maps.append(packed[:, lanes].astype(jnp.float32).astype(jnp.int32))
    for entry in range(count):
        sides = []
        for side in range(2):
            row = 2 * entry + side
            places = maps[row // 8][row % 8 : row % 8 + 1]
            sides.append(jnp.broadcast_to(places, (8, 128)))
        source = packed[:, entry_lanes(entry, width)].astype(jnp.float32)
        store(entry, mapped(source, jnp.concatenate(sides, axis=1)))


def tile_kernel(
    table, place, w_own, w_mate, vale, c_keep, c_y, c_core, c_diag, out, plan,
    slabs, far_v, far_c, c_all, pv, pc, image, wide, arrived,
):
    n_blocks = vale.shape[0] // 2
    width = w_own.shape[0]
    n_z = out.shape[1]
    half_z = n_z // 2
    count = half_z + NSHIFT
    my_ka, core = place[0], place[1] % 2
    my_y = my_ka // n_z
    shift = sum(jnp.where(table[by, 0] == my_ka, by, 0) for by in range(1, NSHIFT + 1))
    chunks = n_blocks // CHUNK
    spans = [pl.ds(chunk * CHUNK * width, CHUNK * width) for chunk in range(chunks)]
    fetches = [
        pltpu.make_async_copy(source, slabs.at[side], arrived.at[side])
        for side, source in enumerate((w_own, w_mate))
    ]
    for fetch in fetches:
        fetch.start()

    upper = lax.broadcasted_iota(jnp.int32, (4, 128), 0) >= 2
    for z in range(n_z):
        tile = jnp.full((4, 128), -1, jnp.int32)
        for by in range(NSHIFT + 1):
            holder = table[by, 0]
            row = jnp.where(upper, holder - n_z, holder)
            tile = jnp.where(row == z, by, tile)
        plan[z] = tile

    def partner(y, entry):
        other = entry - shift
        crossed = jnp.logical_and(core == 0, other < NSHIFT)
        return jnp.where(crossed, 1 - y, y) * count + other

    def form(chunk):
        slot = chunk % far_v.shape[0]
        for y in range(2):
            for inner in range(CHUNK):
                block = chunk * CHUNK + inner

                def store(entry, value):
                    far_v[slot, y * count + entry, :, pl.ds(inner * width, width)] = value

                map_entries(vale.at[y * n_blocks + block], count, width, store)
        for y in range(2):
            for z in range(half_z):
                rows = pl.ds(64 * (y * half_z + z), 64)
                row = partner(y, z + NSHIFT)
                for inner in range(CHUNK):
                    block = chunk * CHUNK + inner
                    lanes = pl.ds(inner * width, width)
                    own = vale[y * n_blocks + block, :, entry_lanes(z + NSHIFT, width)]
                    own = own.astype(jnp.float32)
                    pv[chunk, rows, lanes] = density(own, far_v[slot, row, :, lanes])

    def form_c():
        for side, (mine, other) in enumerate(((c_keep, c_y), (c_core, c_diag))):
            c_all[side, my_y] = mine[...]
            c_all[side, 1 - my_y] = other[...]
        for side in range(2):
            lanes = pl.ds(side * width, width)
            for y in range(2):

                def store(entry, value):
                    far_c[y * count + entry, :, lanes] = value

                map_entries(c_all.at[side, y], count, width, store)
            for y in range(2):
                for z in range(half_z):
                    own = c_all[side, y, :, entry_lanes(z + NSHIFT, width)].astype(jnp.float32)
                    rows = pl.ds(64 * (y * half_z + z), 64)
                    pc[rows, lanes] = density(own, far_c[partner(y, z + NSHIFT), :, lanes])

    form(0)
    for fetch in fetches:
        fetch.wait()
    for chunk in range(chunks):
        if chunk + 1 < chunks:
            form(chunk + 1)
        else:
            form_c()
        for side in range(2):
            lanes = pl.ds(side * width, width)
            term = last_dims(pv[chunk], slabs[side, :, spans[chunk]])
            image[:, lanes] = term if chunk == 0 else image[:, lanes] + term

    low = lax.broadcasted_iota(jnp.int32, (64, 128), 1) < 64
    for y in range(2):
        for part in range(half_z // STEP_K):
            rows = pl.ds(64 * (y * half_z + part * STEP_K), 64 * STEP_K)
            full = last_dims(pc[rows, :], image[rows, :].astype(jnp.bfloat16))
            for pair in range(STEP_K // 2):
                base = 128 * pair
                strip = full[:, base : base + 128]
                tile = jnp.where(low, strip[base : base + 64], strip[base + 64 : base + 128])
                wide[pl.ds(16 * y, 16), pl.ds(8 * part + 4 * pair, 4), :] = tile.reshape(16, 4, 128)
    out[...] = wide[...].astype(jnp.bfloat16)


def tiles(table, place, w_own, w_mate, vale, c_keep, c_y, c_core, c_diag):
    sources = vale.shape[0]
    width, grid_h = w_own.shape
    n_z = table.shape[0] // 2
    count = n_z // 2 + NSHIFT
    rows = n_z * 64
    chunks = sources // 2 // CHUNK
    return pl.pallas_call(
        tile_kernel,
        in_specs=[SMEM, SMEM, HBM, ANY] + [VMEM] * 5,
        out_specs=[VMEM, VMEM],
        out_shape=[
            jax.ShapeDtypeStruct((sources, n_z, 128), jnp.bfloat16),
            jax.ShapeDtypeStruct((n_z, 4, 128), jnp.int32),
        ],
        scratch_shapes=[
            pltpu.VMEM((2,) + w_own.shape, jnp.bfloat16),
            pltpu.VMEM((2, 2 * count, 8, CHUNK * width), jnp.float32),
            pltpu.VMEM((2 * count, 8, 2 * width), jnp.float32),
            pltpu.VMEM((2, 2) + c_keep.shape, jnp.bfloat16),
            pltpu.VMEM((chunks, rows, CHUNK * width), jnp.bfloat16),
            pltpu.VMEM((rows, 2 * width), jnp.bfloat16),
            pltpu.VMEM((rows, 2 * width), jnp.float32),
            pltpu.VMEM((sources, n_z, 128), jnp.float32),
            pltpu.SemaphoreType.DMA((2,)),
        ],
        compiler_params=pltpu.CompilerParams(vmem_limit_bytes=36 * 1024 * 1024),
    )(table, place, *in_hbm(w_own), w_mate, vale, c_keep, c_y, c_core, c_diag)


def spread_kernel(place, cond_in, vale_in, gmap_in, out, cond, vale, gmap, arrived):
    width = cond.shape[2]
    fetches = [
        pltpu.make_async_copy(source, target, arrived.at[number])
        for number, (source, target) in enumerate(((cond_in, cond), (vale_in, vale), (gmap_in, gmap)))
    ]
    for fetch in fetches:
        fetch.start()
    for fetch in fetches:
        fetch.wait()
    places = (gmap[...] - place[1] * width).astype(jnp.float32)
    top = lax.broadcasted_iota(jnp.int32, (8, 128), 0) == 0
    places = jnp.where(top, places[:, :128], places[:, 128:]).astype(jnp.bfloat16)
    for dest in range(out.shape[0]):
        out[dest, :, :width] = vale[0]
        out[dest, :, width : 2 * width] = cond[0]
        out[dest, :, 2 * width :] = places


def spread(place, cond, vale, gmap, dests):
    return pl.pallas_call(
        spread_kernel,
        in_specs=[SMEM] + [HBM] * 3,
        out_specs=VMEM,
        out_shape=jax.ShapeDtypeStruct((dests, 8, 2 * cond.shape[2] + 128), jnp.bfloat16),
        scratch_shapes=[
            pltpu.VMEM(cond.shape, jnp.bfloat16),
            pltpu.VMEM(vale.shape, jnp.bfloat16),
            pltpu.VMEM(gmap.shape, jnp.int32),
            pltpu.SemaphoreType.DMA((3,)),
        ],
        compiler_params=pltpu.CompilerParams(vmem_limit_bytes=4 * 1024 * 1024),
    )(place, *in_hbm(cond, vale, gmap))


def pack_kernel(place, got, v_out, keep, give, block, sent):
    n_z = got.shape[0]
    width = (got.shape[2] - 128) // 2
    half_z = n_z // 2
    count = half_z + NSHIFT
    core = place[1] % 2
    row_id = lax.broadcasted_iota(jnp.int32, (8, 128), 0)
    started = []
    for half in range(2):
        spots = [(half * half_z + entry - NSHIFT) % n_z for entry in range(count)]
        maps = []
        for first in range(0, count, 4):
            tile = jnp.zeros((8, 128), jnp.float32)
            for entry in range(first, min(first + 4, count)):
                pair = got[spots[entry], :, 2 * width :].astype(jnp.float32)
                tile = jnp.where(row_id == 2 * (entry - first), pair[0:1], tile)
                tile = jnp.where(row_id == 2 * (entry - first) + 1, pair[1:2], tile)
            maps.append(tile.astype(jnp.bfloat16))

        def fill(target, column, spots=spots, maps=maps):
            for entry, spot in enumerate(spots):
                lanes = pl.ds(column * width, width)
                target[:, entry_lanes(entry, width)] = got[spot, :, lanes]
            for number, tile in enumerate(maps):
                target[:, pl.ds(count * width + 128 * number, 128)] = tile

        fill(block.at[half], 0)
        copies = [
            pltpu.make_async_copy(block.at[half], v_out.at[dest], sent.at[dest])
            for dest in range(half, v_out.shape[0], 2)
        ]
        for copy in copies:
            copy.start()
        started += copies
        for mine, c_out in ((True, keep), (False, give)):

            @pl.when((core == half) == mine)
            def _(c_out=c_out, fill=fill):
                fill(c_out, 1)

    for copy in started:
        copy.wait()


def pack(place, got, dests):
    n_z = got.shape[0]
    width = (got.shape[2] - 128) // 2
    count = n_z // 2 + NSHIFT
    shape = (8, count * width + 128 * (-(-count // 4)))
    return pl.pallas_call(
        pack_kernel,
        in_specs=[SMEM, VMEM],
        out_specs=[ANY, VMEM, VMEM],
        out_shape=[
            jax.ShapeDtypeStruct((dests,) + shape, jnp.bfloat16),
            jax.ShapeDtypeStruct(shape, jnp.bfloat16),
            jax.ShapeDtypeStruct(shape, jnp.bfloat16),
        ],
        scratch_shapes=[
            pltpu.VMEM((2,) + shape, jnp.bfloat16),
            pltpu.SemaphoreType.DMA((dests,)),
        ],
        compiler_params=pltpu.CompilerParams(vmem_limit_bytes=8 * 1024 * 1024),
    )(place, got)


def total_kernel(shares, out):
    sources, rows, _ = shares.shape
    low = lax.broadcasted_iota(jnp.int32, (1, 128), 1) < 64
    for core in range(2):
        sums = []
        for y in range(2):
            first = y * (sources // 2) + core
            total = shares[first].astype(jnp.float32)
            for source in range(first + 2, first + sources // 2, 2):
                total = total + shares[source].astype(jnp.float32)
            sums.append((total, pltpu.roll(total, 64, 1)))
        for pair in range(rows // 4):
            for odd in range(2):
                lines = []
                for strip, turned in sums:
                    left, right = (turned, strip) if odd else (strip, turned)
                    for row in (4 * pair, 4 * pair + 2):
                        lines.append(jnp.where(low, left[row : row + 1], right[row + 1 : row + 2]))
                out[core * (rows // 2) + 2 * pair + odd] = jnp.concatenate(lines, axis=0)


def totals(shares):
    n_z = shares.shape[1]
    return pl.pallas_call(
        total_kernel,
        in_specs=[VMEM],
        out_specs=VMEM,
        out_shape=jax.ShapeDtypeStruct((n_z, 4, 128), jnp.float32),
        compiler_params=pltpu.CompilerParams(vmem_limit_bytes=4 * 1024 * 1024),
    )(shares)


def pick_kernel(plan, rows, out):
    for by in range(NSHIFT + 1):
        both = jnp.zeros((4, 128), jnp.float32)
        for z in range(rows.shape[0]):
            both = jnp.where(plan[z] == by, rows[z], both)
        pair = both[:2] + both[2:]
        for side in range(2):
            out[by, :, pl.ds(128 * side, 128)] = pair[side : side + 1]


def pick(plan, rows):
    return pl.pallas_call(
        pick_kernel,
        in_specs=[VMEM, VMEM],
        out_specs=VMEM,
        out_shape=jax.ShapeDtypeStruct((NSHIFT + 1, 1, 256), jnp.float32),
        compiler_params=pltpu.CompilerParams(vmem_limit_bytes=4 * 1024 * 1024),
    )(plan, rows)


def per_device(cond, vale, screen, qtable, gmap):
    n_ka = lax.axis_size("ka")
    n_ga = lax.axis_size("ga")
    n_z = n_ka // 2
    my_ka = lax.axis_index("ka")
    my_ga = lax.axis_index("ga")
    place = jnp.stack([my_ka, my_ga]).astype(jnp.int32)
    swap_core = [(i, i ^ 1) for i in range(n_ga)]
    swap_y = [(i, i ^ n_z) for i in range(n_ka)]
    swap_both = [(k * n_ga + g, (k ^ n_z) * n_ga + (g ^ 1)) for k in range(n_ka) for g in range(n_ga)]
    along_z = [list(range(n_z)), list(range(n_z, n_ka))]
    planes = [
        [(y * n_z + z) * n_ga + g for y in range(2) for g in range(n_ga)] for z in range(n_z)
    ]

    slab = screen[0]
    slab_mate = lax.ppermute(slab, "ga", swap_core)

    sent = spread(place, cond, vale, gmap, n_z)
    got = lax.all_to_all(sent, "ka", 0, 0, axis_index_groups=along_z)

    v_sent, c_keep, c_give = pack(place, got, 2 * n_ga)
    c_y = lax.ppermute(c_keep, "ka", swap_y)
    c_core = lax.ppermute(c_give, "ga", swap_core)
    c_diag = lax.ppermute(c_give, ("ka", "ga"), swap_both)
    v_all = lax.all_to_all(v_sent, ("ka", "ga"), 0, 0, axis_index_groups=planes)

    part, plan = tiles(qtable, place, slab, slab_mate, v_all, c_keep, c_y, c_core, c_diag)
    shares = lax.all_to_all(part, ("ka", "ga"), 0, 0, axis_index_groups=planes)
    rows = lax.all_to_all(totals(shares), "ka", 0, 0, axis_index_groups=along_z)
    return jnp.transpose(pick(plan, rows), (1, 0, 2))


def solution(mesh):
    in_specs = (P("ka", None, "ga"), P("ka", None, "ga"), P("ka", "ga", None), P(), P("ka", "ga"))
    out_specs = P("ka", None, "ga")
    return jax.shard_map(
        per_device, mesh=mesh, in_specs=in_specs, out_specs=out_specs, check_vma=False
    )
```

```python
import jax
import jax.numpy as jnp
from jax import lax
from jax.experimental import pallas as pl
from jax.experimental.pallas import tpu as pltpu
from jax.sharding import PartitionSpec as P

NSHIFT = 2
STEP_K = 4
CHUNK = 2
VMEM = pl.BlockSpec(memory_space=pltpu.VMEM)
SMEM = pl.BlockSpec(memory_space=pltpu.SMEM)
HBM = pl.BlockSpec(memory_space=pltpu.HBM)
ANY = pl.BlockSpec(memory_space=pl.ANY)


def in_hbm(*arrays):
    return [pltpu.with_memory_space_constraint(array, pltpu.HBM) for array in arrays]


def last_dims(a, b):
    return lax.dot_general(a, b, (((1,), (1,)), ((), ())), preferred_element_type=jnp.float32)


def density(own, far):
    product = own[:, None, :] * far[None, :, :]
    return product.reshape(64, own.shape[-1]).astype(jnp.bfloat16)


def lane_gather(source, places):
    return jnp.take_along_axis(source, places, axis=1, mode="promise_in_bounds")


def mapped(source, places):
    low, high = source[:, :128], source[:, 128:]
    sides = []
    for part in (places[:, :128], places[:, 128:]):
        inner = part & 127
        sides.append(jnp.where(part < 128, lane_gather(low, inner), lane_gather(high, inner)))
    return jnp.concatenate(sides, axis=1)


def entry_lanes(entry, width):
    return pl.ds(entry * width, width)


def map_entries(packed, count, width, store):
    maps = []
    for first in range(0, 2 * count, 8):
        lanes = pl.ds(count * width + 16 * first, 128)
        maps.append(packed[:, lanes].astype(jnp.float32).astype(jnp.int32))
    for entry in range(count):
        sides = []
        for side in range(2):
            row = 2 * entry + side
            places = maps[row // 8][row % 8 : row % 8 + 1]
            sides.append(jnp.broadcast_to(places, (8, 128)))
        source = packed[:, entry_lanes(entry, width)].astype(jnp.float32)
        store(entry, mapped(source, jnp.concatenate(sides, axis=1)))


def tile_kernel(
    table, place, w_own, w_mate, vale, c_keep, c_y, c_core, c_diag, out, plan,
    slabs, far_v, far_c, c_all, pv, pc, image, wide, arrived,
):
    blocks = vale.shape[0] // 2
    width = w_own.shape[0]
    n_z = plan.shape[0]
    my_ka, core = place[0], place[1] % 2
    my_y = my_ka // n_z
    shift = sum(jnp.where(table[by, 0] == my_ka, by, 0) for by in range(1, NSHIFT + 1))
    fetches = [
        pltpu.make_async_copy(
            source.at[:, pl.ds(pl.multiple_of((2 * block + core) * width, width), width)],
            slabs.at[side, :, pl.ds(block * width, width)],
            arrived.at[side, block],
        )
        for block in range(blocks)
        for side, source in enumerate((w_own, w_mate))
    ]
    for fetch in fetches:
        fetch.start()

    upper = lax.broadcasted_iota(jnp.int32, (4, 128), 0) >= 2
    for z in range(n_z):
        tile = jnp.full((4, 128), -1, jnp.int32)
        for by in range(NSHIFT + 1):
            holder = table[by, 0]
            row = jnp.where(upper, holder - n_z, holder)
            tile = jnp.where(row == z, by, tile)
        plan[z] = tile

    def partner(k):
        return jnp.where(k < shift, k - shift + 2 * n_z, k - shift)

    def form(chunk):
        slot = chunk % far_v.shape[0]
        for y in range(2):
            for inner in range(CHUNK):
                source = y * blocks + chunk * CHUNK + inner

                def store(z, value):
                    far_v[slot, y * n_z + z, :, pl.ds(inner * width, width)] = value

                map_entries(vale.at[source], n_z, width, store)
        for k in range(2 * n_z):
            for inner in range(CHUNK):
                source = k // n_z * blocks + chunk * CHUNK + inner
                lanes = pl.ds(inner * width, width)
                own = vale[source, :, entry_lanes(k % n_z, width)].astype(jnp.float32)
                pv[chunk, pl.ds(64 * k, 64), lanes] = density(own, far_v[slot, partner(k), :, lanes])

    def form_c():
        for side, (mine, other) in enumerate(((c_keep, c_y), (c_core, c_diag))):
            c_all[side, my_y] = mine[...]
            c_all[side, 1 - my_y] = other[...]
        for side in range(2):
            lanes = pl.ds(side * width, width)
            for y in range(2):

                def store(z, value):
                    far_c[y * n_z + z, :, lanes] = value

                map_entries(c_all.at[side, y], n_z, width, store)
            for k in range(2 * n_z):
                own = c_all[side, k // n_z, :, entry_lanes(k % n_z, width)].astype(jnp.float32)
                pc[pl.ds(64 * k, 64), lanes] = density(own, far_c[partner(k), :, lanes])

    chunks = blocks // CHUNK
    form(0)
    for fetch in fetches:
        fetch.wait()
    for chunk in range(chunks):
        if chunk + 1 < chunks:
            form(chunk + 1)
        else:
            form_c()
        for side in range(2):
            lanes = pl.ds(side * width, width)
            term = last_dims(pv[chunk], slabs[side, :, pl.ds(chunk * CHUNK * width, CHUNK * width)])
            image[:, lanes] = term if chunk == 0 else image[:, lanes] + term

    low = lax.broadcasted_iota(jnp.int32, (64, 128), 1) < 64
    for y in range(2):
        for part in range(n_z // STEP_K):
            rows = pl.ds(64 * (y * n_z + part * STEP_K), 64 * STEP_K)
            full = last_dims(pc[rows, :], image[rows, :].astype(jnp.bfloat16))
            for pair in range(STEP_K // 2):
                base = 128 * pair
                strip = full[:, base : base + 128]
                tile = jnp.where(low, strip[base : base + 64], strip[base + 64 : base + 128])
                wide[pl.ds(16 * y, 16), pl.ds(8 * part + 4 * pair, 4), :] = tile.reshape(16, 4, 128)
    out[...] = wide[...].astype(jnp.bfloat16)


def tiles(table, place, w_own, w_mate, vale, c_keep, c_y, c_core, c_diag):
    sources = vale.shape[0]
    width = w_own.shape[0]
    n_z = table.shape[0] // 2
    rows = 2 * n_z * 64
    blocks = sources // 2
    chunks = blocks // CHUNK
    return pl.pallas_call(
        tile_kernel,
        in_specs=[SMEM, SMEM, HBM, ANY] + [VMEM] * 5,
        out_specs=[VMEM, VMEM],
        out_shape=[
            jax.ShapeDtypeStruct((2 * sources, 2 * n_z, 128), jnp.bfloat16),
            jax.ShapeDtypeStruct((n_z, 4, 128), jnp.int32),
        ],
        scratch_shapes=[
            pltpu.VMEM((2, width, blocks * width), jnp.bfloat16),
            pltpu.VMEM((2, 2 * n_z, 8, CHUNK * width), jnp.float32),
            pltpu.VMEM((2 * n_z, 8, 2 * width), jnp.float32),
            pltpu.VMEM((2, 2) + c_keep.shape, jnp.bfloat16),
            pltpu.VMEM((chunks, rows, CHUNK * width), jnp.bfloat16),
            pltpu.VMEM((rows, 2 * width), jnp.bfloat16),
            pltpu.VMEM((rows, 2 * width), jnp.float32),
            pltpu.VMEM((2 * sources, 2 * n_z, 128), jnp.float32),
            pltpu.SemaphoreType.DMA((2, blocks)),
        ],
        compiler_params=pltpu.CompilerParams(vmem_limit_bytes=36 * 1024 * 1024),
    )(table, place, *in_hbm(w_own), w_mate, vale, c_keep, c_y, c_core, c_diag)


def spread_kernel(place, cond_in, vale_in, gmap_in, out, cond, vale, gmap, arrived):
    width = cond.shape[2]
    fetches = [
        pltpu.make_async_copy(source, target, arrived.at[number])
        for number, (source, target) in enumerate(((cond_in, cond), (vale_in, vale), (gmap_in, gmap)))
    ]
    for fetch in fetches:
        fetch.start()
    for fetch in fetches:
        fetch.wait()
    places = (gmap[...] - place[1] * width).astype(jnp.float32)
    top = lax.broadcasted_iota(jnp.int32, (8, 128), 0) == 0
    places = jnp.where(top, places[:, :128], places[:, 128:]).astype(jnp.bfloat16)
    for dest in range(out.shape[0]):
        out[dest, :, :width] = vale[0]
        out[dest, :, width : 2 * width] = cond[0]
        out[dest, :, 2 * width :] = places


def spread(place, cond, vale, gmap, dests):
    return pl.pallas_call(
        spread_kernel,
        in_specs=[SMEM] + [HBM] * 3,
        out_specs=VMEM,
        out_shape=jax.ShapeDtypeStruct((dests, 8, 2 * cond.shape[2] + 128), jnp.bfloat16),
        scratch_shapes=[
            pltpu.VMEM(cond.shape, jnp.bfloat16),
            pltpu.VMEM(vale.shape, jnp.bfloat16),
            pltpu.VMEM(gmap.shape, jnp.int32),
            pltpu.SemaphoreType.DMA((3,)),
        ],
        compiler_params=pltpu.CompilerParams(vmem_limit_bytes=4 * 1024 * 1024),
    )(place, *in_hbm(cond, vale, gmap))


def pack_kernel(got, v_out, c_out, block, sent):
    n_z = got.shape[0]
    width = (got.shape[2] - 128) // 2
    row_id = lax.broadcasted_iota(jnp.int32, (8, 128), 0)
    maps = []
    for first in range(0, n_z, 4):
        tile = jnp.zeros((8, 128), jnp.float32)
        for z in range(first, first + 4):
            pair = got[z, :, 2 * width :].astype(jnp.float32)
            tile = jnp.where(row_id == 2 * (z - first), pair[0:1], tile)
            tile = jnp.where(row_id == 2 * (z - first) + 1, pair[1:2], tile)
        maps.append(tile.astype(jnp.bfloat16))

    def fill(target, column):
        for z in range(n_z):
            target[:, entry_lanes(z, width)] = got[z, :, pl.ds(column * width, width)]
        for number, tile in enumerate(maps):
            target[:, pl.ds(n_z * width + 128 * number, 128)] = tile

    fill(block, 0)
    copies = [
        pltpu.make_async_copy(block, v_out.at[dest], sent.at[dest])
        for dest in range(v_out.shape[0])
    ]
    for copy in copies:
        copy.start()
    fill(c_out, 1)
    for copy in copies:
        copy.wait()


def pack(got, dests):
    n_z = got.shape[0]
    width = (got.shape[2] - 128) // 2
    shape = (8, n_z * width + 128 * (n_z // 4))
    return pl.pallas_call(
        pack_kernel,
        in_specs=[VMEM],
        out_specs=[ANY, VMEM],
        out_shape=[
            jax.ShapeDtypeStruct((dests,) + shape, jnp.bfloat16),
            jax.ShapeDtypeStruct(shape, jnp.bfloat16),
        ],
        scratch_shapes=[
            pltpu.VMEM(shape, jnp.bfloat16),
            pltpu.SemaphoreType.DMA((dests,)),
        ],
        compiler_params=pltpu.CompilerParams(vmem_limit_bytes=8 * 1024 * 1024),
    )(got)


def total_kernel(shares, out):
    sources, rows, _ = shares.shape
    low = lax.broadcasted_iota(jnp.int32, (1, 128), 1) < 64
    sums = []
    for y in range(2):
        first = y * (sources // 2)
        total = shares[first].astype(jnp.float32)
        for source in range(first + 1, first + sources // 2):
            total = total + shares[source].astype(jnp.float32)
        sums.append((total, pltpu.roll(total, 64, 1)))
    for z in range(rows // 2):
        lines = []
        for strip, turned in sums:
            left, right = (turned, strip) if z % 2 else (strip, turned)
            for row in (4 * (z // 2), 4 * (z // 2) + 2):
                lines.append(jnp.where(low, left[row : row + 1], right[row + 1 : row + 2]))
        out[z] = jnp.concatenate(lines, axis=0)


def totals(shares):
    n_z = shares.shape[1] // 2
    return pl.pallas_call(
        total_kernel,
        in_specs=[VMEM],
        out_specs=VMEM,
        out_shape=jax.ShapeDtypeStruct((n_z, 4, 128), jnp.float32),
        compiler_params=pltpu.CompilerParams(vmem_limit_bytes=4 * 1024 * 1024),
    )(shares)


def pick_kernel(plan, rows, out):
    for by in range(NSHIFT + 1):
        both = jnp.zeros((4, 128), jnp.float32)
        for z in range(rows.shape[0]):
            both = jnp.where(plan[z] == by, rows[z], both)
        pair = both[:2] + both[2:]
        for side in range(2):
            out[by, :, pl.ds(128 * side, 128)] = pair[side : side + 1]


def pick(plan, rows):
    return pl.pallas_call(
        pick_kernel,
        in_specs=[VMEM, VMEM],
        out_specs=VMEM,
        out_shape=jax.ShapeDtypeStruct((NSHIFT + 1, 1, 256), jnp.float32),
        compiler_params=pltpu.CompilerParams(vmem_limit_bytes=4 * 1024 * 1024),
    )(plan, rows)


def per_device(cond, vale, screen, qtable, gmap):
    n_ka = lax.axis_size("ka")
    n_ga = lax.axis_size("ga")
    n_z = n_ka // 2
    my_ka = lax.axis_index("ka")
    my_ga = lax.axis_index("ga")
    place = jnp.stack([my_ka, my_ga]).astype(jnp.int32)
    swap_core = [(i, i ^ 1) for i in range(n_ga)]
    swap_y = [(i, i ^ n_z) for i in range(n_ka)]
    swap_both = [(k * n_ga + g, (k ^ n_z) * n_ga + (g ^ 1)) for k in range(n_ka) for g in range(n_ga)]
    along_z = [list(range(n_z)), list(range(n_z, n_ka))]
    planes = [
        [(y * n_z + z) * n_ga + g for y in range(2) for g in range(n_ga)] for z in range(n_z)
    ]
    same_core = [plane[core::2] for plane in planes for core in range(2)]

    sent = spread(place, cond, vale, gmap, n_z)
    sent, slab = lax.optimization_barrier((sent, screen[0]))
    slab_mate = lax.ppermute(slab, "ga", swap_core)
    got = lax.all_to_all(sent, "ka", 0, 0, axis_index_groups=along_z)

    v_sent, c_keep = pack(got, n_ga)
    c_y = lax.ppermute(c_keep, "ka", swap_y)
    c_core = lax.ppermute(c_keep, "ga", swap_core)
    c_diag = lax.ppermute(c_keep, ("ka", "ga"), swap_both)
    v_all = lax.all_to_all(v_sent, ("ka", "ga"), 0, 0, axis_index_groups=same_core)

    part, plan = tiles(qtable, place, slab, slab_mate, v_all, c_keep, c_y, c_core, c_diag)
    shares = lax.all_to_all(part, ("ka", "ga"), 0, 0, axis_index_groups=planes)
    rows = lax.all_to_all(totals(shares), "ka", 0, 0, axis_index_groups=along_z)
    return jnp.transpose(pick(plan, rows), (1, 0, 2))


def solution(mesh):
    in_specs = (P("ka", None, "ga"), P("ka", None, "ga"), P("ka", "ga", None), P(), P("ka", "ga"))
    out_specs = P("ka", None, "ga")
    return jax.shard_map(
        per_device, mesh=mesh, in_specs=in_specs, out_specs=out_specs, check_vma=False
    )
```

```python
import jax
import jax.numpy as jnp
from jax import lax
from jax.experimental import pallas as pl
from jax.experimental.pallas import tpu as pltpu
from jax.sharding import PartitionSpec as P

NSHIFT = 2
STEP_K = 4
BAND_K = 16
CHUNKS = ((0,), (1,2,3), (4,5,6,7))
VMEM = pl.BlockSpec(memory_space=pltpu.VMEM)
SMEM = pl.BlockSpec(memory_space=pltpu.SMEM)
HBM = pl.BlockSpec(memory_space=pltpu.HBM)
ANY = pl.BlockSpec(memory_space=pl.ANY)


def in_hbm(*arrays):
    return [pltpu.with_memory_space_constraint(array, pltpu.HBM) for array in arrays]


def last_dims(a, b):
    return lax.dot_general(a, b, (((1,), (1,)), ((), ())), preferred_element_type=jnp.float32)


def density(own, far):
    product = own[:, None, :] * far[None, :, :]
    return product.reshape(64, own.shape[-1]).astype(jnp.bfloat16)


def lane_gather(source, places):
    return jnp.take_along_axis(source, places, axis=1, mode="promise_in_bounds")


def mapped(source, places):
    low, high = source[:, :128], source[:, 128:]
    sides = []
    for part in (places[:, :128], places[:, 128:]):
        inner = part & 127
        sides.append(jnp.where(part < 128, lane_gather(low, inner), lane_gather(high, inner)))
    return jnp.concatenate(sides, axis=1)


def entry_lanes(entry, width):
    return pl.ds(entry * width, width)


def map_entries(packed, count, width, store):
    maps = []
    for first in range(0, 2 * count, 8):
        lanes = pl.ds(count * width + 16 * first, 128)
        maps.append(packed[:, lanes].astype(jnp.float32).astype(jnp.int32))
    for entry in range(count):
        sides = []
        for side in range(2):
            row = 2 * entry + side
            places = maps[row // 8][row % 8 : row % 8 + 1]
            sides.append(jnp.broadcast_to(places, (8, 128)))
        source = packed[:, entry_lanes(entry, width)].astype(jnp.float32)
        store(entry, mapped(source, jnp.concatenate(sides, axis=1)))


def tile_kernel(
    table, place, w_own, w_mate, vale, c_keep, c_y, c_core, c_diag, out, plan,
    slabs, far_v, far_c, c_all, pv, pc, image, wide, arrived, joined,
):
    blocks = vale.shape[0] // 2
    width = w_own.shape[0]
    n_z = plan.shape[0]
    my_ka, core = place[0], place[1] % 2
    my_y = my_ka // n_z
    shift = sum(jnp.where(table[by, 0] == my_ka, by, 0) for by in range(1, NSHIFT + 1))
    fetches = [
        pltpu.make_async_copy(
            source.at[:, pl.ds(pl.multiple_of((2 * block + core) * width, width), width)],
            slabs.at[side, :, pl.ds(block * width, width)],
            arrived.at[side, block],
        )
        for block in range(blocks)
        for side, source in enumerate((w_own, w_mate))
    ]
    fetches += [
        pltpu.make_async_copy(source, c_all.at[side, y], joined.at[side, other])
        for side, pair in enumerate(((c_keep, c_y), (c_core, c_diag)))
        for other, (source, y) in enumerate(zip(pair, (my_y, 1 - my_y)))
    ]
    for fetch in fetches:
        fetch.start()

    upper = lax.broadcasted_iota(jnp.int32, (4, 128), 0) >= 2
    for z in range(n_z):
        tile = jnp.full((4, 128), -1, jnp.int32)
        for by in range(NSHIFT + 1):
            holder = table[by, 0]
            row = jnp.where(upper, holder - n_z, holder)
            tile = jnp.where(row == z, by, tile)
        plan[z] = tile

    def partner(k):
        return jnp.where(k < shift, k - shift + 2 * n_z, k - shift)

    def form(number):
        slot = number % far_v.shape[0]
        for y in range(2):
            for inner, block in enumerate(CHUNKS[number]):

                def store(z, value):
                    far_v[slot, y * n_z + z, :, pl.ds(inner * width, width)] = value

                map_entries(vale.at[y * blocks + block], n_z, width, store)
        for k in range(2 * n_z):
            for inner, block in enumerate(CHUNKS[number]):
                far = far_v[slot, partner(k), :, pl.ds(inner * width, width)]
                own = vale[k // n_z * blocks + block, :, entry_lanes(k % n_z, width)]
                own = own.astype(jnp.float32)
                pv[pl.ds(64 * k, 64), pl.ds(block * width, width)] = density(own, far)

    def form_c():
        for side in range(2):
            lanes = pl.ds(side * width, width)
            for y in range(2):

                def store(z, value):
                    far_c[y * n_z + z, :, lanes] = value

                map_entries(c_all.at[side, y], n_z, width, store)
            for k in range(2 * n_z):
                own = c_all[side, k // n_z, :, entry_lanes(k % n_z, width)].astype(jnp.float32)
                pc[pl.ds(64 * k, 64), lanes] = density(own, far_c[partner(k), :, lanes])

    def term(rows, number, side):
        span = pl.ds(CHUNKS[number][0] * width, len(CHUNKS[number]) * width)
        return last_dims(pv[rows, span], slabs[side, :, span])

    sides = [pl.ds(side * width, width) for side in range(2)]
    last = len(CHUNKS) - 1
    form(0)
    for fetch in fetches:
        fetch.wait()
    for number in range(last):
        form(number + 1)
        if number + 1 == last:
            form_c()
        for side, lanes in enumerate(sides):
            part = term(pl.ds(0, pv.shape[0]), number, side)
            image[:, lanes] = part if number == 0 else image[:, lanes] + part

    low = lax.broadcasted_iota(jnp.int32, (64, 128), 1) < 64
    for first in range(0, 2 * n_z, BAND_K):
        rows = pl.ds(64 * first, 64 * BAND_K)
        bands = [
            (image[rows, lanes] + term(rows, last, side)).astype(jnp.bfloat16)
            for side, lanes in enumerate(sides)
        ]
        for step in range(0, BAND_K, STEP_K):
            full = None
            for lanes, band in zip(sides, bands):
                band = band[64 * step : 64 * (step + STEP_K)]
                part = last_dims(pc[pl.ds(64 * (first + step), 64 * STEP_K), lanes], band)
                full = part if full is None else full + part
            for pair in range(STEP_K // 2):
                base = 128 * pair
                strip = full[:, base : base + 128]
                tile = jnp.where(low, strip[base : base + 64], strip[base + 64 : base + 128])
                k = first + step + 2 * pair
                dests = pl.ds(16 * (k // n_z), 16)
                wide[dests, pl.ds(2 * (k % n_z), 4), :] = tile.reshape(16, 4, 128)
    out[...] = wide[...].astype(jnp.bfloat16)


def tiles(table, place, w_own, w_mate, vale, c_keep, c_y, c_core, c_diag):
    sources = vale.shape[0]
    width = w_own.shape[0]
    n_z = table.shape[0] // 2
    rows = 2 * n_z * 64
    blocks = sources // 2
    wide = max(len(chunk) for chunk in CHUNKS) * width
    return pl.pallas_call(
        tile_kernel,
        in_specs=[SMEM, SMEM, HBM, ANY, VMEM] + [ANY] * 4,
        out_specs=[VMEM, VMEM],
        out_shape=[
            jax.ShapeDtypeStruct((2 * sources, 2 * n_z, 128), jnp.bfloat16),
            jax.ShapeDtypeStruct((n_z, 4, 128), jnp.int32),
        ],
        scratch_shapes=[
            pltpu.VMEM((2, width, blocks * width), jnp.bfloat16),
            pltpu.VMEM((2, 2 * n_z, 8, wide), jnp.float32),
            pltpu.VMEM((2 * n_z, 8, 2 * width), jnp.float32),
            pltpu.VMEM((2, 2) + c_keep.shape, jnp.bfloat16),
            pltpu.VMEM((rows, blocks * width), jnp.bfloat16),
            pltpu.VMEM((rows, 2 * width), jnp.bfloat16),
            pltpu.VMEM((rows, 2 * width), jnp.float32),
            pltpu.VMEM((2 * sources, 2 * n_z, 128), jnp.float32),
            pltpu.SemaphoreType.DMA((2, blocks)),
            pltpu.SemaphoreType.DMA((2, 2)),
        ],
        compiler_params=pltpu.CompilerParams(vmem_limit_bytes=28 * 1024 * 1024),
    )(table, place, *in_hbm(w_own), w_mate, vale, c_keep, c_y, c_core, c_diag)


def spread_kernel(place, cond_in, vale_in, gmap_in, out, cond, vale, gmap, arrived):
    width = cond.shape[2]
    fetches = [
        pltpu.make_async_copy(source, target, arrived.at[number])
        for number, (source, target) in enumerate(((cond_in, cond), (vale_in, vale), (gmap_in, gmap)))
    ]
    for fetch in fetches:
        fetch.start()
    for fetch in fetches:
        fetch.wait()
    places = (gmap[...] - place[1] * width).astype(jnp.float32)
    top = lax.broadcasted_iota(jnp.int32, (8, 128), 0) == 0
    places = jnp.where(top, places[:, :128], places[:, 128:]).astype(jnp.bfloat16)
    for dest in range(out.shape[0]):
        out[dest, :, :width] = vale[0]
        out[dest, :, width : 2 * width] = cond[0]
        out[dest, :, 2 * width :] = places


def spread(place, cond, vale, gmap, dests):
    return pl.pallas_call(
        spread_kernel,
        in_specs=[SMEM] + [HBM] * 3,
        out_specs=VMEM,
        out_shape=jax.ShapeDtypeStruct((dests, 8, 2 * cond.shape[2] + 128), jnp.bfloat16),
        scratch_shapes=[
            pltpu.VMEM(cond.shape, jnp.bfloat16),
            pltpu.VMEM(vale.shape, jnp.bfloat16),
            pltpu.VMEM(gmap.shape, jnp.int32),
            pltpu.SemaphoreType.DMA((3,)),
        ],
        compiler_params=pltpu.CompilerParams(vmem_limit_bytes=4 * 1024 * 1024),
    )(place, *in_hbm(cond, vale, gmap))


def pack_kernel(got, v_out, c_out, block, sent):
    n_z = got.shape[0]
    width = (got.shape[2] - 128) // 2
    row_id = lax.broadcasted_iota(jnp.int32, (8, 128), 0)
    maps = []
    for first in range(0, n_z, 4):
        tile = jnp.zeros((8, 128), jnp.float32)
        for z in range(first, first + 4):
            pair = got[z, :, 2 * width :].astype(jnp.float32)
            tile = jnp.where(row_id == 2 * (z - first), pair[0:1], tile)
            tile = jnp.where(row_id == 2 * (z - first) + 1, pair[1:2], tile)
        maps.append(tile.astype(jnp.bfloat16))

    def fill(target, column):
        for z in range(n_z):
            target[:, entry_lanes(z, width)] = got[z, :, pl.ds(column * width, width)]
        for number, tile in enumerate(maps):
            target[:, pl.ds(n_z * width + 128 * number, 128)] = tile

    fill(block, 0)
    copies = [
        pltpu.make_async_copy(block, v_out.at[dest], sent.at[dest])
        for dest in range(v_out.shape[0])
    ]
    for copy in copies:
        copy.start()
    fill(c_out, 1)
    for copy in copies:
        copy.wait()


def pack(got, dests):
    n_z = got.shape[0]
    width = (got.shape[2] - 128) // 2
    shape = (8, n_z * width + 128 * (n_z // 4))
    return pl.pallas_call(
        pack_kernel,
        in_specs=[VMEM],
        out_specs=[HBM, VMEM],
        out_shape=[
            pltpu.HBM((dests,) + shape, jnp.bfloat16),
            jax.ShapeDtypeStruct(shape, jnp.bfloat16),
        ],
        scratch_shapes=[
            pltpu.VMEM(shape, jnp.bfloat16),
            pltpu.SemaphoreType.DMA((dests,)),
        ],
        compiler_params=pltpu.CompilerParams(vmem_limit_bytes=8 * 1024 * 1024),
    )(got)


def total_kernel(shares, out):
    sources, rows, _ = shares.shape
    low = lax.broadcasted_iota(jnp.int32, (1, 128), 1) < 64
    sums = []
    for y in range(2):
        first = y * (sources // 2)
        total = shares[first].astype(jnp.float32)
        for source in range(first + 1, first + sources // 2):
            total = total + shares[source].astype(jnp.float32)
        sums.append((total, pltpu.roll(total, 64, 1)))
    for z in range(rows // 2):
        lines = []
        for strip, turned in sums:
            left, right = (turned, strip) if z % 2 else (strip, turned)
            for row in (4 * (z // 2), 4 * (z // 2) + 2):
                lines.append(jnp.where(low, left[row : row + 1], right[row + 1 : row + 2]))
        out[z] = jnp.concatenate(lines, axis=0)


def totals(shares):
    n_z = shares.shape[1] // 2
    return pl.pallas_call(
        total_kernel,
        in_specs=[VMEM],
        out_specs=VMEM,
        out_shape=jax.ShapeDtypeStruct((n_z, 4, 128), jnp.float32),
        compiler_params=pltpu.CompilerParams(vmem_limit_bytes=4 * 1024 * 1024),
    )(shares)


def pick_kernel(plan, rows, out):
    for by in range(NSHIFT + 1):
        both = jnp.zeros((4, 128), jnp.float32)
        for z in range(rows.shape[0]):
            both = jnp.where(plan[z] == by, rows[z], both)
        pair = both[:2] + both[2:]
        for side in range(2):
            out[by, :, pl.ds(128 * side, 128)] = pair[side : side + 1]


def pick(plan, rows):
    return pl.pallas_call(
        pick_kernel,
        in_specs=[VMEM, VMEM],
        out_specs=VMEM,
        out_shape=jax.ShapeDtypeStruct((NSHIFT + 1, 1, 256), jnp.float32),
        compiler_params=pltpu.CompilerParams(vmem_limit_bytes=4 * 1024 * 1024),
    )(plan, rows)


def per_device(cond, vale, screen, qtable, gmap):
    n_ka = lax.axis_size("ka")
    n_ga = lax.axis_size("ga")
    n_z = n_ka // 2
    my_ka = lax.axis_index("ka")
    my_ga = lax.axis_index("ga")
    place = jnp.stack([my_ka, my_ga]).astype(jnp.int32)
    swap_core = [(i, i ^ 1) for i in range(n_ga)]
    swap_y = [(i, i ^ n_z) for i in range(n_ka)]
    swap_both = [(k * n_ga + g, (k ^ n_z) * n_ga + (g ^ 1)) for k in range(n_ka) for g in range(n_ga)]
    along_z = [list(range(n_z)), list(range(n_z, n_ka))]
    planes = [
        [(y * n_z + z) * n_ga + g for y in range(2) for g in range(n_ga)] for z in range(n_z)
    ]
    same_core = [plane[core::2] for plane in planes for core in range(2)]

    sent = spread(place, cond, vale, gmap, n_z)
    got = lax.all_to_all(sent, "ka", 0, 0, axis_index_groups=along_z)

    v_sent, c_keep = pack(got, n_ga)
    v_sent, c_keep, slab = lax.optimization_barrier((v_sent, c_keep, screen[0]))
    c_y = lax.ppermute(c_keep, "ka", swap_y)
    c_core = lax.ppermute(c_keep, "ga", swap_core)
    c_diag = lax.ppermute(c_keep, ("ka", "ga"), swap_both)
    slab_mate = lax.ppermute(slab, "ga", swap_core)
    v_all = lax.all_to_all(v_sent, ("ka", "ga"), 0, 0, axis_index_groups=same_core)

    part, plan = tiles(qtable, place, slab, slab_mate, v_all, c_keep, c_y, c_core, c_diag)
    shares = lax.all_to_all(part, ("ka", "ga"), 0, 0, axis_index_groups=planes)
    rows = lax.all_to_all(totals(shares), "ka", 0, 0, axis_index_groups=along_z)
    return jnp.transpose(pick(plan, rows), (1, 0, 2))


def solution(mesh):
    in_specs = (P("ka", None, "ga"), P("ka", None, "ga"), P("ka", "ga", None), P(), P("ka", "ga"))
    out_specs = P("ka", None, "ga")
    return jax.shard_map(
        per_device, mesh=mesh, in_specs=in_specs, out_specs=out_specs, check_vma=False
    )
```

```python
import jax
import jax.numpy as jnp
from jax import lax
from jax.experimental import pallas as pl
from jax.experimental.pallas import tpu as pltpu
from jax.sharding import PartitionSpec as P

NSHIFT = 2
STEP_K = 4
BAND_K = 16
CHUNKS = ((0,), (1,2,3), (4,5,6,7))
VMEM = pl.BlockSpec(memory_space=pltpu.VMEM)
SMEM = pl.BlockSpec(memory_space=pltpu.SMEM)
HBM = pl.BlockSpec(memory_space=pltpu.HBM)
ANY = pl.BlockSpec(memory_space=pl.ANY)


def in_hbm(*arrays):
    return [pltpu.with_memory_space_constraint(array, pltpu.HBM) for array in arrays]


def last_dims(a, b):
    return lax.dot_general(a, b, (((1,), (1,)), ((), ())), preferred_element_type=jnp.float32)


def density(own, far):
    product = own[:, None, :] * far[None, :, :]
    return product.reshape(64, own.shape[-1]).astype(jnp.bfloat16)


def lane_gather(source, places):
    return jnp.take_along_axis(source, places, axis=1, mode="promise_in_bounds")


def mapped(source, places):
    low, high = source[:, :128], source[:, 128:]
    sides = []
    for part in (places[:, :128], places[:, 128:]):
        inner = part & 127
        sides.append(jnp.where(part < 128, lane_gather(low, inner), lane_gather(high, inner)))
    return jnp.concatenate(sides, axis=1)


def entry_lanes(entry, width):
    return pl.ds(entry * width, width)


def map_entries(packed, count, width, store):
    maps = []
    for first in range(0, 2 * count, 8):
        lanes = pl.ds(count * width + 16 * first, 128)
        maps.append(packed[:, lanes].astype(jnp.float32).astype(jnp.int32))
    for entry in range(count):
        sides = []
        for side in range(2):
            row = 2 * entry + side
            places = maps[row // 8][row % 8 : row % 8 + 1]
            sides.append(jnp.broadcast_to(places, (8, 128)))
        source = packed[:, entry_lanes(entry, width)].astype(jnp.float32)
        store(entry, mapped(source, jnp.concatenate(sides, axis=1)))


def tile_kernel(
    table, place, w_own, w_low, w_high, vale, c_keep, c_y, c_core, c_diag, out, plan,
    slabs, far_v, far_c, c_all, pv, pc, image, wide, arrived, joined,
):
    blocks = vale.shape[0] // 2
    width = w_own.shape[0]
    n_z = plan.shape[0]
    my_ka, core = place[0], place[1] % 2
    my_y = my_ka // n_z
    shift = sum(jnp.where(table[by, 0] == my_ka, by, 0) for by in range(1, NSHIFT + 1))
    fetches = [
        pltpu.make_async_copy(
            w_own.at[:, pl.ds(pl.multiple_of((2 * block + core) * width, width), width)],
            slabs.at[0, :, pl.ds(block * width, width)],
            arrived.at[block],
        )
        for block in range(blocks)
    ]
    half = w_low.shape[1]
    fetches += [
        pltpu.make_async_copy(
            source, slabs.at[1, :, pl.ds(number * half, half)], arrived.at[blocks + number]
        )
        for number, source in enumerate((w_low, w_high))
    ]
    fetches += [
        pltpu.make_async_copy(source, c_all.at[side, y], joined.at[side, other])
        for side, pair in enumerate(((c_keep, c_y), (c_core, c_diag)))
        for other, (source, y) in enumerate(zip(pair, (my_y, 1 - my_y)))
    ]
    for fetch in fetches:
        fetch.start()

    upper = lax.broadcasted_iota(jnp.int32, (4, 128), 0) >= 2
    for z in range(n_z):
        tile = jnp.full((4, 128), -1, jnp.int32)
        for by in range(NSHIFT + 1):
            holder = table[by, 0]
            row = jnp.where(upper, holder - n_z, holder)
            tile = jnp.where(row == z, by, tile)
        plan[z] = tile

    def partner(k):
        return jnp.where(k < shift, k - shift + 2 * n_z, k - shift)

    def form(number):
        slot = number % far_v.shape[0]
        for y in range(2):
            for inner, block in enumerate(CHUNKS[number]):

                def store(z, value):
                    far_v[slot, y * n_z + z, :, pl.ds(inner * width, width)] = value

                map_entries(vale.at[y * blocks + block], n_z, width, store)
        for k in range(2 * n_z):
            for inner, block in enumerate(CHUNKS[number]):
                far = far_v[slot, partner(k), :, pl.ds(inner * width, width)]
                own = vale[k // n_z * blocks + block, :, entry_lanes(k % n_z, width)]
                own = own.astype(jnp.float32)
                pv[pl.ds(64 * k, 64), pl.ds(block * width, width)] = density(own, far)

    def form_c():
        for side in range(2):
            lanes = pl.ds(side * width, width)
            for y in range(2):

                def store(z, value):
                    far_c[y * n_z + z, :, lanes] = value

                map_entries(c_all.at[side, y], n_z, width, store)
            for k in range(2 * n_z):
                own = c_all[side, k // n_z, :, entry_lanes(k % n_z, width)].astype(jnp.float32)
                pc[pl.ds(64 * k, 64), lanes] = density(own, far_c[partner(k), :, lanes])

    def term(rows, number, side):
        span = pl.ds(CHUNKS[number][0] * width, len(CHUNKS[number]) * width)
        return last_dims(pv[rows, span], slabs[side, :, span])

    sides = [pl.ds(side * width, width) for side in range(2)]
    last = len(CHUNKS) - 1
    form(0)
    for fetch in fetches:
        fetch.wait()
    for number in range(last):
        form(number + 1)
        if number + 1 == last:
            form_c()
        for side, lanes in enumerate(sides):
            part = term(pl.ds(0, pv.shape[0]), number, side)
            image[:, lanes] = part if number == 0 else image[:, lanes] + part

    low = lax.broadcasted_iota(jnp.int32, (64, 128), 1) < 64
    for first in range(0, 2 * n_z, BAND_K):
        rows = pl.ds(64 * first, 64 * BAND_K)
        bands = [
            (image[rows, lanes] + term(rows, last, side)).astype(jnp.bfloat16)
            for side, lanes in enumerate(sides)
        ]
        for step in range(0, BAND_K, STEP_K):
            full = None
            for lanes, band in zip(sides, bands):
                band = band[64 * step : 64 * (step + STEP_K)]
                part = last_dims(pc[pl.ds(64 * (first + step), 64 * STEP_K), lanes], band)
                full = part if full is None else full + part
            for pair in range(STEP_K // 2):
                base = 128 * pair
                strip = full[:, base : base + 128]
                tile = jnp.where(low, strip[base : base + 64], strip[base + 64 : base + 128])
                k = first + step + 2 * pair
                dests = pl.ds(16 * (k // n_z), 16)
                wide[dests, pl.ds(2 * (k % n_z), 4), :] = tile.reshape(16, 4, 128)
    out[...] = wide[...].astype(jnp.bfloat16)


def tiles(table, place, w_own, w_low, w_high, vale, c_keep, c_y, c_core, c_diag):
    sources = vale.shape[0]
    width = w_own.shape[0]
    n_z = table.shape[0] // 2
    rows = 2 * n_z * 64
    blocks = sources // 2
    wide = max(len(chunk) for chunk in CHUNKS) * width
    return pl.pallas_call(
        tile_kernel,
        in_specs=[SMEM, SMEM, HBM, ANY, ANY, VMEM] + [ANY] * 4,
        out_specs=[VMEM, VMEM],
        out_shape=[
            jax.ShapeDtypeStruct((2 * sources, 2 * n_z, 128), jnp.bfloat16),
            jax.ShapeDtypeStruct((n_z, 4, 128), jnp.int32),
        ],
        scratch_shapes=[
            pltpu.VMEM((2, width, blocks * width), jnp.bfloat16),
            pltpu.VMEM((2, 2 * n_z, 8, wide), jnp.float32),
            pltpu.VMEM((2 * n_z, 8, 2 * width), jnp.float32),
            pltpu.VMEM((2, 2) + c_keep.shape, jnp.bfloat16),
            pltpu.VMEM((rows, blocks * width), jnp.bfloat16),
            pltpu.VMEM((rows, 2 * width), jnp.bfloat16),
            pltpu.VMEM((rows, 2 * width), jnp.float32),
            pltpu.VMEM((2 * sources, 2 * n_z, 128), jnp.float32),
            pltpu.SemaphoreType.DMA((blocks + 2,)),
            pltpu.SemaphoreType.DMA((2, 2)),
        ],
        compiler_params=pltpu.CompilerParams(vmem_limit_bytes=28 * 1024 * 1024),
    )(table, place, *in_hbm(w_own), w_low, w_high, vale, c_keep, c_y, c_core, c_diag)


def spread_kernel(place, cond_in, vale_in, gmap_in, out, cond, vale, gmap, arrived):
    width = cond.shape[2]
    fetches = [
        pltpu.make_async_copy(source, target, arrived.at[number])
        for number, (source, target) in enumerate(((cond_in, cond), (vale_in, vale), (gmap_in, gmap)))
    ]
    for fetch in fetches:
        fetch.start()
    for fetch in fetches:
        fetch.wait()
    places = (gmap[...] - place[1] * width).astype(jnp.float32)
    top = lax.broadcasted_iota(jnp.int32, (8, 128), 0) == 0
    places = jnp.where(top, places[:, :128], places[:, 128:]).astype(jnp.bfloat16)
    for dest in range(out.shape[0]):
        out[dest, :, :width] = vale[0]
        out[dest, :, width : 2 * width] = cond[0]
        out[dest, :, 2 * width :] = places


def spread(place, cond, vale, gmap, dests):
    return pl.pallas_call(
        spread_kernel,
        in_specs=[SMEM] + [HBM] * 3,
        out_specs=VMEM,
        out_shape=jax.ShapeDtypeStruct((dests, 8, 2 * cond.shape[2] + 128), jnp.bfloat16),
        scratch_shapes=[
            pltpu.VMEM(cond.shape, jnp.bfloat16),
            pltpu.VMEM(vale.shape, jnp.bfloat16),
            pltpu.VMEM(gmap.shape, jnp.int32),
            pltpu.SemaphoreType.DMA((3,)),
        ],
        compiler_params=pltpu.CompilerParams(vmem_limit_bytes=4 * 1024 * 1024),
    )(place, *in_hbm(cond, vale, gmap))


def pack_kernel(place, got, slab, v_out, c_out, w_low, w_high, block, sent, cut):
    n_z = got.shape[0]
    width = (got.shape[2] - 128) // 2
    mate = 1 - place[1] % 2
    half = w_low.shape[1] // width
    slices = []
    for number in range(2 * half):
        lanes = pl.ds(pl.multiple_of((2 * number + mate) * width, width), width)
        target = (w_low, w_high)[number // half]
        slices.append(
            pltpu.make_async_copy(
                slab.at[:, lanes],
                target.at[:, pl.ds(number % half * width, width)],
                cut.at[number],
            )
        )
    for copy in slices:
        copy.start()
    row_id = lax.broadcasted_iota(jnp.int32, (8, 128), 0)
    maps = []
    for first in range(0, n_z, 4):
        tile = jnp.zeros((8, 128), jnp.float32)
        for z in range(first, first + 4):
            pair = got[z, :, 2 * width :].astype(jnp.float32)
            tile = jnp.where(row_id == 2 * (z - first), pair[0:1], tile)
            tile = jnp.where(row_id == 2 * (z - first) + 1, pair[1:2], tile)
        maps.append(tile.astype(jnp.bfloat16))

    def fill(target, column):
        for z in range(n_z):
            target[:, entry_lanes(z, width)] = got[z, :, pl.ds(column * width, width)]
        for number, tile in enumerate(maps):
            target[:, pl.ds(n_z * width + 128 * number, 128)] = tile

    fill(block, 0)
    copies = [
        pltpu.make_async_copy(block, v_out.at[dest], sent.at[dest])
        for dest in range(v_out.shape[0])
    ]
    for copy in copies:
        copy.start()
    fill(c_out, 1)
    for copy in copies + slices:
        copy.wait()


def pack(place, got, slab, dests):
    n_z = got.shape[0]
    width, grid_h = slab.shape
    shape = (8, n_z * width + 128 * (n_z // 4))
    quarter = (width, grid_h // 4)
    return pl.pallas_call(
        pack_kernel,
        in_specs=[SMEM, VMEM, HBM],
        out_specs=[HBM, VMEM, HBM, HBM],
        out_shape=[
            pltpu.HBM((dests,) + shape, jnp.bfloat16),
            jax.ShapeDtypeStruct(shape, jnp.bfloat16),
            pltpu.HBM(quarter, jnp.bfloat16),
            pltpu.HBM(quarter, jnp.bfloat16),
        ],
        scratch_shapes=[
            pltpu.VMEM(shape, jnp.bfloat16),
            pltpu.SemaphoreType.DMA((dests,)),
            pltpu.SemaphoreType.DMA((dests // 2,)),
        ],
        compiler_params=pltpu.CompilerParams(vmem_limit_bytes=8 * 1024 * 1024),
    )(place, got, *in_hbm(slab))


def total_kernel(shares, out):
    sources, rows, _ = shares.shape
    low = lax.broadcasted_iota(jnp.int32, (1, 128), 1) < 64
    sums = []
    for y in range(2):
        first = y * (sources // 2)
        total = shares[first].astype(jnp.float32)
        for source in range(first + 1, first + sources // 2):
            total = total + shares[source].astype(jnp.float32)
        sums.append((total, pltpu.roll(total, 64, 1)))
    for z in range(rows // 2):
        lines = []
        for strip, turned in sums:
            left, right = (turned, strip) if z % 2 else (strip, turned)
            for row in (4 * (z // 2), 4 * (z // 2) + 2):
                lines.append(jnp.where(low, left[row : row + 1], right[row + 1 : row + 2]))
        out[z] = jnp.concatenate(lines, axis=0)


def totals(shares):
    n_z = shares.shape[1] // 2
    return pl.pallas_call(
        total_kernel,
        in_specs=[VMEM],
        out_specs=VMEM,
        out_shape=jax.ShapeDtypeStruct((n_z, 4, 128), jnp.float32),
        compiler_params=pltpu.CompilerParams(vmem_limit_bytes=4 * 1024 * 1024),
    )(shares)


def pick_kernel(plan, rows, out):
    for by in range(NSHIFT + 1):
        both = jnp.zeros((4, 128), jnp.float32)
        for z in range(rows.shape[0]):
            both = jnp.where(plan[z] == by, rows[z], both)
        pair = both[:2] + both[2:]
        for side in range(2):
            out[by, :, pl.ds(128 * side, 128)] = pair[side : side + 1]


def pick(plan, rows):
    return pl.pallas_call(
        pick_kernel,
        in_specs=[VMEM, VMEM],
        out_specs=VMEM,
        out_shape=jax.ShapeDtypeStruct((NSHIFT + 1, 1, 256), jnp.float32),
        compiler_params=pltpu.CompilerParams(vmem_limit_bytes=4 * 1024 * 1024),
    )(plan, rows)


def per_device(cond, vale, screen, qtable, gmap):
    n_ka = lax.axis_size("ka")
    n_ga = lax.axis_size("ga")
    n_z = n_ka // 2
    my_ka = lax.axis_index("ka")
    my_ga = lax.axis_index("ga")
    place = jnp.stack([my_ka, my_ga]).astype(jnp.int32)
    swap_core = [(i, i ^ 1) for i in range(n_ga)]
    swap_y = [(i, i ^ n_z) for i in range(n_ka)]
    swap_both = [(k * n_ga + g, (k ^ n_z) * n_ga + (g ^ 1)) for k in range(n_ka) for g in range(n_ga)]
    along_z = [list(range(n_z)), list(range(n_z, n_ka))]
    planes = [
        [(y * n_z + z) * n_ga + g for y in range(2) for g in range(n_ga)] for z in range(n_z)
    ]
    same_core = [plane[core::2] for plane in planes for core in range(2)]

    sent = spread(place, cond, vale, gmap, n_z)
    got = lax.all_to_all(sent, "ka", 0, 0, axis_index_groups=along_z)

    slab = screen[0]
    v_sent, c_keep, w_low, w_high = pack(place, got, slab, n_ga)
    c_y = lax.ppermute(c_keep, "ka", swap_y)
    c_core = lax.ppermute(c_keep, "ga", swap_core)
    c_diag = lax.ppermute(c_keep, ("ka", "ga"), swap_both)
    w_low = lax.ppermute(w_low, "ga", swap_core)
    w_high = lax.ppermute(w_high, "ga", swap_core)
    v_all = lax.all_to_all(v_sent, ("ka", "ga"), 0, 0, axis_index_groups=same_core)

    part, plan = tiles(qtable, place, slab, w_low, w_high, v_all, c_keep, c_y, c_core, c_diag)
    shares = lax.all_to_all(part, ("ka", "ga"), 0, 0, axis_index_groups=planes)
    rows = lax.all_to_all(totals(shares), "ka", 0, 0, axis_index_groups=along_z)
    return jnp.transpose(pick(plan, rows), (1, 0, 2))


def solution(mesh):
    in_specs = (P("ka", None, "ga"), P("ka", None, "ga"), P("ka", "ga", None), P(), P("ka", "ga"))
    out_specs = P("ka", None, "ga")
    return jax.shard_map(
        per_device, mesh=mesh, in_specs=in_specs, out_specs=out_specs, check_vma=False
    )
```

```python
import jax
import jax.numpy as jnp
from jax import lax
from jax.experimental import pallas as pl
from jax.experimental.pallas import tpu as pltpu
from jax.sharding import PartitionSpec as P

NSHIFT = 2
STEP_K = 4
BAND_K = 16
CHUNKS = ((0,), (1,2,3), (4,5,6,7))
VMEM = pl.BlockSpec(memory_space=pltpu.VMEM)
SMEM = pl.BlockSpec(memory_space=pltpu.SMEM)
HBM = pl.BlockSpec(memory_space=pltpu.HBM)
ANY = pl.BlockSpec(memory_space=pl.ANY)


def in_hbm(*arrays):
    return [pltpu.with_memory_space_constraint(array, pltpu.HBM) for array in arrays]


def last_dims(a, b):
    return lax.dot_general(a, b, (((1,), (1,)), ((), ())), preferred_element_type=jnp.float32)


def density(own, far):
    product = own[:, None, :] * far[None, :, :]
    return product.reshape(64, own.shape[-1]).astype(jnp.bfloat16)


def lane_gather(source, places):
    return jnp.take_along_axis(source, places, axis=1, mode="promise_in_bounds")


def mapped(source, places):
    low, high = source[:, :128], source[:, 128:]
    sides = []
    for part in (places[:, :128], places[:, 128:]):
        inner = part & 127
        sides.append(jnp.where(part < 128, lane_gather(low, inner), lane_gather(high, inner)))
    return jnp.concatenate(sides, axis=1)


def entry_lanes(entry, width):
    return pl.ds(entry * width, width)


def map_entries(packed, count, width, store):
    maps = []
    for first in range(0, 2 * count, 8):
        lanes = pl.ds(count * width + 16 * first, 128)
        maps.append(packed[:, lanes].astype(jnp.float32).astype(jnp.int32))
    for entry in range(count):
        sides = []
        for side in range(2):
            row = 2 * entry + side
            places = maps[row // 8][row % 8 : row % 8 + 1]
            sides.append(jnp.broadcast_to(places, (8, 128)))
        source = packed[:, entry_lanes(entry, width)].astype(jnp.float32)
        store(entry, mapped(source, jnp.concatenate(sides, axis=1)))


def tile_kernel(
    table, place, w_own, w_low, w_high, vale, c_keep, c_y, c_core, c_diag, out, plan,
    slabs, far_v, far_c, c_all, pv, pc, image, wide, arrived, joined,
):
    blocks = vale.shape[0] // 2
    width = w_own.shape[0]
    n_z = plan.shape[0]
    my_ka, core = place[0], place[1] % 2
    my_y = my_ka // n_z
    shift = sum(jnp.where(table[by, 0] == my_ka, by, 0) for by in range(1, NSHIFT + 1))
    fetches = [
        pltpu.make_async_copy(
            w_own.at[:, pl.ds(pl.multiple_of((2 * block + core) * width, width), width)],
            slabs.at[0, :, pl.ds(block * width, width)],
            arrived.at[block],
        )
        for block in range(blocks)
    ]
    half = w_low.shape[1]
    fetches += [
        pltpu.make_async_copy(
            source, slabs.at[1, :, pl.ds(number * half, half)], arrived.at[blocks + number]
        )
        for number, source in enumerate((w_low, w_high))
    ]
    fetches += [
        pltpu.make_async_copy(source, c_all.at[side, y], joined.at[side, other])
        for side, pair in enumerate(((c_keep, c_y), (c_core, c_diag)))
        for other, (source, y) in enumerate(zip(pair, (my_y, 1 - my_y)))
    ]
    for fetch in fetches:
        fetch.start()

    upper = lax.broadcasted_iota(jnp.int32, (4, 128), 0) >= 2
    for z in range(n_z):
        tile = jnp.full((4, 128), -1, jnp.int32)
        for by in range(NSHIFT + 1):
            holder = table[by, 0]
            row = jnp.where(upper, holder - n_z, holder)
            tile = jnp.where(row == z, by, tile)
        plan[z] = tile

    def partner(k):
        return jnp.where(k < shift, k - shift + 2 * n_z, k - shift)

    def form(number):
        slot = number % far_v.shape[0]
        for y in range(2):
            for inner, block in enumerate(CHUNKS[number]):

                def store(z, value):
                    far_v[slot, y * n_z + z, :, pl.ds(inner * width, width)] = value

                map_entries(vale.at[y * blocks + block], n_z, width, store)
        for k in range(2 * n_z):
            for inner, block in enumerate(CHUNKS[number]):
                far = far_v[slot, partner(k), :, pl.ds(inner * width, width)]
                own = vale[k // n_z * blocks + block, :, entry_lanes(k % n_z, width)]
                own = own.astype(jnp.float32)
                pv[pl.ds(64 * k, 64), pl.ds(block * width, width)] = density(own, far)

    def form_c():
        for side in range(2):
            lanes = pl.ds(side * width, width)
            for y in range(2):

                def store(z, value):
                    far_c[y * n_z + z, :, lanes] = value

                map_entries(c_all.at[side, y], n_z, width, store)
            for k in range(2 * n_z):
                own = c_all[side, k // n_z, :, entry_lanes(k % n_z, width)].astype(jnp.float32)
                pc[pl.ds(64 * k, 64), lanes] = density(own, far_c[partner(k), :, lanes])

    def term(rows, number, side):
        span = pl.ds(CHUNKS[number][0] * width, len(CHUNKS[number]) * width)
        return last_dims(pv[rows, span], slabs[side, :, span])

    sides = [pl.ds(side * width, width) for side in range(2)]
    last = len(CHUNKS) - 1
    form(0)
    for fetch in fetches:
        fetch.wait()
    for number in range(last):
        form(number + 1)
        if number + 1 == last:
            form_c()
        for side, lanes in enumerate(sides):
            part = term(pl.ds(0, pv.shape[0]), number, side)
            image[:, lanes] = part if number == 0 else image[:, lanes] + part

    low = lax.broadcasted_iota(jnp.int32, (64, 128), 1) < 64
    for first in range(0, 2 * n_z, BAND_K):
        rows = pl.ds(64 * first, 64 * BAND_K)
        bands = [
            (image[rows, lanes] + term(rows, last, side)).astype(jnp.bfloat16)
            for side, lanes in enumerate(sides)
        ]
        for step in range(0, BAND_K, STEP_K):
            full = None
            for lanes, band in zip(sides, bands):
                band = band[64 * step : 64 * (step + STEP_K)]
                part = last_dims(pc[pl.ds(64 * (first + step), 64 * STEP_K), lanes], band)
                full = part if full is None else full + part
            for pair in range(STEP_K // 2):
                base = 128 * pair
                strip = full[:, base : base + 128]
                tile = jnp.where(low, strip[base : base + 64], strip[base + 64 : base + 128])
                k = first + step + 2 * pair
                dests = pl.ds(16 * (k // n_z), 16)
                wide[dests, pl.ds(2 * (k % n_z), 4), :] = tile.reshape(16, 4, 128)
    out[...] = wide[...].astype(jnp.bfloat16)


def tiles(table, place, w_own, w_low, w_high, vale, c_keep, c_y, c_core, c_diag):
    sources = vale.shape[0]
    width = w_own.shape[0]
    n_z = table.shape[0] // 2
    rows = 2 * n_z * 64
    blocks = sources // 2
    wide = max(len(chunk) for chunk in CHUNKS) * width
    return pl.pallas_call(
        tile_kernel,
        in_specs=[SMEM, SMEM, HBM, ANY, ANY, VMEM] + [ANY] * 4,
        out_specs=[VMEM, VMEM],
        out_shape=[
            jax.ShapeDtypeStruct((2 * sources, 2 * n_z, 128), jnp.bfloat16),
            jax.ShapeDtypeStruct((n_z, 4, 128), jnp.int32),
        ],
        scratch_shapes=[
            pltpu.VMEM((2, width, blocks * width), jnp.bfloat16),
            pltpu.VMEM((2, 2 * n_z, 8, wide), jnp.float32),
            pltpu.VMEM((2 * n_z, 8, 2 * width), jnp.float32),
            pltpu.VMEM((2, 2) + c_keep.shape, jnp.bfloat16),
            pltpu.VMEM((rows, blocks * width), jnp.bfloat16),
            pltpu.VMEM((rows, 2 * width), jnp.bfloat16),
            pltpu.VMEM((rows, 2 * width), jnp.float32),
            pltpu.VMEM((2 * sources, 2 * n_z, 128), jnp.float32),
            pltpu.SemaphoreType.DMA((blocks + 2,)),
            pltpu.SemaphoreType.DMA((2, 2)),
        ],
        compiler_params=pltpu.CompilerParams(vmem_limit_bytes=28 * 1024 * 1024),
    )(table, place, *in_hbm(w_own), w_low, w_high, vale, c_keep, c_y, c_core, c_diag)


def spread_kernel(place, cond_in, vale_in, gmap_in, out, cond, vale, gmap, arrived):
    width = cond.shape[2]
    fetches = [
        pltpu.make_async_copy(source, target, arrived.at[number])
        for number, (source, target) in enumerate(((cond_in, cond), (vale_in, vale), (gmap_in, gmap)))
    ]
    for fetch in fetches:
        fetch.start()
    for fetch in fetches:
        fetch.wait()
    places = (gmap[...] - place[1] * width).astype(jnp.float32)
    top = lax.broadcasted_iota(jnp.int32, (8, 128), 0) == 0
    places = jnp.where(top, places[:, :128], places[:, 128:]).astype(jnp.bfloat16)
    for dest in range(out.shape[0]):
        out[dest, :, :width] = vale[0]
        out[dest, :, width : 2 * width] = cond[0]
        out[dest, :, 2 * width :] = places


def spread(place, cond, vale, gmap, dests):
    return pl.pallas_call(
        spread_kernel,
        in_specs=[SMEM] + [HBM] * 3,
        out_specs=VMEM,
        out_shape=jax.ShapeDtypeStruct((dests, 8, 2 * cond.shape[2] + 128), jnp.bfloat16),
        scratch_shapes=[
            pltpu.VMEM(cond.shape, jnp.bfloat16),
            pltpu.VMEM(vale.shape, jnp.bfloat16),
            pltpu.VMEM(gmap.shape, jnp.int32),
            pltpu.SemaphoreType.DMA((3,)),
        ],
        compiler_params=pltpu.CompilerParams(vmem_limit_bytes=4 * 1024 * 1024),
    )(place, *in_hbm(cond, vale, gmap))


def pack_kernel(got, v_out, c_out, block, sent):
    n_z = got.shape[0]
    width = (got.shape[2] - 128) // 2
    row_id = lax.broadcasted_iota(jnp.int32, (8, 128), 0)
    maps = []
    for first in range(0, n_z, 4):
        tile = jnp.zeros((8, 128), jnp.float32)
        for z in range(first, first + 4):
            pair = got[z, :, 2 * width :].astype(jnp.float32)
            tile = jnp.where(row_id == 2 * (z - first), pair[0:1], tile)
            tile = jnp.where(row_id == 2 * (z - first) + 1, pair[1:2], tile)
        maps.append(tile.astype(jnp.bfloat16))

    def fill(target, column):
        for z in range(n_z):
            target[:, entry_lanes(z, width)] = got[z, :, pl.ds(column * width, width)]
        for number, tile in enumerate(maps):
            target[:, pl.ds(n_z * width + 128 * number, 128)] = tile

    fill(block, 0)
    copies = [
        pltpu.make_async_copy(block, v_out.at[dest], sent.at[dest])
        for dest in range(v_out.shape[0])
    ]
    for copy in copies:
        copy.start()
    fill(c_out, 1)
    for copy in copies:
        copy.wait()


def pack(got, dests):
    n_z = got.shape[0]
    width = (got.shape[2] - 128) // 2
    shape = (8, n_z * width + 128 * (n_z // 4))
    return pl.pallas_call(
        pack_kernel,
        in_specs=[VMEM],
        out_specs=[HBM, VMEM],
        out_shape=[
            pltpu.HBM((dests,) + shape, jnp.bfloat16),
            jax.ShapeDtypeStruct(shape, jnp.bfloat16),
        ],
        scratch_shapes=[
            pltpu.VMEM(shape, jnp.bfloat16),
            pltpu.SemaphoreType.DMA((dests,)),
        ],
        compiler_params=pltpu.CompilerParams(vmem_limit_bytes=8 * 1024 * 1024),
    )(got)


def total_kernel(shares, out):
    sources, rows, _ = shares.shape
    low = lax.broadcasted_iota(jnp.int32, (1, 128), 1) < 64
    sums = []
    for y in range(2):
        first = y * (sources // 2)
        total = shares[first].astype(jnp.float32)
        for source in range(first + 1, first + sources // 2):
            total = total + shares[source].astype(jnp.float32)
        sums.append((total, pltpu.roll(total, 64, 1)))
    for z in range(rows // 2):
        lines = []
        for strip, turned in sums:
            left, right = (turned, strip) if z % 2 else (strip, turned)
            for row in (4 * (z // 2), 4 * (z // 2) + 2):
                lines.append(jnp.where(low, left[row : row + 1], right[row + 1 : row + 2]))
        out[z] = jnp.concatenate(lines, axis=0)


def totals(shares):
    n_z = shares.shape[1] // 2
    return pl.pallas_call(
        total_kernel,
        in_specs=[VMEM],
        out_specs=VMEM,
        out_shape=jax.ShapeDtypeStruct((n_z, 4, 128), jnp.float32),
        compiler_params=pltpu.CompilerParams(vmem_limit_bytes=4 * 1024 * 1024),
    )(shares)


def pick_kernel(plan, rows, out):
    for by in range(NSHIFT + 1):
        both = jnp.zeros((4, 128), jnp.float32)
        for z in range(rows.shape[0]):
            both = jnp.where(plan[z] == by, rows[z], both)
        pair = both[:2] + both[2:]
        for side in range(2):
            out[by, :, pl.ds(128 * side, 128)] = pair[side : side + 1]


def pick(plan, rows):
    return pl.pallas_call(
        pick_kernel,
        in_specs=[VMEM, VMEM],
        out_specs=VMEM,
        out_shape=jax.ShapeDtypeStruct((NSHIFT + 1, 1, 256), jnp.float32),
        compiler_params=pltpu.CompilerParams(vmem_limit_bytes=4 * 1024 * 1024),
    )(plan, rows)


def per_device(cond, vale, screen, qtable, gmap):
    n_ka = lax.axis_size("ka")
    n_ga = lax.axis_size("ga")
    n_z = n_ka // 2
    my_ka = lax.axis_index("ka")
    my_ga = lax.axis_index("ga")
    place = jnp.stack([my_ka, my_ga]).astype(jnp.int32)
    swap_core = [(i, i ^ 1) for i in range(n_ga)]
    swap_y = [(i, i ^ n_z) for i in range(n_ka)]
    swap_both = [(k * n_ga + g, (k ^ n_z) * n_ga + (g ^ 1)) for k in range(n_ka) for g in range(n_ga)]
    along_z = [list(range(n_z)), list(range(n_z, n_ka))]
    planes = [
        [(y * n_z + z) * n_ga + g for y in range(2) for g in range(n_ga)] for z in range(n_z)
    ]
    same_core = [plane[core::2] for plane in planes for core in range(2)]

    sent = spread(place, cond, vale, gmap, n_z)
    got = lax.all_to_all(sent, "ka", 0, 0, axis_index_groups=along_z)

    slab = screen[0]
    v_sent, c_keep = pack(got, n_ga)
    width, grid_h = slab.shape
    by_core = slab.reshape(width, 2, grid_h // (4 * width), 2, width)
    other = 1 - my_ga % 2
    w_low, w_high = (
        lax.dynamic_index_in_dim(by_core[:, part], other, 2, keepdims=False).reshape(width, -1)
        for part in range(2)
    )
    c_y = lax.ppermute(c_keep, "ka", swap_y)
    c_core = lax.ppermute(c_keep, "ga", swap_core)
    c_diag = lax.ppermute(c_keep, ("ka", "ga"), swap_both)
    w_low = lax.ppermute(w_low, "ga", swap_core)
    w_high = lax.ppermute(w_high, "ga", swap_core)
    v_all = lax.all_to_all(v_sent, ("ka", "ga"), 0, 0, axis_index_groups=same_core)

    part, plan = tiles(qtable, place, slab, w_low, w_high, v_all, c_keep, c_y, c_core, c_diag)
    shares = lax.all_to_all(part, ("ka", "ga"), 0, 0, axis_index_groups=planes)
    rows = lax.all_to_all(totals(shares), "ka", 0, 0, axis_index_groups=along_z)
    return jnp.transpose(pick(plan, rows), (1, 0, 2))


def solution(mesh):
    in_specs = (P("ka", None, "ga"), P("ka", None, "ga"), P("ka", "ga", None), P(), P("ka", "ga"))
    out_specs = P("ka", None, "ga")
    return jax.shard_map(
        per_device, mesh=mesh, in_specs=in_specs, out_specs=out_specs, check_vma=False
    )
```

```python
import jax
import jax.numpy as jnp
from jax import lax
from jax.experimental import pallas as pl
from jax.experimental.pallas import tpu as pltpu
from jax.sharding import PartitionSpec as P

NSHIFT = 2
STEP_K = 4
BAND_K = 16
CHUNKS = ((0,), (1,2,3), (4,5,6,7))
VMEM = pl.BlockSpec(memory_space=pltpu.VMEM)
SMEM = pl.BlockSpec(memory_space=pltpu.SMEM)
HBM = pl.BlockSpec(memory_space=pltpu.HBM)
ANY = pl.BlockSpec(memory_space=pl.ANY)


def in_hbm(*arrays):
    return [pltpu.with_memory_space_constraint(array, pltpu.HBM) for array in arrays]


def last_dims(a, b):
    return lax.dot_general(a, b, (((1,), (1,)), ((), ())), preferred_element_type=jnp.float32)


def density(own, far):
    product = own[:, None, :] * far[None, :, :]
    return product.reshape(64, own.shape[-1]).astype(jnp.bfloat16)


def lane_gather(source, places):
    return jnp.take_along_axis(source, places, axis=1, mode="promise_in_bounds")


def mapped(source, places):
    low, high = source[:, :128], source[:, 128:]
    sides = []
    for part in (places[:, :128], places[:, 128:]):
        inner = part & 127
        sides.append(jnp.where(part < 128, lane_gather(low, inner), lane_gather(high, inner)))
    return jnp.concatenate(sides, axis=1)


def entry_lanes(entry, width):
    return pl.ds(entry * width, width)


def map_entries(packed, count, width, store):
    maps = []
    for first in range(0, 2 * count, 8):
        lanes = pl.ds(count * width + 16 * first, 128)
        maps.append(packed[:, lanes].astype(jnp.float32).astype(jnp.int32))
    for entry in range(count):
        sides = []
        for side in range(2):
            row = 2 * entry + side
            places = maps[row // 8][row % 8 : row % 8 + 1]
            sides.append(jnp.broadcast_to(places, (8, 128)))
        source = packed[:, entry_lanes(entry, width)].astype(jnp.float32)
        store(entry, mapped(source, jnp.concatenate(sides, axis=1)))


def tile_kernel(
    table, place, w_own, w_low, w_high, vale, c_keep, c_y, c_core, c_diag, out, plan,
    slabs, far_v, far_c, c_all, pv, pc, image, wide, arrived, joined,
):
    blocks = vale.shape[0] // 2
    width = w_own.shape[0]
    n_z = plan.shape[0]
    my_ka, core = place[0], place[1] % 2
    my_y = my_ka // n_z
    shift = sum(jnp.where(table[by, 0] == my_ka, by, 0) for by in range(1, NSHIFT + 1))
    fetches = [
        pltpu.make_async_copy(
            w_own.at[:, pl.ds(pl.multiple_of((2 * block + core) * width, width), width)],
            slabs.at[0, :, pl.ds(block * width, width)],
            arrived.at[block],
        )
        for block in range(blocks)
    ]
    half = w_low.shape[1]
    fetches += [
        pltpu.make_async_copy(
            source, slabs.at[1, :, pl.ds(number * half, half)], arrived.at[blocks + number]
        )
        for number, source in enumerate((w_low, w_high))
    ]
    fetches += [
        pltpu.make_async_copy(source, c_all.at[side, y], joined.at[side, other])
        for side, pair in enumerate(((c_keep, c_y), (c_core, c_diag)))
        for other, (source, y) in enumerate(zip(pair, (my_y, 1 - my_y)))
    ]
    for fetch in fetches:
        fetch.start()

    upper = lax.broadcasted_iota(jnp.int32, (4, 128), 0) >= 2
    for z in range(n_z):
        tile = jnp.full((4, 128), -1, jnp.int32)
        for by in range(NSHIFT + 1):
            holder = table[by, 0]
            row = jnp.where(upper, holder - n_z, holder)
            tile = jnp.where(row == z, by, tile)
        plan[z] = tile

    def partner(k):
        return jnp.where(k < shift, k - shift + 2 * n_z, k - shift)

    def form(number):
        slot = number % far_v.shape[0]
        for y in range(2):
            for inner, block in enumerate(CHUNKS[number]):

                def store(z, value):
                    far_v[slot, y * n_z + z, :, pl.ds(inner * width, width)] = value

                map_entries(vale.at[y * blocks + block], n_z, width, store)
        for k in range(2 * n_z):
            for inner, block in enumerate(CHUNKS[number]):
                far = far_v[slot, partner(k), :, pl.ds(inner * width, width)]
                own = vale[k // n_z * blocks + block, :, entry_lanes(k % n_z, width)]
                own = own.astype(jnp.float32)
                pv[pl.ds(64 * k, 64), pl.ds(block * width, width)] = density(own, far)

    def form_c():
        for side in range(2):
            lanes = pl.ds(side * width, width)
            for y in range(2):

                def store(z, value):
                    far_c[y * n_z + z, :, lanes] = value

                map_entries(c_all.at[side, y], n_z, width, store)
            for k in range(2 * n_z):
                own = c_all[side, k // n_z, :, entry_lanes(k % n_z, width)].astype(jnp.float32)
                pc[pl.ds(64 * k, 64), lanes] = density(own, far_c[partner(k), :, lanes])

    def term(rows, number, side):
        span = pl.ds(CHUNKS[number][0] * width, len(CHUNKS[number]) * width)
        return last_dims(pv[rows, span], slabs[side, :, span])

    sides = [pl.ds(side * width, width) for side in range(2)]
    last = len(CHUNKS) - 1
    form(0)
    for fetch in fetches:
        fetch.wait()
    for number in range(last):
        form(number + 1)
        if number + 1 == last:
            form_c()
        for side, lanes in enumerate(sides):
            part = term(pl.ds(0, pv.shape[0]), number, side)
            image[:, lanes] = part if number == 0 else image[:, lanes] + part

    low = lax.broadcasted_iota(jnp.int32, (64, 128), 1) < 64
    for first in range(0, 2 * n_z, BAND_K):
        rows = pl.ds(64 * first, 64 * BAND_K)
        bands = [
            (image[rows, lanes] + term(rows, last, side)).astype(jnp.bfloat16)
            for side, lanes in enumerate(sides)
        ]
        for step in range(0, BAND_K, STEP_K):
            full = None
            for lanes, band in zip(sides, bands):
                band = band[64 * step : 64 * (step + STEP_K)]
                part = last_dims(pc[pl.ds(64 * (first + step), 64 * STEP_K), lanes], band)
                full = part if full is None else full + part
            for pair in range(STEP_K // 2):
                base = 128 * pair
                strip = full[:, base : base + 128]
                tile = jnp.where(low, strip[base : base + 64], strip[base + 64 : base + 128])
                k = first + step + 2 * pair
                dests = pl.ds(16 * (k // n_z), 16)
                wide[dests, pl.ds(2 * (k % n_z), 4), :] = tile.reshape(16, 4, 128)
    out[...] = wide[...].astype(jnp.bfloat16)


def tiles(table, place, w_own, w_low, w_high, vale, c_keep, c_y, c_core, c_diag):
    sources = vale.shape[0]
    width = w_own.shape[0]
    n_z = table.shape[0] // 2
    rows = 2 * n_z * 64
    blocks = sources // 2
    wide = max(len(chunk) for chunk in CHUNKS) * width
    return pl.pallas_call(
        tile_kernel,
        in_specs=[SMEM, SMEM, HBM, ANY, ANY, VMEM] + [ANY] * 4,
        out_specs=[VMEM, VMEM],
        out_shape=[
            jax.ShapeDtypeStruct((2 * sources, 2 * n_z, 128), jnp.bfloat16),
            jax.ShapeDtypeStruct((n_z, 4, 128), jnp.int32),
        ],
        scratch_shapes=[
            pltpu.VMEM((2, width, blocks * width), jnp.bfloat16),
            pltpu.VMEM((2, 2 * n_z, 8, wide), jnp.float32),
            pltpu.VMEM((2 * n_z, 8, 2 * width), jnp.float32),
            pltpu.VMEM((2, 2) + c_keep.shape, jnp.bfloat16),
            pltpu.VMEM((rows, blocks * width), jnp.bfloat16),
            pltpu.VMEM((rows, 2 * width), jnp.bfloat16),
            pltpu.VMEM((rows, 2 * width), jnp.float32),
            pltpu.VMEM((2 * sources, 2 * n_z, 128), jnp.float32),
            pltpu.SemaphoreType.DMA((blocks + 2,)),
            pltpu.SemaphoreType.DMA((2, 2)),
        ],
        compiler_params=pltpu.CompilerParams(vmem_limit_bytes=28 * 1024 * 1024),
    )(table, place, *in_hbm(w_own), w_low, w_high, vale, c_keep, c_y, c_core, c_diag)


def spread_kernel(place, cond_in, vale_in, gmap_in, out, cond, vale, gmap, arrived):
    width = cond.shape[2]
    fetches = [
        pltpu.make_async_copy(source, target, arrived.at[number])
        for number, (source, target) in enumerate(((cond_in, cond), (vale_in, vale), (gmap_in, gmap)))
    ]
    for fetch in fetches:
        fetch.start()
    for fetch in fetches:
        fetch.wait()
    places = (gmap[...] - place[1] * width).astype(jnp.float32)
    top = lax.broadcasted_iota(jnp.int32, (8, 128), 0) == 0
    places = jnp.where(top, places[:, :128], places[:, 128:]).astype(jnp.bfloat16)
    for dest in range(out.shape[0]):
        out[dest, :, :width] = vale[0]
        out[dest, :, width : 2 * width] = cond[0]
        out[dest, :, 2 * width :] = places


def spread(place, cond, vale, gmap, dests):
    return pl.pallas_call(
        spread_kernel,
        in_specs=[SMEM] + [HBM] * 3,
        out_specs=VMEM,
        out_shape=jax.ShapeDtypeStruct((dests, 8, 2 * cond.shape[2] + 128), jnp.bfloat16),
        scratch_shapes=[
            pltpu.VMEM(cond.shape, jnp.bfloat16),
            pltpu.VMEM(vale.shape, jnp.bfloat16),
            pltpu.VMEM(gmap.shape, jnp.int32),
            pltpu.SemaphoreType.DMA((3,)),
        ],
        compiler_params=pltpu.CompilerParams(vmem_limit_bytes=4 * 1024 * 1024),
    )(place, *in_hbm(cond, vale, gmap))


def pack_kernel(got, v_out, c_out, block, sent):
    n_z = got.shape[0]
    width = (got.shape[2] - 128) // 2
    row_id = lax.broadcasted_iota(jnp.int32, (8, 128), 0)
    maps = []
    for first in range(0, n_z, 4):
        tile = jnp.zeros((8, 128), jnp.float32)
        for z in range(first, first + 4):
            pair = got[z, :, 2 * width :].astype(jnp.float32)
            tile = jnp.where(row_id == 2 * (z - first), pair[0:1], tile)
            tile = jnp.where(row_id == 2 * (z - first) + 1, pair[1:2], tile)
        maps.append(tile.astype(jnp.bfloat16))

    def fill(target, column):
        for z in range(n_z):
            target[:, entry_lanes(z, width)] = got[z, :, pl.ds(column * width, width)]
        for number, tile in enumerate(maps):
            target[:, pl.ds(n_z * width + 128 * number, 128)] = tile

    fill(block, 0)
    copies = [
        pltpu.make_async_copy(block, v_out.at[dest], sent.at[dest])
        for dest in range(v_out.shape[0])
    ]
    for copy in copies:
        copy.start()
    fill(c_out, 1)
    for copy in copies:
        copy.wait()


def pack(got, dests):
    n_z = got.shape[0]
    width = (got.shape[2] - 128) // 2
    shape = (8, n_z * width + 128 * (n_z // 4))
    return pl.pallas_call(
        pack_kernel,
        in_specs=[VMEM],
        out_specs=[HBM, VMEM],
        out_shape=[
            pltpu.HBM((dests,) + shape, jnp.bfloat16),
            jax.ShapeDtypeStruct(shape, jnp.bfloat16),
        ],
        scratch_shapes=[
            pltpu.VMEM(shape, jnp.bfloat16),
            pltpu.SemaphoreType.DMA((dests,)),
        ],
        compiler_params=pltpu.CompilerParams(vmem_limit_bytes=8 * 1024 * 1024),
    )(got)


def cut_kernel(place, slab, w_low, w_high, whole, arrived):
    width = slab.shape[0]
    fetch = pltpu.make_async_copy(slab, whole, arrived)
    fetch.start()
    fetch.wait()
    half = w_low.shape[1] // width
    for number in range(2 * half):
        block = 2 * number + 1 - place[1] % 2
        lanes = pl.ds(pl.multiple_of(block * width, width), width)
        target = (w_low, w_high)[number // half]
        target[:, pl.ds(number % half * width, width)] = whole[:, lanes]


def cut(place, slab):
    width, grid_h = slab.shape
    quarter = jax.ShapeDtypeStruct((width, grid_h // 4), jnp.bfloat16)
    return pl.pallas_call(
        cut_kernel,
        in_specs=[SMEM, HBM],
        out_specs=[VMEM, VMEM],
        out_shape=[quarter, quarter],
        scratch_shapes=[pltpu.VMEM(slab.shape, jnp.bfloat16), pltpu.SemaphoreType.DMA(())],
        compiler_params=pltpu.CompilerParams(vmem_limit_bytes=6 * 1024 * 1024),
        cost_estimate=pl.CostEstimate(
            flops=0, bytes_accessed=3 * width * grid_h, transcendentals=0
        ),
    )(place, *in_hbm(slab))


def total_kernel(shares, out):
    sources, rows, _ = shares.shape
    low = lax.broadcasted_iota(jnp.int32, (1, 128), 1) < 64
    sums = []
    for y in range(2):
        first = y * (sources // 2)
        total = shares[first].astype(jnp.float32)
        for source in range(first + 1, first + sources // 2):
            total = total + shares[source].astype(jnp.float32)
        sums.append((total, pltpu.roll(total, 64, 1)))
    for z in range(rows // 2):
        lines = []
        for strip, turned in sums:
            left, right = (turned, strip) if z % 2 else (strip, turned)
            for row in (4 * (z // 2), 4 * (z // 2) + 2):
                lines.append(jnp.where(low, left[row : row + 1], right[row + 1 : row + 2]))
        out[z] = jnp.concatenate(lines, axis=0)


def totals(shares):
    n_z = shares.shape[1] // 2
    return pl.pallas_call(
        total_kernel,
        in_specs=[VMEM],
        out_specs=VMEM,
        out_shape=jax.ShapeDtypeStruct((n_z, 4, 128), jnp.float32),
        compiler_params=pltpu.CompilerParams(vmem_limit_bytes=4 * 1024 * 1024),
    )(shares)


def pick_kernel(plan, rows, out):
    for by in range(NSHIFT + 1):
        both = jnp.zeros((4, 128), jnp.float32)
        for z in range(rows.shape[0]):
            both = jnp.where(plan[z] == by, rows[z], both)
        pair = both[:2] + both[2:]
        for side in range(2):
            out[by, :, pl.ds(128 * side, 128)] = pair[side : side + 1]


def pick(plan, rows):
    return pl.pallas_call(
        pick_kernel,
        in_specs=[VMEM, VMEM],
        out_specs=VMEM,
        out_shape=jax.ShapeDtypeStruct((NSHIFT + 1, 1, 256), jnp.float32),
        compiler_params=pltpu.CompilerParams(vmem_limit_bytes=4 * 1024 * 1024),
    )(plan, rows)


def per_device(cond, vale, screen, qtable, gmap):
    n_ka = lax.axis_size("ka")
    n_ga = lax.axis_size("ga")
    n_z = n_ka // 2
    my_ka = lax.axis_index("ka")
    my_ga = lax.axis_index("ga")
    place = jnp.stack([my_ka, my_ga]).astype(jnp.int32)
    swap_core = [(i, i ^ 1) for i in range(n_ga)]
    swap_y = [(i, i ^ n_z) for i in range(n_ka)]
    swap_both = [(k * n_ga + g, (k ^ n_z) * n_ga + (g ^ 1)) for k in range(n_ka) for g in range(n_ga)]
    along_z = [list(range(n_z)), list(range(n_z, n_ka))]
    planes = [
        [(y * n_z + z) * n_ga + g for y in range(2) for g in range(n_ga)] for z in range(n_z)
    ]
    same_core = [plane[core::2] for plane in planes for core in range(2)]

    sent = spread(place, cond, vale, gmap, n_z)
    got = lax.all_to_all(sent, "ka", 0, 0, axis_index_groups=along_z)

    slab = screen[0]
    v_sent, c_keep = pack(got, n_ga)
    w_low, w_high = cut(place, slab)
    c_y = lax.ppermute(c_keep, "ka", swap_y)
    c_core = lax.ppermute(c_keep, "ga", swap_core)
    c_diag = lax.ppermute(c_keep, ("ka", "ga"), swap_both)
    w_low = lax.ppermute(w_low, "ga", swap_core)
    w_high = lax.ppermute(w_high, "ga", swap_core)
    v_all = lax.all_to_all(v_sent, ("ka", "ga"), 0, 0, axis_index_groups=same_core)

    part, plan = tiles(qtable, place, slab, w_low, w_high, v_all, c_keep, c_y, c_core, c_diag)
    shares = lax.all_to_all(part, ("ka", "ga"), 0, 0, axis_index_groups=planes)
    rows = lax.all_to_all(totals(shares), "ka", 0, 0, axis_index_groups=along_z)
    return jnp.transpose(pick(plan, rows), (1, 0, 2))


def solution(mesh):
    in_specs = (P("ka", None, "ga"), P("ka", None, "ga"), P("ka", "ga", None), P(), P("ka", "ga"))
    out_specs = P("ka", None, "ga")
    return jax.shard_map(
        per_device, mesh=mesh, in_specs=in_specs, out_specs=out_specs, check_vma=False
    )
```

```python
import jax
import jax.numpy as jnp
from jax import lax
from jax.experimental import pallas as pl
from jax.experimental.pallas import tpu as pltpu
from jax.sharding import PartitionSpec as P

NSHIFT = 2
STEP_K = 4
BAND_K = 16
CHUNKS = ((0,), (1,2,3), (4,5,6,7))
VMEM = pl.BlockSpec(memory_space=pltpu.VMEM)
SMEM = pl.BlockSpec(memory_space=pltpu.SMEM)
HBM = pl.BlockSpec(memory_space=pltpu.HBM)
ANY = pl.BlockSpec(memory_space=pl.ANY)


def in_hbm(*arrays):
    return [pltpu.with_memory_space_constraint(array, pltpu.HBM) for array in arrays]


def last_dims(a, b):
    return lax.dot_general(a, b, (((1,), (1,)), ((), ())), preferred_element_type=jnp.float32)


def density(own, far):
    product = own[:, None, :] * far[None, :, :]
    return product.reshape(64, own.shape[-1]).astype(jnp.bfloat16)


def lane_gather(source, places):
    return jnp.take_along_axis(source, places, axis=1, mode="promise_in_bounds")


def mapped(source, places):
    low, high = source[:, :128], source[:, 128:]
    sides = []
    for part in (places[:, :128], places[:, 128:]):
        inner = part & 127
        sides.append(jnp.where(part < 128, lane_gather(low, inner), lane_gather(high, inner)))
    return jnp.concatenate(sides, axis=1)


def entry_lanes(entry, width):
    return pl.ds(entry * width, width)


def map_entries(packed, count, width, store):
    maps = []
    for first in range(0, 2 * count, 8):
        lanes = pl.ds(count * width + 16 * first, 128)
        maps.append(packed[:, lanes].astype(jnp.float32).astype(jnp.int32))
    for entry in range(count):
        sides = []
        for side in range(2):
            row = 2 * entry + side
            places = maps[row // 8][row % 8 : row % 8 + 1]
            sides.append(jnp.broadcast_to(places, (8, 128)))
        source = packed[:, entry_lanes(entry, width)].astype(jnp.float32)
        store(entry, mapped(source, jnp.concatenate(sides, axis=1)))


def tile_kernel(
    table, place, w_own, w_mate, vale, c_keep, c_y, c_core, c_diag, out, plan,
    slabs, far_v, far_c, c_all, pv, pc, image, wide, arrived, joined,
):
    blocks = vale.shape[0] // 2
    width = w_own.shape[0]
    n_z = plan.shape[0]
    my_ka, core = place[0], place[1] % 2
    my_y = my_ka // n_z
    shift = sum(jnp.where(table[by, 0] == my_ka, by, 0) for by in range(1, NSHIFT + 1))
    fetches = [
        pltpu.make_async_copy(
            w_own.at[:, pl.ds(pl.multiple_of((2 * block + core) * width, width), width)],
            slabs.at[0, :, pl.ds(block * width, width)],
            arrived.at[block],
        )
        for block in range(blocks)
    ]
    fetches.append(pltpu.make_async_copy(w_mate, slabs.at[1], arrived.at[blocks]))
    fetches += [
        pltpu.make_async_copy(source, c_all.at[side, y], joined.at[side, other])
        for side, pair in enumerate(((c_keep, c_y), (c_core, c_diag)))
        for other, (source, y) in enumerate(zip(pair, (my_y, 1 - my_y)))
    ]
    for fetch in fetches:
        fetch.start()

    upper = lax.broadcasted_iota(jnp.int32, (4, 128), 0) >= 2
    for z in range(n_z):
        tile = jnp.full((4, 128), -1, jnp.int32)
        for by in range(NSHIFT + 1):
            holder = table[by, 0]
            row = jnp.where(upper, holder - n_z, holder)
            tile = jnp.where(row == z, by, tile)
        plan[z] = tile

    def partner(k):
        return jnp.where(k < shift, k - shift + 2 * n_z, k - shift)

    def form(number):
        slot = number % far_v.shape[0]
        for y in range(2):
            for inner, block in enumerate(CHUNKS[number]):

                def store(z, value):
                    far_v[slot, y * n_z + z, :, pl.ds(inner * width, width)] = value

                map_entries(vale.at[y * blocks + block], n_z, width, store)
        for k in range(2 * n_z):
            for inner, block in enumerate(CHUNKS[number]):
                far = far_v[slot, partner(k), :, pl.ds(inner * width, width)]
                own = vale[k // n_z * blocks + block, :, entry_lanes(k % n_z, width)]
                own = own.astype(jnp.float32)
                pv[pl.ds(64 * k, 64), pl.ds(block * width, width)] = density(own, far)

    def form_c():
        for side in range(2):
            lanes = pl.ds(side * width, width)
            for y in range(2):

                def store(z, value):
                    far_c[y * n_z + z, :, lanes] = value

                map_entries(c_all.at[side, y], n_z, width, store)
            for k in range(2 * n_z):
                own = c_all[side, k // n_z, :, entry_lanes(k % n_z, width)].astype(jnp.float32)
                pc[pl.ds(64 * k, 64), lanes] = density(own, far_c[partner(k), :, lanes])

    def term(rows, number, side):
        span = pl.ds(CHUNKS[number][0] * width, len(CHUNKS[number]) * width)
        return last_dims(pv[rows, span], slabs[side, :, span])

    sides = [pl.ds(side * width, width) for side in range(2)]
    last = len(CHUNKS) - 1
    form(0)
    for fetch in fetches:
        fetch.wait()
    for number in range(last):
        form(number + 1)
        if number + 1 == last:
            form_c()
        for side, lanes in enumerate(sides):
            part = term(pl.ds(0, pv.shape[0]), number, side)
            image[:, lanes] = part if number == 0 else image[:, lanes] + part

    low = lax.broadcasted_iota(jnp.int32, (64, 128), 1) < 64
    for first in range(0, 2 * n_z, BAND_K):
        rows = pl.ds(64 * first, 64 * BAND_K)
        bands = [
            (image[rows, lanes] + term(rows, last, side)).astype(jnp.bfloat16)
            for side, lanes in enumerate(sides)
        ]
        for step in range(0, BAND_K, STEP_K):
            full = None
            for lanes, band in zip(sides, bands):
                band = band[64 * step : 64 * (step + STEP_K)]
                part = last_dims(pc[pl.ds(64 * (first + step), 64 * STEP_K), lanes], band)
                full = part if full is None else full + part
            for pair in range(STEP_K // 2):
                base = 128 * pair
                strip = full[:, base : base + 128]
                tile = jnp.where(low, strip[base : base + 64], strip[base + 64 : base + 128])
                k = first + step + 2 * pair
                dests = pl.ds(16 * (k // n_z), 16)
                wide[dests, pl.ds(2 * (k % n_z), 4), :] = tile.reshape(16, 4, 128)
    out[...] = wide[...].astype(jnp.bfloat16)


def tiles(table, place, w_own, w_mate, vale, c_keep, c_y, c_core, c_diag):
    sources = vale.shape[0]
    width = w_own.shape[0]
    n_z = table.shape[0] // 2
    rows = 2 * n_z * 64
    blocks = sources // 2
    wide = max(len(chunk) for chunk in CHUNKS) * width
    return pl.pallas_call(
        tile_kernel,
        in_specs=[SMEM, SMEM, HBM, ANY, VMEM] + [ANY] * 4,
        out_specs=[VMEM, VMEM],
        out_shape=[
            jax.ShapeDtypeStruct((2 * sources, 2 * n_z, 128), jnp.bfloat16),
            jax.ShapeDtypeStruct((n_z, 4, 128), jnp.int32),
        ],
        scratch_shapes=[
            pltpu.VMEM((2, width, blocks * width), jnp.bfloat16),
            pltpu.VMEM((2, 2 * n_z, 8, wide), jnp.float32),
            pltpu.VMEM((2 * n_z, 8, 2 * width), jnp.float32),
            pltpu.VMEM((2, 2) + c_keep.shape, jnp.bfloat16),
            pltpu.VMEM((rows, blocks * width), jnp.bfloat16),
            pltpu.VMEM((rows, 2 * width), jnp.bfloat16),
            pltpu.VMEM((rows, 2 * width), jnp.float32),
            pltpu.VMEM((2 * sources, 2 * n_z, 128), jnp.float32),
            pltpu.SemaphoreType.DMA((blocks + 1,)),
            pltpu.SemaphoreType.DMA((2, 2)),
        ],
        compiler_params=pltpu.CompilerParams(vmem_limit_bytes=28 * 1024 * 1024),
    )(table, place, *in_hbm(w_own), w_mate, vale, c_keep, c_y, c_core, c_diag)


def spread_kernel(place, cond_in, vale_in, gmap_in, out, cond, vale, gmap, arrived):
    width = cond.shape[2]
    fetches = [
        pltpu.make_async_copy(source, target, arrived.at[number])
        for number, (source, target) in enumerate(((cond_in, cond), (vale_in, vale), (gmap_in, gmap)))
    ]
    for fetch in fetches:
        fetch.start()
    for fetch in fetches:
        fetch.wait()
    places = (gmap[...] - place[1] * width).astype(jnp.float32)
    top = lax.broadcasted_iota(jnp.int32, (8, 128), 0) == 0
    places = jnp.where(top, places[:, :128], places[:, 128:]).astype(jnp.bfloat16)
    for dest in range(out.shape[0]):
        out[dest, :, :width] = vale[0]
        out[dest, :, width : 2 * width] = cond[0]
        out[dest, :, 2 * width :] = places


def spread(place, cond, vale, gmap, dests):
    return pl.pallas_call(
        spread_kernel,
        in_specs=[SMEM] + [HBM] * 3,
        out_specs=VMEM,
        out_shape=jax.ShapeDtypeStruct((dests, 8, 2 * cond.shape[2] + 128), jnp.bfloat16),
        scratch_shapes=[
            pltpu.VMEM(cond.shape, jnp.bfloat16),
            pltpu.VMEM(vale.shape, jnp.bfloat16),
            pltpu.VMEM(gmap.shape, jnp.int32),
            pltpu.SemaphoreType.DMA((3,)),
        ],
        compiler_params=pltpu.CompilerParams(vmem_limit_bytes=4 * 1024 * 1024),
    )(place, *in_hbm(cond, vale, gmap))


def pack_kernel(got, v_out, c_out, block, sent):
    n_z = got.shape[0]
    width = (got.shape[2] - 128) // 2
    row_id = lax.broadcasted_iota(jnp.int32, (8, 128), 0)
    maps = []
    for first in range(0, n_z, 4):
        tile = jnp.zeros((8, 128), jnp.float32)
        for z in range(first, first + 4):
            pair = got[z, :, 2 * width :].astype(jnp.float32)
            tile = jnp.where(row_id == 2 * (z - first), pair[0:1], tile)
            tile = jnp.where(row_id == 2 * (z - first) + 1, pair[1:2], tile)
        maps.append(tile.astype(jnp.bfloat16))

    def fill(target, column):
        for z in range(n_z):
            target[:, entry_lanes(z, width)] = got[z, :, pl.ds(column * width, width)]
        for number, tile in enumerate(maps):
            target[:, pl.ds(n_z * width + 128 * number, 128)] = tile

    fill(block, 0)
    copies = [
        pltpu.make_async_copy(block, v_out.at[dest], sent.at[dest])
        for dest in range(v_out.shape[0])
    ]
    for copy in copies:
        copy.start()
    fill(c_out, 1)
    for copy in copies:
        copy.wait()


def pack(got, dests):
    n_z = got.shape[0]
    width = (got.shape[2] - 128) // 2
    shape = (8, n_z * width + 128 * (n_z // 4))
    return pl.pallas_call(
        pack_kernel,
        in_specs=[VMEM],
        out_specs=[HBM, VMEM],
        out_shape=[
            pltpu.HBM((dests,) + shape, jnp.bfloat16),
            jax.ShapeDtypeStruct(shape, jnp.bfloat16),
        ],
        scratch_shapes=[
            pltpu.VMEM(shape, jnp.bfloat16),
            pltpu.SemaphoreType.DMA((dests,)),
        ],
        compiler_params=pltpu.CompilerParams(vmem_limit_bytes=8 * 1024 * 1024),
    )(got)


def cut_kernel(place, slab, w_half, whole, arrived):
    width = slab.shape[0]
    fetch = pltpu.make_async_copy(slab, whole, arrived)
    fetch.start()
    fetch.wait()
    for number in range(w_half.shape[1] // width):
        block = 2 * number + 1 - place[1] % 2
        lanes = pl.ds(pl.multiple_of(block * width, width), width)
        w_half[:, pl.ds(number * width, width)] = whole[:, lanes]


def cut(place, slab):
    width, grid_h = slab.shape
    return pl.pallas_call(
        cut_kernel,
        in_specs=[SMEM, HBM],
        out_specs=VMEM,
        out_shape=jax.ShapeDtypeStruct((width, grid_h // 2), jnp.bfloat16),
        scratch_shapes=[pltpu.VMEM(slab.shape, jnp.bfloat16), pltpu.SemaphoreType.DMA(())],
        compiler_params=pltpu.CompilerParams(vmem_limit_bytes=6 * 1024 * 1024),
        cost_estimate=pl.CostEstimate(
            flops=0, bytes_accessed=3 * width * grid_h, transcendentals=0
        ),
    )(place, *in_hbm(slab))


def total_kernel(shares, out):
    sources, rows, _ = shares.shape
    low = lax.broadcasted_iota(jnp.int32, (1, 128), 1) < 64
    sums = []
    for y in range(2):
        first = y * (sources // 2)
        total = shares[first].astype(jnp.float32)
        for source in range(first + 1, first + sources // 2):
            total = total + shares[source].astype(jnp.float32)
        sums.append((total, pltpu.roll(total, 64, 1)))
    for z in range(rows // 2):
        lines = []
        for strip, turned in sums:
            left, right = (turned, strip) if z % 2 else (strip, turned)
            for row in (4 * (z // 2), 4 * (z // 2) + 2):
                lines.append(jnp.where(low, left[row : row + 1], right[row + 1 : row + 2]))
        out[z] = jnp.concatenate(lines, axis=0)


def totals(shares):
    n_z = shares.shape[1] // 2
    return pl.pallas_call(
        total_kernel,
        in_specs=[VMEM],
        out_specs=VMEM,
        out_shape=jax.ShapeDtypeStruct((n_z, 4, 128), jnp.float32),
        compiler_params=pltpu.CompilerParams(vmem_limit_bytes=4 * 1024 * 1024),
    )(shares)


def pick_kernel(plan, rows, out):
    for by in range(NSHIFT + 1):
        both = jnp.zeros((4, 128), jnp.float32)
        for z in range(rows.shape[0]):
            both = jnp.where(plan[z] == by, rows[z], both)
        pair = both[:2] + both[2:]
        for side in range(2):
            out[by, :, pl.ds(128 * side, 128)] = pair[side : side + 1]


def pick(plan, rows):
    return pl.pallas_call(
        pick_kernel,
        in_specs=[VMEM, VMEM],
        out_specs=VMEM,
        out_shape=jax.ShapeDtypeStruct((NSHIFT + 1, 1, 256), jnp.float32),
        compiler_params=pltpu.CompilerParams(vmem_limit_bytes=4 * 1024 * 1024),
    )(plan, rows)


def per_device(cond, vale, screen, qtable, gmap):
    n_ka = lax.axis_size("ka")
    n_ga = lax.axis_size("ga")
    n_z = n_ka // 2
    my_ka = lax.axis_index("ka")
    my_ga = lax.axis_index("ga")
    place = jnp.stack([my_ka, my_ga]).astype(jnp.int32)
    swap_core = [(i, i ^ 1) for i in range(n_ga)]
    swap_y = [(i, i ^ n_z) for i in range(n_ka)]
    swap_both = [(k * n_ga + g, (k ^ n_z) * n_ga + (g ^ 1)) for k in range(n_ka) for g in range(n_ga)]
    along_z = [list(range(n_z)), list(range(n_z, n_ka))]
    planes = [
        [(y * n_z + z) * n_ga + g for y in range(2) for g in range(n_ga)] for z in range(n_z)
    ]
    same_core = [plane[core::2] for plane in planes for core in range(2)]

    sent = spread(place, cond, vale, gmap, n_z)
    got = lax.all_to_all(sent, "ka", 0, 0, axis_index_groups=along_z)

    slab = screen[0]
    v_sent, c_keep = pack(got, n_ga)
    w_mate = cut(place, slab)
    c_y = lax.ppermute(c_keep, "ka", swap_y)
    c_core = lax.ppermute(c_keep, "ga", swap_core)
    c_diag = lax.ppermute(c_keep, ("ka", "ga"), swap_both)
    w_mate = lax.ppermute(w_mate, "ga", swap_core)
    v_all = lax.all_to_all(v_sent, ("ka", "ga"), 0, 0, axis_index_groups=same_core)

    part, plan = tiles(qtable, place, slab, w_mate, v_all, c_keep, c_y, c_core, c_diag)
    shares = lax.all_to_all(part, ("ka", "ga"), 0, 0, axis_index_groups=planes)
    rows = lax.all_to_all(totals(shares), "ka", 0, 0, axis_index_groups=along_z)
    return jnp.transpose(pick(plan, rows), (1, 0, 2))


def solution(mesh):
    in_specs = (P("ka", None, "ga"), P("ka", None, "ga"), P("ka", "ga", None), P(), P("ka", "ga"))
    out_specs = P("ka", None, "ga")
    return jax.shard_map(
        per_device, mesh=mesh, in_specs=in_specs, out_specs=out_specs, check_vma=False
    )
```

```python
import jax
import jax.numpy as jnp
from jax import lax
from jax.experimental import pallas as pl
from jax.experimental.pallas import tpu as pltpu
from jax.sharding import PartitionSpec as P

NSHIFT = 2
STEP_K = 4
BAND_K = 16
CHUNKS = ((0,), (1,2,3), (4,5,6,7))
VMEM = pl.BlockSpec(memory_space=pltpu.VMEM)
SMEM = pl.BlockSpec(memory_space=pltpu.SMEM)
HBM = pl.BlockSpec(memory_space=pltpu.HBM)
ANY = pl.BlockSpec(memory_space=pl.ANY)


def in_hbm(*arrays):
    return [pltpu.with_memory_space_constraint(array, pltpu.HBM) for array in arrays]


def last_dims(a, b):
    return lax.dot_general(a, b, (((1,), (1,)), ((), ())), preferred_element_type=jnp.float32)


def density(own, far):
    product = own[:, None, :] * far[None, :, :]
    return product.reshape(64, own.shape[-1]).astype(jnp.bfloat16)


def lane_gather(source, places):
    return jnp.take_along_axis(source, places, axis=1, mode="promise_in_bounds")


def mapped(source, places):
    low, high = source[:, :128], source[:, 128:]
    sides = []
    for part in (places[:, :128], places[:, 128:]):
        inner = part & 127
        sides.append(jnp.where(part < 128, lane_gather(low, inner), lane_gather(high, inner)))
    return jnp.concatenate(sides, axis=1)


def entry_lanes(entry, width):
    return pl.ds(entry * width, width)


def map_entries(packed, count, width, store):
    maps = []
    for first in range(0, 2 * count, 8):
        lanes = pl.ds(count * width + 16 * first, 128)
        maps.append(packed[:, lanes].astype(jnp.float32).astype(jnp.int32))
    for entry in range(count):
        sides = []
        for side in range(2):
            row = 2 * entry + side
            places = maps[row // 8][row % 8 : row % 8 + 1]
            sides.append(jnp.broadcast_to(places, (8, 128)))
        source = packed[:, entry_lanes(entry, width)].astype(jnp.float32)
        store(entry, mapped(source, jnp.concatenate(sides, axis=1)))


def tile_kernel(
    table, place, w_own, w_mate, vale, c_keep, c_y, c_core, c_diag, out, plan,
    slabs, far_v, far_c, c_all, pv, pc, image, wide, arrived, joined,
):
    blocks = vale.shape[0] // 2
    width = w_own.shape[0]
    n_z = plan.shape[0]
    my_ka, core = place[0], place[1] % 2
    my_y = my_ka // n_z
    shift = sum(jnp.where(table[by, 0] == my_ka, by, 0) for by in range(1, NSHIFT + 1))
    fetches = [
        pltpu.make_async_copy(
            w_own.at[:, pl.ds(pl.multiple_of((2 * block + core) * width, width), width)],
            slabs.at[0, :, pl.ds(block * width, width)],
            arrived.at[block],
        )
        for block in range(blocks)
    ]
    fetches.append(pltpu.make_async_copy(w_mate, slabs.at[1], arrived.at[blocks]))
    fetches += [
        pltpu.make_async_copy(source, c_all.at[side, y], joined.at[side, other])
        for side, pair in enumerate(((c_keep, c_y), (c_core, c_diag)))
        for other, (source, y) in enumerate(zip(pair, (my_y, 1 - my_y)))
    ]
    for fetch in fetches:
        fetch.start()

    upper = lax.broadcasted_iota(jnp.int32, (4, 128), 0) >= 2
    for z in range(n_z):
        tile = jnp.full((4, 128), -1, jnp.int32)
        for by in range(NSHIFT + 1):
            holder = table[by, 0]
            row = jnp.where(upper, holder - n_z, holder)
            tile = jnp.where(row == z, by, tile)
        plan[z] = tile

    def partner(k):
        return jnp.where(k < shift, k - shift + 2 * n_z, k - shift)

    def form(number):
        slot = number % far_v.shape[0]
        for y in range(2):
            for inner, block in enumerate(CHUNKS[number]):

                def store(z, value):
                    far_v[slot, y * n_z + z, :, pl.ds(inner * width, width)] = value

                map_entries(vale.at[y * blocks + block], n_z, width, store)
        for k in range(2 * n_z):
            for inner, block in enumerate(CHUNKS[number]):
                far = far_v[slot, partner(k), :, pl.ds(inner * width, width)]
                own = vale[k // n_z * blocks + block, :, entry_lanes(k % n_z, width)]
                own = own.astype(jnp.float32)
                pv[pl.ds(64 * k, 64), pl.ds(block * width, width)] = density(own, far)

    def form_c():
        for side in range(2):
            lanes = pl.ds(side * width, width)
            for y in range(2):

                def store(z, value):
                    far_c[y * n_z + z, :, lanes] = value

                map_entries(c_all.at[side, y], n_z, width, store)
            for k in range(2 * n_z):
                own = c_all[side, k // n_z, :, entry_lanes(k % n_z, width)].astype(jnp.float32)
                pc[pl.ds(64 * k, 64), lanes] = density(own, far_c[partner(k), :, lanes])

    def term(rows, number, side):
        span = pl.ds(CHUNKS[number][0] * width, len(CHUNKS[number]) * width)
        return last_dims(pv[rows, span], slabs[side, :, span])

    sides = [pl.ds(side * width, width) for side in range(2)]
    last = len(CHUNKS) - 1
    form(0)
    for fetch in fetches:
        fetch.wait()
    for number in range(last):
        form(number + 1)
        if number + 1 == last:
            form_c()
        for side, lanes in enumerate(sides):
            part = term(pl.ds(0, pv.shape[0]), number, side)
            image[:, lanes] = part if number == 0 else image[:, lanes] + part

    low = lax.broadcasted_iota(jnp.int32, (64, 128), 1) < 64
    for first in range(0, 2 * n_z, BAND_K):
        rows = pl.ds(64 * first, 64 * BAND_K)
        bands = [
            (image[rows, lanes] + term(rows, last, side)).astype(jnp.bfloat16)
            for side, lanes in enumerate(sides)
        ]
        for step in range(0, BAND_K, STEP_K):
            full = None
            for lanes, band in zip(sides, bands):
                band = band[64 * step : 64 * (step + STEP_K)]
                part = last_dims(pc[pl.ds(64 * (first + step), 64 * STEP_K), lanes], band)
                full = part if full is None else full + part
            for pair in range(STEP_K // 2):
                base = 128 * pair
                strip = full[:, base : base + 128]
                tile = jnp.where(low, strip[base : base + 64], strip[base + 64 : base + 128])
                k = first + step + 2 * pair
                dests = pl.ds(16 * (k // n_z), 16)
                wide[dests, pl.ds(2 * (k % n_z), 4), :] = tile.reshape(16, 4, 128)
    out[...] = wide[...].astype(jnp.bfloat16)


def tiles(table, place, w_own, w_mate, vale, c_keep, c_y, c_core, c_diag):
    sources = vale.shape[0]
    width = w_own.shape[0]
    n_z = table.shape[0] // 2
    rows = 2 * n_z * 64
    blocks = sources // 2
    wide = max(len(chunk) for chunk in CHUNKS) * width
    return pl.pallas_call(
        tile_kernel,
        in_specs=[SMEM, SMEM, HBM, ANY, VMEM] + [ANY] * 4,
        out_specs=[VMEM, VMEM],
        out_shape=[
            jax.ShapeDtypeStruct((2 * sources, 2 * n_z, 128), jnp.bfloat16),
            jax.ShapeDtypeStruct((n_z, 4, 128), jnp.int32),
        ],
        scratch_shapes=[
            pltpu.VMEM((2, width, blocks * width), jnp.bfloat16),
            pltpu.VMEM((2, 2 * n_z, 8, wide), jnp.float32),
            pltpu.VMEM((2 * n_z, 8, 2 * width), jnp.float32),
            pltpu.VMEM((2, 2) + c_keep.shape, jnp.bfloat16),
            pltpu.VMEM((rows, blocks * width), jnp.bfloat16),
            pltpu.VMEM((rows, 2 * width), jnp.bfloat16),
            pltpu.VMEM((rows, 2 * width), jnp.float32),
            pltpu.VMEM((2 * sources, 2 * n_z, 128), jnp.float32),
            pltpu.SemaphoreType.DMA((blocks + 1,)),
            pltpu.SemaphoreType.DMA((2, 2)),
        ],
        compiler_params=pltpu.CompilerParams(vmem_limit_bytes=28 * 1024 * 1024),
    )(table, place, *in_hbm(w_own), w_mate, vale, c_keep, c_y, c_core, c_diag)


def spread_kernel(place, cond_in, vale_in, gmap_in, out, cond, vale, gmap, arrived):
    width = cond.shape[2]
    fetches = [
        pltpu.make_async_copy(source, target, arrived.at[number])
        for number, (source, target) in enumerate(((cond_in, cond), (vale_in, vale), (gmap_in, gmap)))
    ]
    for fetch in fetches:
        fetch.start()
    for fetch in fetches:
        fetch.wait()
    places = (gmap[...] - place[1] * width).astype(jnp.float32)
    top = lax.broadcasted_iota(jnp.int32, (8, 128), 0) == 0
    places = jnp.where(top, places[:, :128], places[:, 128:]).astype(jnp.bfloat16)
    for dest in range(out.shape[0]):
        out[dest, :, :width] = vale[0]
        out[dest, :, width : 2 * width] = cond[0]
        out[dest, :, 2 * width :] = places


def spread(place, cond, vale, gmap, dests):
    return pl.pallas_call(
        spread_kernel,
        in_specs=[SMEM] + [HBM] * 3,
        out_specs=VMEM,
        out_shape=jax.ShapeDtypeStruct((dests, 8, 2 * cond.shape[2] + 128), jnp.bfloat16),
        scratch_shapes=[
            pltpu.VMEM(cond.shape, jnp.bfloat16),
            pltpu.VMEM(vale.shape, jnp.bfloat16),
            pltpu.VMEM(gmap.shape, jnp.int32),
            pltpu.SemaphoreType.DMA((3,)),
        ],
        compiler_params=pltpu.CompilerParams(vmem_limit_bytes=4 * 1024 * 1024),
    )(place, *in_hbm(cond, vale, gmap))


def pack_kernel(got, v_out, c_out, block, sent):
    n_z = got.shape[0]
    width = (got.shape[2] - 128) // 2
    row_id = lax.broadcasted_iota(jnp.int32, (8, 128), 0)
    maps = []
    for first in range(0, n_z, 4):
        tile = jnp.zeros((8, 128), jnp.float32)
        for z in range(first, first + 4):
            pair = got[z, :, 2 * width :].astype(jnp.float32)
            tile = jnp.where(row_id == 2 * (z - first), pair[0:1], tile)
            tile = jnp.where(row_id == 2 * (z - first) + 1, pair[1:2], tile)
        maps.append(tile.astype(jnp.bfloat16))

    def fill(target, column):
        for z in range(n_z):
            target[:, entry_lanes(z, width)] = got[z, :, pl.ds(column * width, width)]
        for number, tile in enumerate(maps):
            target[:, pl.ds(n_z * width + 128 * number, 128)] = tile

    fill(block, 0)
    copies = [
        pltpu.make_async_copy(block, v_out.at[dest], sent.at[dest])
        for dest in range(v_out.shape[0])
    ]
    for copy in copies:
        copy.start()
    fill(c_out, 1)
    for copy in copies:
        copy.wait()


def pack(got, dests):
    n_z = got.shape[0]
    width = (got.shape[2] - 128) // 2
    shape = (8, n_z * width + 128 * (n_z // 4))
    return pl.pallas_call(
        pack_kernel,
        in_specs=[VMEM],
        out_specs=[HBM, VMEM],
        out_shape=[
            pltpu.HBM((dests,) + shape, jnp.bfloat16),
            jax.ShapeDtypeStruct(shape, jnp.bfloat16),
        ],
        scratch_shapes=[
            pltpu.VMEM(shape, jnp.bfloat16),
            pltpu.SemaphoreType.DMA((dests,)),
        ],
        compiler_params=pltpu.CompilerParams(vmem_limit_bytes=8 * 1024 * 1024),
    )(got)


def cut_kernel(place, slab, w_half, whole, arrived):
    width = slab.shape[0]
    fetch = pltpu.make_async_copy(slab, whole, arrived)
    fetch.start()
    fetch.wait()
    for number in range(w_half.shape[1] // width):
        block = 2 * number + 1 - place[1] % 2
        lanes = pl.ds(pl.multiple_of(block * width, width), width)
        w_half[:, pl.ds(number * width, width)] = whole[:, lanes]


def cut(place, slab):
    width, grid_h = slab.shape
    return pl.pallas_call(
        cut_kernel,
        in_specs=[SMEM, HBM],
        out_specs=VMEM,
        out_shape=jax.ShapeDtypeStruct((width, grid_h // 2), jnp.bfloat16),
        scratch_shapes=[pltpu.VMEM(slab.shape, jnp.bfloat16), pltpu.SemaphoreType.DMA(())],
        compiler_params=pltpu.CompilerParams(vmem_limit_bytes=6 * 1024 * 1024),
        cost_estimate=pl.CostEstimate(
            flops=0, bytes_accessed=3 * width * grid_h, transcendentals=0
        ),
    )(place, *in_hbm(slab))


def total_kernel(shares, out):
    sources, rows, _ = shares.shape
    low = lax.broadcasted_iota(jnp.int32, (1, 128), 1) < 64
    sums = []
    for y in range(2):
        first = y * (sources // 2)
        total = shares[first].astype(jnp.float32)
        for source in range(first + 1, first + sources // 2):
            total = total + shares[source].astype(jnp.float32)
        sums.append((total, pltpu.roll(total, 64, 1)))
    for z in range(rows // 2):
        lines = []
        for strip, turned in sums:
            left, right = (turned, strip) if z % 2 else (strip, turned)
            for row in (4 * (z // 2), 4 * (z // 2) + 2):
                lines.append(jnp.where(low, left[row : row + 1], right[row + 1 : row + 2]))
        out[z] = jnp.concatenate(lines, axis=0)


def totals(shares):
    n_z = shares.shape[1] // 2
    return pl.pallas_call(
        total_kernel,
        in_specs=[VMEM],
        out_specs=VMEM,
        out_shape=jax.ShapeDtypeStruct((n_z, 4, 128), jnp.float32),
        compiler_params=pltpu.CompilerParams(vmem_limit_bytes=4 * 1024 * 1024),
    )(shares)


def pick_kernel(plan, rows, out):
    for by in range(NSHIFT + 1):
        both = jnp.zeros((4, 128), jnp.float32)
        for z in range(rows.shape[0]):
            both = jnp.where(plan[z] == by, rows[z], both)
        pair = both[:2] + both[2:]
        for side in range(2):
            out[by, :, pl.ds(128 * side, 128)] = pair[side : side + 1]


def pick(plan, rows):
    return pl.pallas_call(
        pick_kernel,
        in_specs=[VMEM, VMEM],
        out_specs=VMEM,
        out_shape=jax.ShapeDtypeStruct((NSHIFT + 1, 1, 256), jnp.float32),
        compiler_params=pltpu.CompilerParams(vmem_limit_bytes=4 * 1024 * 1024),
    )(plan, rows)


def per_device(cond, vale, screen, qtable, gmap):
    n_ka = lax.axis_size("ka")
    n_ga = lax.axis_size("ga")
    n_z = n_ka // 2
    my_ka = lax.axis_index("ka")
    my_ga = lax.axis_index("ga")
    place = jnp.stack([my_ka, my_ga]).astype(jnp.int32)
    swap_core = [(i, i ^ 1) for i in range(n_ga)]
    swap_y = [(i, i ^ n_z) for i in range(n_ka)]
    swap_both = [(k * n_ga + g, (k ^ n_z) * n_ga + (g ^ 1)) for k in range(n_ka) for g in range(n_ga)]
    along_z = [list(range(n_z)), list(range(n_z, n_ka))]
    planes = [
        [(y * n_z + z) * n_ga + g for y in range(2) for g in range(n_ga)] for z in range(n_z)
    ]
    same_core = [plane[core::2] for plane in planes for core in range(2)]

    sent = spread(place, cond, vale, gmap, n_z)
    got = lax.all_to_all(sent, "ka", 0, 0, axis_index_groups=along_z)

    slab = screen[0]
    v_sent, c_keep = pack(got, n_ga)
    w_mate = cut(place, slab)
    c_core = lax.ppermute(c_keep, "ga", swap_core)
    c_y = lax.ppermute(c_keep, "ka", swap_y)
    c_diag = lax.ppermute(c_keep, ("ka", "ga"), swap_both)
    w_mate = lax.ppermute(w_mate, "ga", swap_core)
    v_all = lax.all_to_all(v_sent, ("ka", "ga"), 0, 0, axis_index_groups=same_core)

    part, plan = tiles(qtable, place, slab, w_mate, v_all, c_keep, c_y, c_core, c_diag)
    shares = lax.all_to_all(part, ("ka", "ga"), 0, 0, axis_index_groups=planes)
    rows = lax.all_to_all(totals(shares), "ka", 0, 0, axis_index_groups=along_z)
    return jnp.transpose(pick(plan, rows), (1, 0, 2))


def solution(mesh):
    in_specs = (P("ka", None, "ga"), P("ka", None, "ga"), P("ka", "ga", None), P(), P("ka", "ga"))
    out_specs = P("ka", None, "ga")
    return jax.shard_map(
        per_device, mesh=mesh, in_specs=in_specs, out_specs=out_specs, check_vma=False
    )
```

```python
import jax
import jax.numpy as jnp
from jax import lax
from jax.experimental import pallas as pl
from jax.experimental.pallas import tpu as pltpu
from jax.sharding import PartitionSpec as P

NSHIFT = 2
STEP_K = 4
BAND_K = 16
CHUNKS = ((0,), (1,2,3), (4,5,6,7))
VMEM = pl.BlockSpec(memory_space=pltpu.VMEM)
SMEM = pl.BlockSpec(memory_space=pltpu.SMEM)
HBM = pl.BlockSpec(memory_space=pltpu.HBM)
ANY = pl.BlockSpec(memory_space=pl.ANY)


def in_hbm(*arrays):
    return [pltpu.with_memory_space_constraint(array, pltpu.HBM) for array in arrays]


def last_dims(a, b):
    return lax.dot_general(a, b, (((1,), (1,)), ((), ())), preferred_element_type=jnp.float32)


def density(own, far):
    product = own[:, None, :] * far[None, :, :]
    return product.reshape(64, own.shape[-1]).astype(jnp.bfloat16)


def lane_gather(source, places):
    return jnp.take_along_axis(source, places, axis=1, mode="promise_in_bounds")


def mapped(source, places):
    low, high = source[:, :128], source[:, 128:]
    sides = []
    for part in (places[:, :128], places[:, 128:]):
        inner = part & 127
        sides.append(jnp.where(part < 128, lane_gather(low, inner), lane_gather(high, inner)))
    return jnp.concatenate(sides, axis=1)


def entry_lanes(entry, width):
    return pl.ds(entry * width, width)


def map_entries(packed, count, width, store):
    maps = []
    for first in range(0, 2 * count, 8):
        lanes = pl.ds(count * width + 16 * first, 128)
        maps.append(packed[:, lanes].astype(jnp.float32).astype(jnp.int32))
    for entry in range(count):
        sides = []
        for side in range(2):
            row = 2 * entry + side
            places = maps[row // 8][row % 8 : row % 8 + 1]
            sides.append(jnp.broadcast_to(places, (8, 128)))
        source = packed[:, entry_lanes(entry, width)].astype(jnp.float32)
        store(entry, mapped(source, jnp.concatenate(sides, axis=1)))


def tile_kernel(
    table, place, w_own, w_mate, vale, c_keep, c_core, c_y, c_diag, out, plan,
    slabs, far_v, far_c, c_all, pv, pc, image, wide, arrived, joined,
):
    blocks = vale.shape[0] // 2
    width = w_own.shape[0]
    n_z = plan.shape[0]
    my_ka, core = place[0], place[1] % 2
    my_y = my_ka // n_z
    shift = sum(jnp.where(table[by, 0] == my_ka, by, 0) for by in range(1, NSHIFT + 1))
    fetches = [
        pltpu.make_async_copy(
            w_own.at[:, pl.ds(pl.multiple_of((2 * block + core) * width, width), width)],
            slabs.at[0, :, pl.ds(block * width, width)],
            arrived.at[block],
        )
        for block in range(blocks)
    ]
    fetches.append(pltpu.make_async_copy(w_mate, slabs.at[1], arrived.at[blocks]))
    fetches += [
        pltpu.make_async_copy(source, c_all.at[side, y], joined.at[side, other])
        for side, pair in enumerate(((c_keep, c_y), (c_core, c_diag)))
        for other, (source, y) in enumerate(zip(pair, (my_y, 1 - my_y)))
    ]
    for fetch in fetches:
        fetch.start()

    upper = lax.broadcasted_iota(jnp.int32, (4, 128), 0) >= 2
    for z in range(n_z):
        tile = jnp.full((4, 128), -1, jnp.int32)
        for by in range(NSHIFT + 1):
            holder = table[by, 0]
            row = jnp.where(upper, holder - n_z, holder)
            tile = jnp.where(row == z, by, tile)
        plan[z] = tile

    def partner(k):
        return jnp.where(k < shift, k - shift + 2 * n_z, k - shift)

    def form(number):
        slot = number % far_v.shape[0]
        for y in range(2):
            for inner, block in enumerate(CHUNKS[number]):

                def store(z, value):
                    far_v[slot, y * n_z + z, :, pl.ds(inner * width, width)] = value

                map_entries(vale.at[y * blocks + block], n_z, width, store)
        for k in range(2 * n_z):
            for inner, block in enumerate(CHUNKS[number]):
                far = far_v[slot, partner(k), :, pl.ds(inner * width, width)]
                own = vale[k // n_z * blocks + block, :, entry_lanes(k % n_z, width)]
                own = own.astype(jnp.float32)
                pv[pl.ds(64 * k, 64), pl.ds(block * width, width)] = density(own, far)

    def form_c():
        for side in range(2):
            lanes = pl.ds(side * width, width)
            for y in range(2):

                def store(z, value):
                    far_c[y * n_z + z, :, lanes] = value

                map_entries(c_all.at[side, y], n_z, width, store)
            for k in range(2 * n_z):
                own = c_all[side, k // n_z, :, entry_lanes(k % n_z, width)].astype(jnp.float32)
                pc[pl.ds(64 * k, 64), lanes] = density(own, far_c[partner(k), :, lanes])

    def term(rows, number, side):
        span = pl.ds(CHUNKS[number][0] * width, len(CHUNKS[number]) * width)
        return last_dims(pv[rows, span], slabs[side, :, span])

    sides = [pl.ds(side * width, width) for side in range(2)]
    last = len(CHUNKS) - 1
    form(0)
    for fetch in fetches:
        fetch.wait()
    for number in range(last):
        form(number + 1)
        if number + 1 == last:
            form_c()
        for side, lanes in enumerate(sides):
            part = term(pl.ds(0, pv.shape[0]), number, side)
            image[:, lanes] = part if number == 0 else image[:, lanes] + part

    low = lax.broadcasted_iota(jnp.int32, (64, 128), 1) < 64
    for first in range(0, 2 * n_z, BAND_K):
        rows = pl.ds(64 * first, 64 * BAND_K)
        bands = [
            (image[rows, lanes] + term(rows, last, side)).astype(jnp.bfloat16)
            for side, lanes in enumerate(sides)
        ]
        for step in range(0, BAND_K, STEP_K):
            full = None
            for lanes, band in zip(sides, bands):
                band = band[64 * step : 64 * (step + STEP_K)]
                part = last_dims(pc[pl.ds(64 * (first + step), 64 * STEP_K), lanes], band)
                full = part if full is None else full + part
            for pair in range(STEP_K // 2):
                base = 128 * pair
                strip = full[:, base : base + 128]
                tile = jnp.where(low, strip[base : base + 64], strip[base + 64 : base + 128])
                k = first + step + 2 * pair
                dests = pl.ds(16 * (k // n_z), 16)
                wide[dests, pl.ds(2 * (k % n_z), 4), :] = tile.reshape(16, 4, 128)
    out[...] = wide[...].astype(jnp.bfloat16)


def tiles(table, place, w_own, w_mate, vale, c_keep, c_core, c_y, c_diag):
    sources = vale.shape[0]
    width = w_own.shape[0]
    n_z = table.shape[0] // 2
    rows = 2 * n_z * 64
    blocks = sources // 2
    wide = max(len(chunk) for chunk in CHUNKS) * width
    return pl.pallas_call(
        tile_kernel,
        in_specs=[SMEM, SMEM, HBM, ANY, VMEM] + [ANY] * 4,
        out_specs=[VMEM, VMEM],
        out_shape=[
            jax.ShapeDtypeStruct((2 * sources, 2 * n_z, 128), jnp.bfloat16),
            jax.ShapeDtypeStruct((n_z, 4, 128), jnp.int32),
        ],
        scratch_shapes=[
            pltpu.VMEM((2, width, blocks * width), jnp.bfloat16),
            pltpu.VMEM((2, 2 * n_z, 8, wide), jnp.float32),
            pltpu.VMEM((2 * n_z, 8, 2 * width), jnp.float32),
            pltpu.VMEM((2, 2) + c_keep.shape, jnp.bfloat16),
            pltpu.VMEM((rows, blocks * width), jnp.bfloat16),
            pltpu.VMEM((rows, 2 * width), jnp.bfloat16),
            pltpu.VMEM((rows, 2 * width), jnp.float32),
            pltpu.VMEM((2 * sources, 2 * n_z, 128), jnp.float32),
            pltpu.SemaphoreType.DMA((blocks + 1,)),
            pltpu.SemaphoreType.DMA((2, 2)),
        ],
        compiler_params=pltpu.CompilerParams(vmem_limit_bytes=28 * 1024 * 1024),
    )(table, place, *in_hbm(w_own), w_mate, vale, c_keep, c_core, c_y, c_diag)


def spread_kernel(place, cond_in, vale_in, gmap_in, out, cond, vale, gmap, arrived):
    width = cond.shape[2]
    fetches = [
        pltpu.make_async_copy(source, target, arrived.at[number])
        for number, (source, target) in enumerate(((cond_in, cond), (vale_in, vale), (gmap_in, gmap)))
    ]
    for fetch in fetches:
        fetch.start()
    for fetch in fetches:
        fetch.wait()
    places = (gmap[...] - place[1] * width).astype(jnp.float32)
    top = lax.broadcasted_iota(jnp.int32, (8, 128), 0) == 0
    places = jnp.where(top, places[:, :128], places[:, 128:]).astype(jnp.bfloat16)
    for dest in range(out.shape[0]):
        out[dest, :, :width] = vale[0]
        out[dest, :, width : 2 * width] = cond[0]
        out[dest, :, 2 * width :] = places


def spread(place, cond, vale, gmap, dests):
    return pl.pallas_call(
        spread_kernel,
        in_specs=[SMEM] + [HBM] * 3,
        out_specs=VMEM,
        out_shape=jax.ShapeDtypeStruct((dests, 8, 2 * cond.shape[2] + 128), jnp.bfloat16),
        scratch_shapes=[
            pltpu.VMEM(cond.shape, jnp.bfloat16),
            pltpu.VMEM(vale.shape, jnp.bfloat16),
            pltpu.VMEM(gmap.shape, jnp.int32),
            pltpu.SemaphoreType.DMA((3,)),
        ],
        compiler_params=pltpu.CompilerParams(vmem_limit_bytes=4 * 1024 * 1024),
    )(place, *in_hbm(cond, vale, gmap))


def pack_kernel(got, v_out, c_out, block, sent):
    n_z = got.shape[0]
    width = (got.shape[2] - 128) // 2
    row_id = lax.broadcasted_iota(jnp.int32, (8, 128), 0)
    maps = []
    for first in range(0, n_z, 4):
        tile = jnp.zeros((8, 128), jnp.float32)
        for z in range(first, first + 4):
            pair = got[z, :, 2 * width :].astype(jnp.float32)
            tile = jnp.where(row_id == 2 * (z - first), pair[0:1], tile)
            tile = jnp.where(row_id == 2 * (z - first) + 1, pair[1:2], tile)
        maps.append(tile.astype(jnp.bfloat16))

    def fill(target, column):
        for z in range(n_z):
            target[:, entry_lanes(z, width)] = got[z, :, pl.ds(column * width, width)]
        for number, tile in enumerate(maps):
            target[:, pl.ds(n_z * width + 128 * number, 128)] = tile

    fill(block, 0)
    copies = [
        pltpu.make_async_copy(block, v_out.at[dest], sent.at[dest])
        for dest in range(v_out.shape[0])
    ]
    for copy in copies:
        copy.start()
    fill(c_out, 1)
    for copy in copies:
        copy.wait()


def pack(got, dests):
    n_z = got.shape[0]
    width = (got.shape[2] - 128) // 2
    shape = (8, n_z * width + 128 * (n_z // 4))
    return pl.pallas_call(
        pack_kernel,
        in_specs=[VMEM],
        out_specs=[HBM, VMEM],
        out_shape=[
            pltpu.HBM((dests,) + shape, jnp.bfloat16),
            jax.ShapeDtypeStruct(shape, jnp.bfloat16),
        ],
        scratch_shapes=[
            pltpu.VMEM(shape, jnp.bfloat16),
            pltpu.SemaphoreType.DMA((dests,)),
        ],
        compiler_params=pltpu.CompilerParams(vmem_limit_bytes=8 * 1024 * 1024),
    )(got)


def cut_kernel(place, slab, w_half, whole, arrived):
    width = slab.shape[0]
    fetch = pltpu.make_async_copy(slab, whole, arrived)
    fetch.start()
    fetch.wait()
    for number in range(w_half.shape[1] // width):
        block = 2 * number + 1 - place[1] % 2
        lanes = pl.ds(pl.multiple_of(block * width, width), width)
        w_half[:, pl.ds(number * width, width)] = whole[:, lanes]


def cut(place, slab):
    width, grid_h = slab.shape
    return pl.pallas_call(
        cut_kernel,
        in_specs=[SMEM, HBM],
        out_specs=VMEM,
        out_shape=jax.ShapeDtypeStruct((width, grid_h // 2), jnp.bfloat16),
        scratch_shapes=[pltpu.VMEM(slab.shape, jnp.bfloat16), pltpu.SemaphoreType.DMA(())],
        compiler_params=pltpu.CompilerParams(vmem_limit_bytes=6 * 1024 * 1024),
        cost_estimate=pl.CostEstimate(
            flops=0, bytes_accessed=3 * width * grid_h, transcendentals=0
        ),
    )(place, *in_hbm(slab))


def total_kernel(shares, out):
    sources, rows, _ = shares.shape
    low = lax.broadcasted_iota(jnp.int32, (1, 128), 1) < 64
    sums = []
    for y in range(2):
        first = y * (sources // 2)
        total = shares[first].astype(jnp.float32)
        for source in range(first + 1, first + sources // 2):
            total = total + shares[source].astype(jnp.float32)
        sums.append((total, pltpu.roll(total, 64, 1)))
    for z in range(rows // 2):
        lines = []
        for strip, turned in sums:
            left, right = (turned, strip) if z % 2 else (strip, turned)
            for row in (4 * (z // 2), 4 * (z // 2) + 2):
                lines.append(jnp.where(low, left[row : row + 1], right[row + 1 : row + 2]))
        out[z] = jnp.concatenate(lines, axis=0)


def totals(shares):
    n_z = shares.shape[1] // 2
    return pl.pallas_call(
        total_kernel,
        in_specs=[VMEM],
        out_specs=VMEM,
        out_shape=jax.ShapeDtypeStruct((n_z, 4, 128), jnp.float32),
        compiler_params=pltpu.CompilerParams(vmem_limit_bytes=4 * 1024 * 1024),
    )(shares)


def pick_kernel(plan, rows, out):
    for by in range(NSHIFT + 1):
        both = jnp.zeros((4, 128), jnp.float32)
        for z in range(rows.shape[0]):
            both = jnp.where(plan[z] == by, rows[z], both)
        pair = both[:2] + both[2:]
        for side in range(2):
            out[by, :, pl.ds(128 * side, 128)] = pair[side : side + 1]


def pick(plan, rows):
    return pl.pallas_call(
        pick_kernel,
        in_specs=[VMEM, VMEM],
        out_specs=VMEM,
        out_shape=jax.ShapeDtypeStruct((NSHIFT + 1, 1, 256), jnp.float32),
        compiler_params=pltpu.CompilerParams(vmem_limit_bytes=4 * 1024 * 1024),
    )(plan, rows)


def per_device(cond, vale, screen, qtable, gmap):
    n_ka = lax.axis_size("ka")
    n_ga = lax.axis_size("ga")
    n_z = n_ka // 2
    my_ka = lax.axis_index("ka")
    my_ga = lax.axis_index("ga")
    place = jnp.stack([my_ka, my_ga]).astype(jnp.int32)
    swap_core = [(i, i ^ 1) for i in range(n_ga)]
    swap_y = [(i, i ^ n_z) for i in range(n_ka)]
    swap_both = [(k * n_ga + g, (k ^ n_z) * n_ga + (g ^ 1)) for k in range(n_ka) for g in range(n_ga)]
    along_z = [list(range(n_z)), list(range(n_z, n_ka))]
    planes = [
        [(y * n_z + z) * n_ga + g for y in range(2) for g in range(n_ga)] for z in range(n_z)
    ]
    same_core = [plane[core::2] for plane in planes for core in range(2)]

    sent = spread(place, cond, vale, gmap, n_z)
    got = lax.all_to_all(sent, "ka", 0, 0, axis_index_groups=along_z)

    slab = screen[0]
    v_sent, c_keep = pack(got, n_ga)
    w_mate = cut(place, slab)
    c_core = lax.ppermute(c_keep, "ga", swap_core)
    c_y = lax.ppermute(c_keep, "ka", swap_y)
    c_diag = lax.ppermute(c_keep, ("ka", "ga"), swap_both)
    w_mate = lax.ppermute(w_mate, "ga", swap_core)
    v_all = lax.all_to_all(v_sent, ("ka", "ga"), 0, 0, axis_index_groups=same_core)

    part, plan = tiles(qtable, place, slab, w_mate, v_all, c_keep, c_core, c_y, c_diag)
    shares = lax.all_to_all(part, ("ka", "ga"), 0, 0, axis_index_groups=planes)
    rows = lax.all_to_all(totals(shares), "ka", 0, 0, axis_index_groups=along_z)
    return jnp.transpose(pick(plan, rows), (1, 0, 2))


def solution(mesh):
    in_specs = (P("ka", None, "ga"), P("ka", None, "ga"), P("ka", "ga", None), P(), P("ka", "ga"))
    out_specs = P("ka", None, "ga")
    return jax.shard_map(
        per_device, mesh=mesh, in_specs=in_specs, out_specs=out_specs, check_vma=False
    )
```
